256 devices in a mesh: session: 64 (over x, z, core), kvhead: 4 (over y).
Axes of the slice: x: 4, y: 4, z: 8, core: 2. Of those that a mesh axis runs over, the one named last changes fastest.
Arguments:
- queries: bfloat16 [256, 16384], P(('session', 'kvhead')), may hold values from -12 to 12
- new_keys: bfloat16 [256, 1024], P('session', 'kvhead'), may hold values from -10.5 to 10.5
- new_values: bfloat16 [256, 1024], P('session', 'kvhead'), may hold values from -24 to 24
- sink_keys: bfloat16 [256, 4, 1024], P('session', None, 'kvhead'), may hold values from -10.5 to 10.5
- sink_values: bfloat16 [256, 4, 1024], P('session', None, 'kvhead'), may hold values from -24 to 24
- window_keys: bfloat16 [256, 512, 1024], P('session', None, 'kvhead'), may hold values from -9 to 9
- window_values: bfloat16 [256, 512, 1024], P('session', None, 'kvhead'), may hold values from -24 to 24
- window_len: int32 [256], P('session'), may hold values from 1 to 512, as said below
- root_keys: bfloat16 [32768, 1024], P('session', 'kvhead'), may hold values from -6 to 6
- root_values: bfloat16 [32768, 1024], P('session', 'kvhead'), may hold values from -24 to 24
- prefix_keys: bfloat16 [65536, 1024], P('session', 'kvhead'), may hold values from -6 to 6
- prefix_values: bfloat16 [65536, 1024], P('session', 'kvhead'), may hold values from -24 to 24
- tenant_of: int32 [256], replicated, may hold values from 0 to 63, as said below
- owner: int32 [64], replicated, may hold values from 0 to 63, each once
Outputs:
- attended: bfloat16 [256, 16384], P(('session', 'kvhead'))
The draws below stay inside these ranges and needn't reach their ends.
Inputs may be any that keep to these rules, and one draw needn't show every extreme that they name: `window_len`: every device's 4 chats include one whose window holds 512 used slots. `tenant_of`: no tenant has more than 16 chats, and one tenant has exactly 16.
All inputs are finite; a program needn't handle non-finite values.
Results may differ from the reference program's by a relative error of at most 0.007.
Values may be sent and summed in bfloat16 or wider, within the bound.
No kernel may reach another device: no remote copies, remote signals or barrier semaphores. Data moves between devices by JAX's collectives and lax.ppermute only.
A program may use at most 64 MiB of HBM per device.

```python
import jax
import jax.numpy as jnp
from jax import lax

HEADS = 128
KVH = 8
HD = 128
GROUP = 16
CHAT_DEV = 4
CHATS = 256
ROOT_DEV = 512
ROOT = 32768
TENANTS = 64
PREFIX = 1024
SINKS = 4
WINDOW = 512
TCAP = 16
N_SESSION = 64


def draw_queries(key, part):
    key = jax.random.fold_in(key, 11)
    first = jax.random.fold_in(key, 0)
    base = jnp.clip(jax.random.normal(first, (CHATS, HEADS, HD), jnp.float32) * 2.5, -12.0, 12.0)
    return base.reshape(CHATS, HEADS * HD).astype(jnp.bfloat16)


def draw_root_keys(key, part):
    key = jax.random.fold_in(key, 12)
    first = jax.random.fold_in(key, 0)
    base = jnp.clip(jax.random.normal(first, (ROOT, KVH, HD), jnp.float32), -6.0, 6.0)
    return base.reshape(ROOT, KVH * HD).astype(jnp.bfloat16)


def draw_window_len(key, part):
    key = jax.random.fold_in(key, 13)
    first, second = jax.random.split(key, 2)
    blocks = CHATS // CHAT_DEV
    lengths = jax.random.randint(first, (blocks, CHAT_DEV), 1, WINDOW + 1)
    chosen = jax.random.randint(second, (blocks, 1), 0, CHAT_DEV)
    lengths = jnp.where(jnp.arange(CHAT_DEV)[None, :] == chosen, WINDOW, lengths)
    return lengths.reshape(CHATS).astype(jnp.int32)


def draw_tenant_of(key, part):
    key = jax.random.fold_in(key, 14)
    first, second, third = jax.random.split(key, 3)
    order = jax.random.permutation(first, CHATS)
    hottest = jax.random.randint(second, (), 0, TENANTS)
    spare = jax.random.permutation(third, (TENANTS - 1) * TCAP)[:CHATS - TCAP] // TCAP
    spare = spare + (spare >= hottest).astype(jnp.int32)
    filled = jnp.concatenate([jnp.full((TCAP,), hottest, jnp.int32), spare.astype(jnp.int32)])
    return jnp.zeros((CHATS,), jnp.int32).at[order].set(filled)


def shard_levels(rng, dims, pieces, least, high):
    gain, own = 1.0, jax.random.fold_in(rng, 6)
    for axis_at, blocks in pieces:
        draws = jnp.exp(jax.random.uniform(jax.random.fold_in(own, axis_at), (blocks,), jnp.float32, least / len(pieces), high / len(pieces)))
        gain = gain * jnp.repeat(draws, dims[axis_at] // blocks).reshape([-1 if axis == axis_at else 1 for axis in range(len(dims))])
    return gain


def scatter_about(rng, extent, width, most, shards=(), kind=jnp.bfloat16):
    entries = jax.random.normal(rng, extent, jnp.float32) * width
    if len(shards) > 0:
        entries = shard_levels(rng, extent, shards, -0.22, 0.18) * entries
    return jnp.clip(entries, min=-most, max=most).astype(kind)


def setup_inputs(seed: int = 0) -> dict:
    splits = jax.random.split(jax.random.key(seed), 15)
    return {
        "queries": draw_queries(jax.random.fold_in(splits[14], 71), 0),
        "new_keys": scatter_about(splits[1], (CHATS, KVH * HD), 1.75, 10.5, ((0, 64), (1, 4))),
        "new_values": scatter_about(splits[2], (CHATS, KVH * HD), 4.0, 24.0, ((0, 64), (1, 4))),
        "sink_keys": scatter_about(splits[3], (CHATS, SINKS, KVH * HD), 1.75, 10.5, ((0, 64), (2, 4))),
        "sink_values": scatter_about(splits[4], (CHATS, SINKS, KVH * HD), 4.0, 24.0, ((0, 64), (2, 4))),
        "window_keys": scatter_about(splits[5], (CHATS, WINDOW, KVH * HD), 1.5, 9.0, ((0, 64), (2, 4))),
        "window_values": scatter_about(splits[6], (CHATS, WINDOW, KVH * HD), 4.0, 24.0, ((0, 64), (2, 4))),
        "window_len": draw_window_len(jax.random.fold_in(splits[14], 71), 0),
        "root_keys": draw_root_keys(jax.random.fold_in(splits[14], 71), 0),
        "root_values": scatter_about(splits[9], (ROOT, KVH * HD), 4.0, 24.0, ((0, 64), (1, 4))),
        "prefix_keys": scatter_about(splits[10], (TENANTS * PREFIX, KVH * HD), 1.0, 6.0, ((0, 64), (1, 4))),
        "prefix_values": scatter_about(splits[11], (TENANTS * PREFIX, KVH * HD), 4.0, 24.0, ((0, 64), (1, 4))),
        "tenant_of": draw_tenant_of(jax.random.fold_in(splits[14], 71), 0),
        "owner": jax.random.permutation(splits[13], TENANTS).astype(jnp.int32),
    }


floor_score = -1.0e30


def to_bf16(values):
    return lax.optimization_barrier(values.astype(jnp.bfloat16)).astype(jnp.float32)


def reference(queries, new_keys, new_values, sink_keys, sink_values, window_keys, window_values, window_len, root_keys, root_values, prefix_keys, prefix_values, tenant_of, owner):
    factor = HD ** -0.5
    root_kf = root_keys.reshape(N_SESSION, ROOT_DEV, KVH, HD).astype(jnp.float32)
    root_vf = root_values.reshape(N_SESSION, ROOT_DEV, KVH, HD).astype(jnp.float32)
    prefix_kb = prefix_keys.reshape(TENANTS, PREFIX, KVH, HD)
    prefix_vb = prefix_values.reshape(TENANTS, PREFIX, KVH, HD)
    positions = jnp.arange(WINDOW, dtype=jnp.int32)
    blocks_all = jnp.arange(N_SESSION, dtype=jnp.int32)

    def one_chat(chat):
        query = queries[chat].reshape(KVH, GROUP, HD).astype(jnp.float32)
        holder = owner[tenant_of[chat]].astype(jnp.int32)
        here = blocks_all == holder
        tenant_k = lax.dynamic_index_in_dim(prefix_kb, holder, 0, keepdims=False).astype(jnp.float32)
        tenant_v = lax.dynamic_index_in_dim(prefix_vb, holder, 0, keepdims=False).astype(jnp.float32)
        root_scores = jnp.einsum("gqd,srgd->gqsr", query, root_kf) * factor
        pre_scores = jnp.einsum("gqd,pgd->gqp", query, tenant_k) * factor
        block_peak = jnp.max(root_scores, axis=-1)
        pre_peak = jnp.max(pre_scores, axis=-1)
        block_peak = jnp.where(here, jnp.maximum(block_peak, pre_peak[..., None]), block_peak)
        holder_peak = lax.dynamic_index_in_dim(block_peak, holder, 2, keepdims=False)
        root_w = jnp.exp(root_scores - block_peak[..., None])
        pre_w = jnp.exp(pre_scores - holder_peak[..., None])
        block_total = jnp.sum(root_w, axis=-1) + jnp.where(here, jnp.sum(pre_w, axis=-1)[..., None], 0.0)
        block_numer = jnp.einsum("gqsr,srgd->gqsd", to_bf16(root_w), root_vf)
        pre_numer = jnp.einsum("gqp,pgd->gqd", to_bf16(pre_w), tenant_v)
        block_numer = block_numer + jnp.where(here[:, None], pre_numer[:, :, None, :], 0.0)
        share = to_bf16(block_numer / block_total[..., None])

        key_sets = [sink_keys[chat].reshape(SINKS, KVH, HD).astype(jnp.float32),
                    window_keys[chat].reshape(WINDOW, KVH, HD).astype(jnp.float32),
                    new_keys[chat].reshape(1, KVH, HD).astype(jnp.float32)]
        value_sets = [sink_values[chat].reshape(SINKS, KVH, HD).astype(jnp.float32),
                      window_values[chat].reshape(WINDOW, KVH, HD).astype(jnp.float32),
                      new_values[chat].reshape(1, KVH, HD).astype(jnp.float32)]
        scores = jnp.concatenate([jnp.einsum("gqd,kgd->gqk", query, key_rows) for key_rows in key_sets], axis=-1) * factor
        valid = jnp.concatenate([jnp.ones((SINKS,), jnp.bool_), positions < window_len[chat], jnp.ones((1,), jnp.bool_)])
        scores = jnp.where(valid, scores, floor_score)
        home_peak = jnp.max(scores, axis=-1)
        weights = jnp.exp(scores - home_peak[..., None])
        home_total = jnp.sum(weights, axis=-1)
        rounded = to_bf16(weights)
        home_numer = jnp.zeros((KVH, GROUP, HD), jnp.float32)
        offset = 0
        for value_rows in value_sets:
            length = value_rows.shape[0]
            home_numer = home_numer + jnp.einsum("gqk,kgd->gqd", rounded[..., offset:offset + length], value_rows)
            offset = offset + length

        top = jnp.maximum(jnp.max(block_peak, axis=-1), home_peak)
        far = block_total * jnp.exp(block_peak - top[..., None])
        near = jnp.exp(home_peak - top)
        total = near * home_total + jnp.sum(far, axis=-1)
        numer = near[..., None] * home_numer + jnp.sum(far[..., None] * share, axis=2)
        return (numer / total[..., None]).astype(jnp.bfloat16).reshape(HEADS * HD)

    return lax.map(one_chat, jnp.arange(CHATS, dtype=jnp.int32))
```

```python
import functools
import math

import jax
import jax.numpy as jnp
from jax import lax
from jax.experimental import pallas as pl
from jax.experimental.pallas import tpu as pltpu
from jax.sharding import Mesh, PartitionSpec as P

HD = 128
GROUP = 16
KV = 2
HEADS = KV * GROUP
HOME = 4
NX, NZ, NC, NY = 4, 8, 2, 4
ROWS = 40
SCALE2 = HD**-0.5 * math.log2(math.e)
FLOOR = -1e30
COLUMN = NZ * HOME
MEMBER = 8
ROOM = 8
MIB = 2**20

NT = (((1,), (1,)), ((), ()))
VMEM = pl.BlockSpec(memory_space=pltpu.VMEM)
SMEM = pl.BlockSpec(memory_space=pltpu.SMEM)
BF16 = jnp.bfloat16
F32 = jnp.float32


def scores_of(query, keys):
    return lax.dot_general(query, keys, NT, preferred_element_type=F32)


def dot(a, b):
    return jnp.dot(a, b, preferred_element_type=F32)


def iota(shape, dim):
    return lax.broadcasted_iota(jnp.int32, shape, dim)


def head_diagonal():
    return (iota((HEADS, HD), 1) % HEADS) == iota((HEADS, HD), 0)


def level_parts(level):
    first = level.astype(BF16).astype(F32)
    second = (level - first).astype(BF16).astype(F32)
    third = level - first - second
    row = iota((1, 8, HD), 1)
    parts = jnp.where(row == 2, third[:, None], 0.0)
    parts = jnp.where(row == 1, second[:, None], parts)
    return jnp.where(row == 0, first[:, None], parts).astype(BF16)


def prepare_kernel(tenant_ref, owner_ref, t_row, o_row, plan, rounds):
    x, z, c = lax.axis_index("x"), lax.axis_index("z"), lax.axis_index("c")
    zero = jnp.int32(0)

    def clear(i, _):
        for t in range(NX):
            plan[t, i] = zero
        return 0

    lax.fori_loop(0, COLUMN + 1, clear, 0, unroll=11)

    def slot_of(s, i):
        return owner_ref[tenant_ref[((s * NZ + (i >> 2)) * 2 + c) * HOME + (i & 3)]]

    def scan_send(i, found):
        slot = slot_of(x, i)
        target = jnp.where(((slot >> 1) & (NZ - 1)) == z, slot >> 4, NX)
        new = []
        for t in range(NX):
            plan[t, found[t]] = i
            new.append(found[t] + (target == t).astype(jnp.int32))
        return tuple(new)

    found = lax.fori_loop(0, COLUMN, scan_send, (zero,) * NX, unroll=8)
    for t in range(NX):
        plan[2 * NX, t] = found[t]

    mine = x * NZ + z

    def scan_recv(i, found):
        new = []
        for s in range(NX):
            slot = slot_of(s, i)
            plan[NX + s, found[s]] = (slot & 1) ^ c
            new.append(found[s] + ((slot >> 1) == mine).astype(jnp.int32))
        return tuple(new)

    found = lax.fori_loop(0, COLUMN, scan_recv, (zero,) * NX, unroll=4)
    for s in range(NX):
        plan[2 * NX, NX + s] = found[s]

    chats = NX * NC * COLUMN
    tenants = o_row.shape[1]
    o_col = jnp.sum(
        jnp.where(iota((tenants, tenants), 0) == iota((tenants, tenants), 1), o_row[...] >> 1, 0),
        axis=1,
        keepdims=True,
    )
    by_row = jnp.sum(
        jnp.where(t_row[...] == iota((tenants, chats), 0), o_col, 0), axis=0, keepdims=True
    )

    def key(chip, chat):
        place = chat >> 2
        return (((place >> 4) * 2 + (place & 1)) << 5) + chip

    row = key(by_row, iota((1, chats), 1))
    square = (chats, chats)
    col = jnp.sum(
        jnp.where(iota(square, 0) == iota(square, 1), row, 0), axis=1, keepdims=True
    )
    fullest = jnp.max(jnp.sum(jnp.where(col == row, 1.0, 0.0), axis=1, keepdims=True))
    rounds[0] = (fullest.astype(jnp.int32) + ROOM - 1) >> 3


def root_part(q_ref, blocks, values, out):
    for g in range(KV):
        for n, (_, _, v0, v1) in enumerate(blocks):
            for i, v in enumerate((v0, v1)):
                rows = slice(n * 1024 + i * 512, n * 1024 + (i + 1) * 512)
                values[g, rows, :HD] = v[:, g * HD : (g + 1) * HD]
                values[g, rows, HD:] = jnp.ones((512, HD), BF16)
    diagonal = head_diagonal()
    rows = COLUMN // 2
    for h in range(2):
        chats = slice(h * rows, (h + 1) * rows)
        line = None
        for g in range(KV):
            heads = slice(g * GROUP, (g + 1) * GROUP)
            lanes = slice(g * HD, (g + 1) * HD)
            query = q_ref[chats, heads, :].reshape(rows * GROUP, HD)
            scores = [scores_of(query, k[:, lanes]) for block in blocks for k in block[:2]]
            peak = functools.reduce(
                jnp.maximum, [jnp.max(s, axis=1, keepdims=True) for s in scores]
            )
            numer = None
            for n, s in enumerate(scores):
                weights = jnp.exp2((s - peak) * SCALE2).astype(BF16)
                part = dot(weights, values[g, n * 512 : (n + 1) * 512, :])
                numer = part if numer is None else numer + part
            total = numer[:, HD:]
            share = (numer[:, :HD] / total).astype(BF16)
            out[chats, heads, :] = share.reshape(rows, GROUP, HD)
            level = (peak * SCALE2 + jnp.log2(total)).reshape(rows, GROUP, HD)
            part = jnp.sum(jnp.where(diagonal[None, heads], level, 0.0), axis=1)
            line = part if line is None else line + part
        out[chats, HEADS:, :] = level_parts(line)


def home_part(length_ref, q_ref, wk, wv, sk, sv, nk, nv, share_ref, level_ref):
    diagonal = head_diagonal()
    first = lax.axis_index("z") * HOME
    pad = jnp.zeros((3, KV * HD), F32)
    few_k, few_v = (
        [
            jnp.concatenate([s[j].astype(F32), n[j : j + 1].astype(F32), pad]).astype(BF16)
            for j in range(HOME)
        ]
        for s, n in ((sk, nk), (sv, nv))
    )
    pairs = [(g, j) for g in range(KV) for j in range(HOME)]
    recent, few = [], []
    for g, j in pairs:
        lanes = slice(g * HD, (g + 1) * HD)
        query = q_ref[first + j, g * GROUP : (g + 1) * GROUP, :]
        used = iota((GROUP, 512), 1) < length_ref[j]
        recent.append(jnp.where(used, scores_of(query, wk[j, :, lanes]), FLOOR))
        few.append(scores_of(query, few_k[j][:, lanes]))
    recent = jnp.concatenate(recent, axis=0)
    few = jnp.concatenate(few, axis=0)
    few = jnp.where(iota(few.shape, 1) < 5, few, FLOOR)
    peak = jnp.maximum(jnp.max(recent, axis=1, keepdims=True), jnp.max(few, axis=1, keepdims=True))
    recent = jnp.exp2((recent - peak) * SCALE2)
    few = jnp.exp2((few - peak) * SCALE2)
    total = jnp.sum(recent, axis=1, keepdims=True) + jnp.sum(few, axis=1, keepdims=True)
    recent, few = recent.astype(BF16), few.astype(BF16)
    level = jnp.broadcast_to(peak * SCALE2 + jnp.log2(total), (KV * HOME * GROUP, HD))
    level = level.reshape(KV, HOME, GROUP, HD)
    line = None
    for g in range(KV):
        part = jnp.where(diagonal[None, g * GROUP : (g + 1) * GROUP], level[g], 0.0)
        part = jnp.sum(part, axis=1)
        line = part if line is None else line + part
    level_ref[...] = line
    for n, (g, j) in enumerate(pairs):
        lanes = slice(g * HD, (g + 1) * HD)
        rows = slice(n * GROUP, (n + 1) * GROUP)
        numer = dot(recent[rows], wv[j, :, lanes]) + dot(few[rows], few_v[j][:, lanes])
        share_ref[j, g * GROUP : (g + 1) * GROUP, :] = numer / total[rows]


def near_kernel(
    length_ref, q_ref, k0, k1, v0, v1, wk, wv, sk, sv, nk, nv, out, share, level, values, wks, wvs, sems
):
    copies = [
        pltpu.make_async_copy(wk, wks, sems.at[0]),
        pltpu.make_async_copy(wv, wvs, sems.at[1]),
    ]
    for copy in copies:
        copy.start()
    root_part(q_ref, [(k0, k1, v0, v1)], values, out)
    for copy in copies:
        copy.wait()
    home_part(length_ref, q_ref, wks, wvs, sk, sv, nk, nv, share, level)


def far_kernel(q_ref, *refs):
    out, values = refs[-2:]
    root_part(q_ref, [refs[4 * n : 4 * n + 4] for n in range(NX - 1)], values, out)


def select_kernel(plan, turn, q_ref, out):
    start = turn if isinstance(turn, int) else turn[0] * ROOM
    chats = [plan[t, start + e] for t in range(NX) for e in range(ROOM)]
    for n, chat in enumerate(chats):
        out[n] = q_ref[chat]


def prefix_kernel(plan, turn, q_ref, pk0, pk1, pv0, pv1, out, qs, lists):
    start = turn if isinstance(turn, int) else turn[0] * ROOM
    diagonal = head_diagonal()
    zero = jnp.int32(0)
    lists[0, 0] = zero
    lists[1, 0] = zero
    n0, n1 = zero, zero
    for s in range(NX):

        def scan(e, found, s=s):
            slot = plan[NX + s, start + e]
            lists[0, found[0]] = s * ROOM + e
            lists[1, found[1]] = s * ROOM + e
            return found[0] + 1 - slot, found[1] + slot

        left = jnp.clip(plan[2 * NX, NX + s] - start, 0, ROOM)
        n0, n1 = lax.fori_loop(0, left, scan, (n0, n1))
    slots = ((pk0, pv0, n0), (pk1, pv1, n1))

    def step(b, _):
        results = []
        for i, (pk, pv, count) in enumerate(slots):
            last = jnp.maximum(count - 1, 0)
            chats = [lists[i, jnp.minimum(b * MEMBER + j, last)] for j in range(MEMBER)]
            line = None
            shares = []
            for g in range(KV):
                heads = slice(g * GROUP, (g + 1) * GROUP)
                lanes = slice(g * HD, (g + 1) * HD)
                for j, chat in enumerate(chats):
                    qs[i, g, j] = q_ref[chat, heads, :]
                scores = scores_of(qs[i, g].reshape(MEMBER * GROUP, HD), pk[:, lanes])
                peak = jnp.max(scores, axis=1, keepdims=True)
                weights = jnp.exp2((scores - peak) * SCALE2)
                total = jnp.sum(weights, axis=1, keepdims=True)
                numer = dot(weights.astype(BF16), pv[:, lanes])
                shares.append((numer / total).astype(BF16))
                level = jnp.broadcast_to(peak * SCALE2 + jnp.log2(total), (MEMBER * GROUP, HD))
                level = level.reshape(MEMBER, GROUP, HD)
                part = jnp.sum(jnp.where(diagonal[None, heads], level, 0.0), axis=1)
                line = part if line is None else line + part
            results.append((chats, shares, level_parts(line)))
        for (chats, shares, parts), (_, _, count) in zip(results, slots):

            @pl.when(b * MEMBER < count)
            def _(chats=chats, shares=shares, parts=parts):
                for j, chat in enumerate(chats):
                    for g in range(KV):
                        rows = slice(j * GROUP, (j + 1) * GROUP)
                        out[chat, g * GROUP : (g + 1) * GROUP, :] = shares[g][rows]
                    out[chat, HEADS:, :] = parts[j]

        return 0

    lax.fori_loop(0, (jnp.maximum(n0, n1) + MEMBER - 1) >> 3, step, 0)


def place_answers(plan, start, back, out):
    for t in range(NX):

        def place(e, _, t=t):
            out[plan[t, start + e]] = back[t * ROOM + e]
            return 0

        lax.fori_loop(0, jnp.clip(plan[2 * NX, t] - start, 0, ROOM), place, 0)


def scatter_kernel(plan, turn, back, before, out):
    out[...] = before[...]
    place_answers(plan, turn[0] * ROOM, back, out)


def weights_of(levels):
    top = functools.reduce(jnp.maximum, levels)
    weights = [jnp.exp2(v - top) for v in levels]
    total = functools.reduce(jnp.add, weights)
    return [w / total for w in weights], top + jnp.log2(total)


def read_level(ref):
    return jnp.sum(ref[:, HEADS:, :].astype(F32), axis=1)


def four_lines(weights):
    quarter = iota((1, HD), 1) // HEADS
    return functools.reduce(
        jnp.add, [jnp.where(quarter == i, w, 0.0) for i, w in enumerate(weights)]
    )


def mix(diagonal, line, shares):
    spread = jnp.where(diagonal, line, 0.0)
    high = spread.astype(BF16)
    low = (spread - high.astype(F32)).astype(BF16)
    return dot(high, shares) + dot(low, shares)


def merge_row_kernel(plan, near, far, back, before, share_ref, level_ref, out, prefix, lines, levels):
    diagonal = head_diagonal()
    prefix[...] = before[...]
    place_answers(plan, 0, back, prefix)
    level = [read_level(r) for r in (near, far, prefix)]
    weights, total = weights_of(level)
    line = four_lines(weights)
    for n, v in enumerate(level):
        levels[n] = v
    out[:, HEADS:, :] = level_parts(total)
    empty = jnp.zeros((HEADS, HD), BF16)

    def parts(i, fourth):
        sources = [near[i, :HEADS, :], far[i, :HEADS, :], prefix[i, :HEADS, :], fourth]
        return jnp.concatenate(sources, axis=0)

    for i in range(COLUMN):
        out[i, :HEADS, :] = mix(diagonal, line[i : i + 1], parts(i, empty)).astype(BF16)

    first = lax.axis_index("z") * HOME
    own = pl.ds(first, HOME)
    weights, total = weights_of([levels[n, own, :] for n in range(3)] + [level_ref[...]])
    line = four_lines(weights)
    rest = four_lines(weights[3:])
    out[own, HEADS:, :] = level_parts(total)
    nothing = jnp.zeros((3 * HEADS, HD), BF16)
    for j in range(HOME):
        home = share_ref[j]
        high = home.astype(BF16)
        low = jnp.concatenate([(home - high.astype(F32)).astype(BF16), nothing], axis=0)
        total = mix(diagonal, line[j : j + 1], parts(first + j, high))
        total = total + mix(diagonal, rest[j : j + 1], low)
        out[first + j, :HEADS, :] = total.astype(BF16)


def merge_kernel(in_ref, out):
    diagonal = head_diagonal()
    for y in range(NY):
        level = jnp.sum(in_ref[:, y, HEADS:, :].astype(F32), axis=1)
        weights = jnp.exp2(level - jnp.max(level, axis=0, keepdims=True))
        weights = weights / jnp.sum(weights, axis=0, keepdims=True)
        total = jnp.zeros((HEADS, HD), F32)
        for k in range(0, NZ, 4):
            line = four_lines([weights[k + i : k + i + 1] for i in range(4)])
            shares = in_ref[k : k + 4, y, :HEADS, :].reshape(4 * HEADS, HD)
            total = total + mix(diagonal, line, shares)
        out[y] = total.astype(BF16)


def kernel(
    body, name, outs, args, scalars=0, scratch=(), limit=8, us=0.5, in_specs=None, out_specs=None
):
    return pl.pallas_call(
        body,
        out_shape=outs,
        in_specs=in_specs or [SMEM] * scalars + [VMEM] * (len(args) - scalars),
        out_specs=out_specs if out_specs is not None else jax.tree.map(lambda _: VMEM, outs),
        scratch_shapes=list(scratch),
        compiler_params=pltpu.CompilerParams(vmem_limit_bytes=limit * MIB),
        cost_estimate=pl.CostEstimate(
            flops=int(us * 8e8), bytes_accessed=int(us * 1e6), transcendentals=0
        ),
        name=name,
    )(*args)


def send(array, axis, shift):
    size = {"x": NX, "z": NZ, "c": NC, "y": NY}[axis]
    return lax.ppermute(array, axis, [(i, (i + shift) % size) for i in range(size)])


def shaped(*shape, dtype=BF16):
    return jax.ShapeDtypeStruct(shape, dtype)


def local(
    queries,
    new_keys,
    new_values,
    sink_keys,
    sink_values,
    window_keys,
    window_values,
    window_len,
    root_keys,
    root_values,
    prefix_keys,
    prefix_values,
    tenant_of,
    owner,
):
    spread = jnp.broadcast_to(queries.reshape(1, NY, HEADS, HD), (NZ, NY, HEADS, HD))
    q = lax.all_to_all(
        spread.reshape(COLUMN, HEADS, HD), ("z", "y"), split_axis=0, concat_axis=0, tiled=True
    )

    k_left, v_left = send(root_keys, "x", 1), send(root_values, "x", 1)
    k_right, v_right = send(root_keys, "x", -1), send(root_values, "x", -1)
    k_far, v_far = send(k_left, "x", 1), send(v_right, "x", -1)
    (rk, rv, pk, pv), (k_left, v_left, k_right, v_right) = lax.optimization_barrier(
        (
            (root_keys, root_values, prefix_keys, prefix_values),
            (k_left, v_left, k_right, v_right),
        )
    )
    own, *others = [
        (k, send(k, "c", 1), v, send(v, "c", 1))
        for k, v in ((rk, rv), (k_left, v_left), (k_right, v_right), (k_far, v_far))
    ]
    pk1, pv1 = send(pk, "c", 1), send(pv, "c", 1)

    i32 = jnp.int32
    plan, rounds = kernel(
        prepare_kernel,
        "prepare",
        [shaped(2 * NX + 1, COLUMN + 1, dtype=i32), shaped(1, dtype=i32)],
        [tenant_of, owner, tenant_of.reshape(1, -1), owner.reshape(1, -1)],
        scalars=2,
        out_specs=[SMEM] * 2,
        us=2,
    )
    anywhere = pl.BlockSpec(memory_space=pl.ANY)
    near, home_share, home_level = kernel(
        near_kernel,
        "near",
        [
            shaped(COLUMN, ROWS, HD),
            shaped(HOME, HEADS, HD, dtype=F32),
            shaped(HOME, HD, dtype=F32),
        ],
        [
            window_len,
            q,
            *own,
            window_keys,
            window_values,
            sink_keys,
            sink_values,
            new_keys,
            new_values,
        ],
        in_specs=[SMEM] + [VMEM] * 5 + [anywhere] * 2 + [VMEM] * 4,
        scratch=[
            pltpu.VMEM((KV, 1024, 2 * HD), BF16),
            pltpu.VMEM(window_keys.shape, BF16),
            pltpu.VMEM(window_values.shape, BF16),
            pltpu.SemaphoreType.DMA((2,)),
        ],
        limit=24,
        us=4,
    )

    def scalar_kernel(body, name, outs, turn, args, **options):
        if isinstance(turn, int):
            return kernel(
                lambda plan, *refs: body(plan, turn, *refs),
                name,
                outs,
                [plan, *args],
                scalars=1,
                **options,
            )
        return kernel(body, name, outs, [plan, turn, *args], scalars=2, **options)

    def prefix_answers(turn):
        picked = scalar_kernel(
            select_kernel, "select", shaped(NX * ROOM, HEADS, HD), turn, [q]
        )
        asked = lax.all_to_all(picked, "x", split_axis=0, concat_axis=0, tiled=True)
        answer = scalar_kernel(
            prefix_kernel,
            "prefix",
            shaped(NX * ROOM, ROWS, HD),
            turn,
            [asked, pk, pk1, pv, pv1],
            scratch=[
                pltpu.VMEM((2, KV, MEMBER, GROUP, HD), BF16),
                pltpu.SMEM((2, NX * ROOM + 1), i32),
            ],
            us=2,
        )
        return lax.all_to_all(answer, "x", split_axis=0, concat_axis=0, tiled=True)

    def more(state):
        turn, before = state
        after = scalar_kernel(
            scatter_kernel,
            "scatter",
            shaped(COLUMN, ROWS, HD),
            turn,
            [prefix_answers(turn), before],
        )
        return turn + 1, after

    row = lax.broadcasted_iota(i32, (COLUMN, ROWS, HD), 1)
    none = jnp.where(row == HEADS, FLOOR, 0.0).astype(BF16)
    answers = prefix_answers(0)
    _, later = lax.while_loop(
        lambda state: state[0][0] < rounds[0], more, (jnp.ones((1,), i32), none)
    )
    far = kernel(
        far_kernel,
        "far",
        shaped(COLUMN, ROWS, HD),
        [q, *(ref for block in others for ref in block)],
        scratch=[pltpu.VMEM((KV, (NX - 1) * 1024, 2 * HD), BF16)],
        limit=32,
        us=6,
    )
    merged = kernel(
        merge_row_kernel,
        "merge_row",
        shaped(COLUMN, ROWS, HD),
        [plan, near, far, answers, later, home_share, home_level],
        scalars=1,
        scratch=[
            pltpu.VMEM((COLUMN, ROWS, HD), BF16),
            pltpu.VMEM((COLUMN, HD), F32),
            pltpu.VMEM((3, COLUMN, HD), F32),
        ],
        us=1.5,
    )
    back = lax.all_to_all(merged, ("z", "y"), split_axis=0, concat_axis=0, tiled=True)
    out = kernel(
        merge_kernel, "merge", shaped(NY, HEADS, HD), [back.reshape(NZ, NY, ROWS, HD)]
    )
    return out.reshape(1, NY * HEADS * HD)


def solution(mesh):
    fine = Mesh(mesh.devices.reshape(NX, NZ, NC, NY), ("x", "z", "c", "y"))
    session = ("x", "z", "c")
    placed = (
        P(("x", "z", "c", "y"), None),
        P(session, "y"),
        P(session, "y"),
        P(session, None, "y"),
        P(session, None, "y"),
        P(session, None, "y"),
        P(session, None, "y"),
        P(session),
        P(session, "y"),
        P(session, "y"),
        P(session, "y"),
        P(session, "y"),
        P(),
        P(),
    )
    return jax.shard_map(
        local,
        mesh=fine,
        in_specs=placed,
        out_specs=P(("x", "z", "c", "y"), None),
        check_vma=False,
    )
```

```python
import functools
import math

import jax
import jax.numpy as jnp
from jax import lax
from jax.experimental import pallas as pl
from jax.experimental.pallas import tpu as pltpu
from jax.sharding import Mesh, PartitionSpec as P

HD = 128
GROUP = 16
KV = 2
HEADS = KV * GROUP
HOME = 4
NX, NZ, NC, NY = 4, 8, 2, 4
ROWS = 40
SCALE2 = HD**-0.5 * math.log2(math.e)
FLOOR = -1e30
COLUMN = NZ * HOME
MEMBER = 8
ROOM = 8
MIB = 2**20

NT = (((1,), (1,)), ((), ()))
VMEM = pl.BlockSpec(memory_space=pltpu.VMEM)
SMEM = pl.BlockSpec(memory_space=pltpu.SMEM)
BF16 = jnp.bfloat16
F32 = jnp.float32


def scores_of(query, keys):
    return lax.dot_general(query, keys, NT, preferred_element_type=F32)


def dot(a, b):
    return jnp.dot(a, b, preferred_element_type=F32)


def iota(shape, dim):
    return lax.broadcasted_iota(jnp.int32, shape, dim)


def head_diagonal():
    return (iota((HEADS, HD), 1) % HEADS) == iota((HEADS, HD), 0)


def level_parts(level):
    first = level.astype(BF16).astype(F32)
    second = (level - first).astype(BF16).astype(F32)
    third = level - first - second
    row = iota((1, 8, HD), 1)
    parts = jnp.where(row == 2, third[:, None], 0.0)
    parts = jnp.where(row == 1, second[:, None], parts)
    return jnp.where(row == 0, first[:, None], parts).astype(BF16)


def prepare_kernel(tenant_ref, owner_ref, t_row, o_row, plan, rounds):
    x, z, c = lax.axis_index("x"), lax.axis_index("z"), lax.axis_index("c")
    zero = jnp.int32(0)

    def clear(i, _):
        for t in range(NX):
            plan[t, i] = zero
        return 0

    lax.fori_loop(0, COLUMN + 1, clear, 0, unroll=11)

    def slot_of(s, i):
        return owner_ref[tenant_ref[((s * NZ + (i >> 2)) * 2 + c) * HOME + (i & 3)]]

    def scan_send(i, found):
        slot = slot_of(x, i)
        target = jnp.where(((slot >> 1) & (NZ - 1)) == z, slot >> 4, NX)
        new = []
        for t in range(NX):
            plan[t, found[t]] = i
            new.append(found[t] + (target == t).astype(jnp.int32))
        return tuple(new)

    found = lax.fori_loop(0, COLUMN, scan_send, (zero,) * NX, unroll=8)
    for t in range(NX):
        plan[2 * NX, t] = found[t]

    mine = x * NZ + z

    def scan_recv(i, found):
        new = []
        for s in range(NX):
            slot = slot_of(s, i)
            plan[NX + s, found[s]] = (slot & 1) ^ c
            new.append(found[s] + ((slot >> 1) == mine).astype(jnp.int32))
        return tuple(new)

    found = lax.fori_loop(0, COLUMN, scan_recv, (zero,) * NX, unroll=4)
    for s in range(NX):
        plan[2 * NX, NX + s] = found[s]

    chats = NX * NC * COLUMN
    tenants = o_row.shape[1]
    o_col = jnp.sum(
        jnp.where(iota((tenants, tenants), 0) == iota((tenants, tenants), 1), o_row[...] >> 1, 0),
        axis=1,
        keepdims=True,
    )
    by_row = jnp.sum(
        jnp.where(t_row[...] == iota((tenants, chats), 0), o_col, 0), axis=0, keepdims=True
    )

    def key(chip, chat):
        place = chat >> 2
        return (((place >> 4) * 2 + (place & 1)) << 5) + chip

    row = key(by_row, iota((1, chats), 1))
    square = (chats, chats)
    col = jnp.sum(
        jnp.where(iota(square, 0) == iota(square, 1), row, 0), axis=1, keepdims=True
    )
    fullest = jnp.max(jnp.sum(jnp.where(col == row, 1.0, 0.0), axis=1, keepdims=True))
    rounds[0] = (fullest.astype(jnp.int32) + ROOM - 1) >> 3


def root_part(q_ref, blocks, ready, values, out):
    diagonal = head_diagonal()
    rows = COLUMN // 2

    def score(h, g, block):
        query = q_ref[h * rows : (h + 1) * rows, g * GROUP : (g + 1) * GROUP, :]
        return scores_of(query.reshape(rows * GROUP, HD), block[:512, g * HD : (g + 1) * HD])

    first = []
    for n, block in enumerate(blocks):
        ready(n)
        first.append(score(0, 0, block))
        for g in range(KV):
            values[g, n * 512 : (n + 1) * 512, :HD] = block[512:, g * HD : (g + 1) * HD]
            values[g, n * 512 : (n + 1) * 512, HD:] = jnp.ones((512, HD), BF16)
    for h in range(2):
        chats = slice(h * rows, (h + 1) * rows)
        line = None
        for g in range(KV):
            heads = slice(g * GROUP, (g + 1) * GROUP)
            scores = first if h + g == 0 else [score(h, g, block) for block in blocks]
            peak = functools.reduce(
                jnp.maximum, [jnp.max(s, axis=1, keepdims=True) for s in scores]
            )
            numer = None
            for n, s in enumerate(scores):
                weights = jnp.exp2((s - peak) * SCALE2).astype(BF16)
                part = dot(weights, values[g, n * 512 : (n + 1) * 512, :])
                numer = part if numer is None else numer + part
            total = numer[:, HD:]
            share = (numer[:, :HD] / total).astype(BF16)
            out[chats, heads, :] = share.reshape(rows, GROUP, HD)
            level = (peak * SCALE2 + jnp.log2(total)).reshape(rows, GROUP, HD)
            part = jnp.sum(jnp.where(diagonal[None, heads], level, 0.0), axis=1)
            line = part if line is None else line + part
        out[chats, HEADS:, :] = level_parts(line)


def fetch(sources, targets, sems):
    copies = [
        pltpu.make_async_copy(source, target, sems.at[n])
        for n, (source, target) in enumerate(zip(sources, targets))
    ]
    for copy in copies:
        copy.start()
    return copies


def home_part(length_ref, q_ref, wk, wv, sk, sv, nk, nv, share_ref, level_ref):
    diagonal = head_diagonal()
    first = lax.axis_index("z") * HOME
    pad = jnp.zeros((3, KV * HD), F32)
    few_k, few_v = (
        [
            jnp.concatenate([s[j].astype(F32), n[j : j + 1].astype(F32), pad]).astype(BF16)
            for j in range(HOME)
        ]
        for s, n in ((sk, nk), (sv, nv))
    )
    pairs = [(g, j) for g in range(KV) for j in range(HOME)]
    recent, few = [], []
    for g, j in pairs:
        lanes = slice(g * HD, (g + 1) * HD)
        query = q_ref[first + j, g * GROUP : (g + 1) * GROUP, :]
        used = iota((GROUP, 512), 1) < length_ref[j]
        recent.append(jnp.where(used, scores_of(query, wk[j, :, lanes]), FLOOR))
        few.append(scores_of(query, few_k[j][:, lanes]))
    recent = jnp.concatenate(recent, axis=0)
    few = jnp.concatenate(few, axis=0)
    few = jnp.where(iota(few.shape, 1) < 5, few, FLOOR)
    peak = jnp.maximum(jnp.max(recent, axis=1, keepdims=True), jnp.max(few, axis=1, keepdims=True))
    recent = jnp.exp2((recent - peak) * SCALE2)
    few = jnp.exp2((few - peak) * SCALE2)
    total = jnp.sum(recent, axis=1, keepdims=True) + jnp.sum(few, axis=1, keepdims=True)
    recent, few = recent.astype(BF16), few.astype(BF16)
    level = jnp.broadcast_to(peak * SCALE2 + jnp.log2(total), (KV * HOME * GROUP, HD))
    level = level.reshape(KV, HOME, GROUP, HD)
    line = None
    for g in range(KV):
        part = jnp.where(diagonal[None, g * GROUP : (g + 1) * GROUP], level[g], 0.0)
        part = jnp.sum(part, axis=1)
        line = part if line is None else line + part
    level_ref[...] = line
    for n, (g, j) in enumerate(pairs):
        lanes = slice(g * HD, (g + 1) * HD)
        rows = slice(n * GROUP, (n + 1) * GROUP)
        numer = dot(recent[rows], wv[j, :, lanes]) + dot(few[rows], few_v[j][:, lanes])
        share_ref[j, g * GROUP : (g + 1) * GROUP, :] = numer / total[rows]


def near_kernel(
    length_ref, q_hbm, own, other, wk, wv, sk, sv, nk, nv, out_hbm, share_hbm, level, *scratch
):
    q_ref, blocks, values, wks, wvs, out, share, sems = scratch
    copies = fetch(
        (q_hbm, own, other, wk, wv), (q_ref, blocks.at[0], blocks.at[1], wks, wvs), sems
    )
    copies[0].wait()
    root_part(
        q_ref, [blocks.at[n] for n in range(2)], lambda n: copies[n + 1].wait(), values, out
    )
    leave = [pltpu.make_async_copy(out, out_hbm, sems.at[5])]
    leave[0].start()
    copies[3].wait()
    copies[4].wait()
    home_part(length_ref, q_ref, wks, wvs, sk, sv, nk, nv, share, level)
    leave.append(pltpu.make_async_copy(share, share_hbm, sems.at[6]))
    leave[1].start()
    for copy in leave:
        copy.wait()


def far_kernel(q_hbm, *refs):
    *sources, out, q_ref, blocks, values, sems = refs
    targets = [blocks.at[n] for n in range(4)]
    targets += [blocks.at[n, pl.ds(i * 512, 512)] for n in (4, 5) for i in range(2)]
    copies = fetch((q_hbm, *sources), (q_ref, *targets), sems)
    copies[0].wait()

    def ready(n):
        for i in (n + 1,) if n < 4 else (2 * n - 3, 2 * n - 2):
            copies[i].wait()

    root_part(q_ref, [blocks.at[n] for n in range(6)], ready, values, out)


def select_kernel(plan, turn, q_hbm, out, sems):
    start = turn if isinstance(turn, int) else turn[0] * ROOM
    chats = [plan[t, start + e] for t in range(NX) for e in range(ROOM)]
    copies = fetch(
        [q_hbm.at[chat] for chat in chats], [out.at[n] for n in range(NX * ROOM)], sems
    )
    for copy in copies:
        copy.wait()


def prefix_kernel(plan, turn, q_hbm, pk0, pk1, pv0, pv1, out, q_ref, prefixes, qs, lists, sems):
    start = turn if isinstance(turn, int) else turn[0] * ROOM
    copies = fetch(
        (q_hbm, pk0, pk1, pv0, pv1), (q_ref, *(prefixes.at[n] for n in range(4))), sems
    )
    pk0, pk1, pv0, pv1 = (prefixes.at[n] for n in range(4))
    diagonal = head_diagonal()
    zero = jnp.int32(0)
    lists[0, 0] = zero
    lists[1, 0] = zero
    n0, n1 = zero, zero
    for s in range(NX):

        def scan(e, found, s=s):
            slot = plan[NX + s, start + e]
            lists[0, found[0]] = s * ROOM + e
            lists[1, found[1]] = s * ROOM + e
            return found[0] + 1 - slot, found[1] + slot

        left = jnp.clip(plan[2 * NX, NX + s] - start, 0, ROOM)
        n0, n1 = lax.fori_loop(0, left, scan, (n0, n1))
    slots = ((pk0, pv0, n0), (pk1, pv1, n1))
    for copy in copies:
        copy.wait()

    def step(b, _):
        results = []
        for i, (pk, pv, count) in enumerate(slots):
            last = jnp.maximum(count - 1, 0)
            chats = [lists[i, jnp.minimum(b * MEMBER + j, last)] for j in range(MEMBER)]
            line = None
            shares = []
            for g in range(KV):
                heads = slice(g * GROUP, (g + 1) * GROUP)
                lanes = slice(g * HD, (g + 1) * HD)
                for j, chat in enumerate(chats):
                    qs[i, g, j] = q_ref[chat, heads, :]
                scores = scores_of(qs[i, g].reshape(MEMBER * GROUP, HD), pk[:, lanes])
                peak = jnp.max(scores, axis=1, keepdims=True)
                weights = jnp.exp2((scores - peak) * SCALE2)
                total = jnp.sum(weights, axis=1, keepdims=True)
                numer = dot(weights.astype(BF16), pv[:, lanes])
                shares.append((numer / total).astype(BF16))
                level = jnp.broadcast_to(peak * SCALE2 + jnp.log2(total), (MEMBER * GROUP, HD))
                level = level.reshape(MEMBER, GROUP, HD)
                part = jnp.sum(jnp.where(diagonal[None, heads], level, 0.0), axis=1)
                line = part if line is None else line + part
            results.append((chats, shares, level_parts(line)))
        for (chats, shares, parts), (_, _, count) in zip(results, slots):

            @pl.when(b * MEMBER < count)
            def _(chats=chats, shares=shares, parts=parts):
                for j, chat in enumerate(chats):
                    for g in range(KV):
                        rows = slice(j * GROUP, (j + 1) * GROUP)
                        out[chat, g * GROUP : (g + 1) * GROUP, :] = shares[g][rows]
                    out[chat, HEADS:, :] = parts[j]

        return 0

    lax.fori_loop(0, (jnp.maximum(n0, n1) + MEMBER - 1) >> 3, step, 0)


def place_answers(plan, start, back, out):
    for t in range(NX):

        def place(e, _, t=t):
            out[plan[t, start + e]] = back[t * ROOM + e]
            return 0

        lax.fori_loop(0, jnp.clip(plan[2 * NX, t] - start, 0, ROOM), place, 0)


def scatter_kernel(plan, turn, back, before, out):
    out[...] = before[...]
    place_answers(plan, turn[0] * ROOM, back, out)


def weights_of(levels):
    top = functools.reduce(jnp.maximum, levels)
    weights = [jnp.exp2(v - top) for v in levels]
    total = functools.reduce(jnp.add, weights)
    return [w / total for w in weights], top + jnp.log2(total)


def read_level(ref):
    return jnp.sum(ref[:, HEADS:, :].astype(F32), axis=1)


def four_lines(weights):
    quarter = iota((1, HD), 1) // HEADS
    return functools.reduce(
        jnp.add, [jnp.where(quarter == i, w, 0.0) for i, w in enumerate(weights)]
    )


def mix(diagonal, line, shares):
    spread = jnp.where(diagonal, line, 0.0)
    high = spread.astype(BF16)
    low = (spread - high.astype(F32)).astype(BF16)
    return dot(high, shares) + dot(low, shares)


def merge_row_kernel(plan, near, far, back, before, share_ref, level_ref, out, prefix, lines, levels):
    diagonal = head_diagonal()
    prefix[...] = before[...]
    place_answers(plan, 0, back, prefix)
    level = [read_level(r) for r in (near, far, prefix)]
    weights, total = weights_of(level)
    line = four_lines(weights)
    for n, v in enumerate(level):
        levels[n] = v
    out[:, HEADS:, :] = level_parts(total)
    empty = jnp.zeros((HEADS, HD), BF16)

    def parts(i, fourth):
        sources = [near[i, :HEADS, :], far[i, :HEADS, :], prefix[i, :HEADS, :], fourth]
        return jnp.concatenate(sources, axis=0)

    for i in range(COLUMN):
        out[i, :HEADS, :] = mix(diagonal, line[i : i + 1], parts(i, empty)).astype(BF16)

    first = lax.axis_index("z") * HOME
    own = pl.ds(first, HOME)
    weights, total = weights_of([levels[n, own, :] for n in range(3)] + [level_ref[...]])
    line = four_lines(weights)
    rest = four_lines(weights[3:])
    out[own, HEADS:, :] = level_parts(total)
    nothing = jnp.zeros((3 * HEADS, HD), BF16)
    for j in range(HOME):
        home = share_ref[j]
        high = home.astype(BF16)
        low = jnp.concatenate([(home - high.astype(F32)).astype(BF16), nothing], axis=0)
        total = mix(diagonal, line[j : j + 1], parts(first + j, high))
        total = total + mix(diagonal, rest[j : j + 1], low)
        out[first + j, :HEADS, :] = total.astype(BF16)


def merge_kernel(in_ref, out):
    diagonal = head_diagonal()
    for y in range(NY):
        level = jnp.sum(in_ref[:, y, HEADS:, :].astype(F32), axis=1)
        weights = jnp.exp2(level - jnp.max(level, axis=0, keepdims=True))
        weights = weights / jnp.sum(weights, axis=0, keepdims=True)
        total = jnp.zeros((HEADS, HD), F32)
        for k in range(0, NZ, 4):
            line = four_lines([weights[k + i : k + i + 1] for i in range(4)])
            shares = in_ref[k : k + 4, y, :HEADS, :].reshape(4 * HEADS, HD)
            total = total + mix(diagonal, line, shares)
        out[y] = total.astype(BF16)


def kernel(
    body, name, outs, args, scalars=0, scratch=(), limit=8, us=0.5, in_specs=None, out_specs=None
):
    return pl.pallas_call(
        body,
        out_shape=outs,
        in_specs=in_specs or [SMEM] * scalars + [VMEM] * (len(args) - scalars),
        out_specs=out_specs if out_specs is not None else jax.tree.map(lambda _: VMEM, outs),
        scratch_shapes=list(scratch),
        compiler_params=pltpu.CompilerParams(vmem_limit_bytes=limit * MIB),
        cost_estimate=pl.CostEstimate(
            flops=int(us * 8e8), bytes_accessed=int(us * 1e6), transcendentals=0
        ),
        name=name,
    )(*args)


def send(array, axis, shift):
    size = {"x": NX, "z": NZ, "c": NC, "y": NY}[axis]
    return lax.ppermute(array, axis, [(i, (i + shift) % size) for i in range(size)])


def shaped(*shape, dtype=BF16):
    return jax.ShapeDtypeStruct(shape, dtype)


def local(
    queries,
    new_keys,
    new_values,
    sink_keys,
    sink_values,
    window_keys,
    window_values,
    window_len,
    root_keys,
    root_values,
    prefix_keys,
    prefix_values,
    tenant_of,
    owner,
):
    spread = jnp.broadcast_to(queries.reshape(1, NY, HEADS, HD), (NZ, NY, HEADS, HD))
    q = lax.all_to_all(
        spread.reshape(COLUMN, HEADS, HD), ("z", "y"), split_axis=0, concat_axis=0, tiled=True
    )

    root = jnp.concatenate([root_keys, root_values], axis=0)
    left, right = send(root, "x", 1), send(root, "x", -1)
    root1, pk1, pv1 = (send(a, "c", 1) for a in (root, prefix_keys, prefix_values))
    left, right, root1, tenant_of = lax.optimization_barrier((left, right, root1, tenant_of))
    far = [send(left[:512], "x", 1), send(right[512:], "x", -1)]
    left1, right1 = send(left, "c", 1), send(right, "c", 1)

    i32 = jnp.int32
    tenant_of, owner, _ = lax.optimization_barrier((tenant_of, owner, spread))
    plan, rounds = kernel(
        prepare_kernel,
        "prepare",
        [shaped(2 * NX + 1, COLUMN + 1, dtype=i32), shaped(1, dtype=i32)],
        [tenant_of, owner, tenant_of.reshape(1, -1), owner.reshape(1, -1)],
        scalars=2,
        out_specs=[SMEM] * 2,
        us=2,
    )
    anywhere = pl.BlockSpec(memory_space=pltpu.HBM)
    near, home_share, home_level = kernel(
        near_kernel,
        "near",
        [
            shaped(COLUMN, ROWS, HD),
            shaped(HOME, HEADS, HD, dtype=F32),
            shaped(HOME, HD, dtype=F32),
        ],
        [
            window_len,
            q,
            root,
            root1,
            window_keys,
            window_values,
            sink_keys,
            sink_values,
            new_keys,
            new_values,
        ],
        in_specs=[SMEM] + [anywhere] * 5 + [VMEM] * 4,
        out_specs=[anywhere, anywhere, VMEM],
        scratch=[
            pltpu.VMEM((COLUMN, HEADS, HD), BF16),
            pltpu.VMEM((2, 1024, KV * HD), BF16),
            pltpu.VMEM((KV, 1024, 2 * HD), BF16),
            pltpu.VMEM(window_keys.shape, BF16),
            pltpu.VMEM(window_values.shape, BF16),
            pltpu.VMEM((COLUMN, ROWS, HD), BF16),
            pltpu.VMEM((HOME, HEADS, HD), F32),
            pltpu.SemaphoreType.DMA((7,)),
        ],
        limit=16,
        us=4,
    )

    def scalar_kernel(body, name, outs, turn, args, rest=anywhere, **options):
        if isinstance(turn, int):
            whole, args = (lambda plan, *refs: body(plan, turn, *refs)), [plan, *args]
            scalars = 1
        else:
            whole, args, scalars = body, [plan, turn, *args], 2
        specs = [SMEM] * scalars + [rest] * (len(args) - scalars)
        return kernel(whole, name, outs, args, in_specs=specs, **options)

    def prefix_asked(turn):
        picked = scalar_kernel(
            select_kernel,
            "select",
            shaped(NX * ROOM, HEADS, HD),
            turn,
            [q],
            out_specs=anywhere,
            scratch=[pltpu.SemaphoreType.DMA((NX * ROOM,))],
        )
        return lax.all_to_all(picked, "x", split_axis=0, concat_axis=0, tiled=True)

    def prefix_answers(turn, asked):
        answer = scalar_kernel(
            prefix_kernel,
            "prefix",
            shaped(NX * ROOM, ROWS, HD),
            turn,
            [asked, prefix_keys, pk1, prefix_values, pv1],
            scratch=[
                pltpu.VMEM((NX * ROOM, HEADS, HD), BF16),
                pltpu.VMEM((4, *prefix_keys.shape), BF16),
                pltpu.VMEM((2, KV, MEMBER, GROUP, HD), BF16),
                pltpu.SMEM((2, NX * ROOM + 1), i32),
                pltpu.SemaphoreType.DMA((5,)),
            ],
            limit=12,
            us=2,
        )
        return lax.all_to_all(answer, "x", split_axis=0, concat_axis=0, tiled=True)

    def more(state):
        turn, before = state
        after = scalar_kernel(
            scatter_kernel,
            "scatter",
            shaped(COLUMN, ROWS, HD),
            turn,
            [prefix_answers(turn, prefix_asked(turn)), before],
            rest=VMEM,
        )
        return turn + 1, after

    row = lax.broadcasted_iota(i32, (COLUMN, ROWS, HD), 1)
    none = jnp.where(row == HEADS, FLOOR, 0.0).astype(BF16)
    asked = prefix_asked(0)
    others = [left, left1, right, right1, *far, *(send(f, "c", 1) for f in far)]
    answers = prefix_answers(0, asked)
    _, later = lax.while_loop(
        lambda state: state[0][0] < rounds[0], more, (jnp.ones((1,), i32), none)
    )
    rest = kernel(
        far_kernel,
        "far",
        shaped(COLUMN, ROWS, HD),
        [q, *others],
        in_specs=[anywhere] * 9,
        scratch=[
            pltpu.VMEM((COLUMN, HEADS, HD), BF16),
            pltpu.VMEM((6, 1024, KV * HD), BF16),
            pltpu.VMEM((KV, 6 * 512, 2 * HD), BF16),
            pltpu.SemaphoreType.DMA((9,)),
        ],
        limit=24,
        us=6,
    )
    merged = kernel(
        merge_row_kernel,
        "merge_row",
        shaped(COLUMN, ROWS, HD),
        [plan, near, rest, answers, later, home_share, home_level],
        scalars=1,
        scratch=[
            pltpu.VMEM((COLUMN, ROWS, HD), BF16),
            pltpu.VMEM((COLUMN, HD), F32),
            pltpu.VMEM((3, COLUMN, HD), F32),
        ],
        us=1.5,
    )
    back = lax.all_to_all(merged, ("z", "y"), split_axis=0, concat_axis=0, tiled=True)
    out = kernel(
        merge_kernel, "merge", shaped(NY, HEADS, HD), [back.reshape(NZ, NY, ROWS, HD)]
    )
    return out.reshape(1, NY * HEADS * HD)


def solution(mesh):
    fine = Mesh(mesh.devices.reshape(NX, NZ, NC, NY), ("x", "z", "c", "y"))
    session = ("x", "z", "c")
    placed = (
        P(("x", "z", "c", "y"), None),
        P(session, "y"),
        P(session, "y"),
        P(session, None, "y"),
        P(session, None, "y"),
        P(session, None, "y"),
        P(session, None, "y"),
        P(session),
        P(session, "y"),
        P(session, "y"),
        P(session, "y"),
        P(session, "y"),
        P(),
        P(),
    )
    return jax.shard_map(
        local,
        mesh=fine,
        in_specs=placed,
        out_specs=P(("x", "z", "c", "y"), None),
        check_vma=False,
    )
```

```python
import functools
import math

import jax
import jax.numpy as jnp
from jax import lax
from jax.experimental import pallas as pl
from jax.experimental.pallas import tpu as pltpu
from jax.sharding import Mesh, PartitionSpec as P

HD = 128
GROUP = 16
KV = 2
HEADS = KV * GROUP
HOME = 4
NX, NZ, NC, NY = 4, 8, 2, 4
ROWS = 40
SCALE2 = HD**-0.5 * math.log2(math.e)
FLOOR = -1e30
COLUMN = NZ * HOME
MEMBER = 8
ROOM = 8
MIB = 2**20

NT = (((1,), (1,)), ((), ()))
VMEM = pl.BlockSpec(memory_space=pltpu.VMEM)
SMEM = pl.BlockSpec(memory_space=pltpu.SMEM)
BF16 = jnp.bfloat16
F32 = jnp.float32


def scores_of(query, keys):
    return lax.dot_general(query, keys, NT, preferred_element_type=F32)


def dot(a, b):
    return jnp.dot(a, b, preferred_element_type=F32)


def iota(shape, dim):
    return lax.broadcasted_iota(jnp.int32, shape, dim)


def head_diagonal():
    return (iota((HEADS, HD), 1) % HEADS) == iota((HEADS, HD), 0)


def level_parts(level):
    first = level.astype(BF16).astype(F32)
    second = (level - first).astype(BF16).astype(F32)
    third = level - first - second
    row = iota((1, 8, HD), 1)
    parts = jnp.where(row == 2, third[:, None], 0.0)
    parts = jnp.where(row == 1, second[:, None], parts)
    return jnp.where(row == 0, first[:, None], parts).astype(BF16)


def spread_kernel(q_ref, out):
    rows = q_ref[...].astype(F32).reshape(NY * HEADS, HD).astype(BF16).reshape(NY, HEADS, HD)
    for z in range(NZ):
        out[z] = rows


def prepare_kernel(tenant_ref, owner_ref, t_row, o_row, plan, rounds):
    x, z, c = lax.axis_index("x"), lax.axis_index("z"), lax.axis_index("c")
    zero = jnp.int32(0)

    def clear(i, _):
        for t in range(NX):
            plan[t, i] = zero
        return 0

    lax.fori_loop(0, COLUMN + 1, clear, 0, unroll=11)

    def slot_of(s, i):
        return owner_ref[tenant_ref[((s * NZ + (i >> 2)) * 2 + c) * HOME + (i & 3)]]

    def scan_send(i, found):
        slot = slot_of(x, i)
        target = jnp.where(((slot >> 1) & (NZ - 1)) == z, slot >> 4, NX)
        new = []
        for t in range(NX):
            plan[t, found[t]] = i
            new.append(found[t] + (target == t).astype(jnp.int32))
        return tuple(new)

    found = lax.fori_loop(0, COLUMN, scan_send, (zero,) * NX, unroll=8)
    for t in range(NX):
        plan[2 * NX, t] = found[t]

    mine = x * NZ + z

    def scan_recv(i, found):
        new = []
        for s in range(NX):
            slot = slot_of(s, i)
            plan[NX + s, found[s]] = (slot & 1) ^ c
            new.append(found[s] + ((slot >> 1) == mine).astype(jnp.int32))
        return tuple(new)

    found = lax.fori_loop(0, COLUMN, scan_recv, (zero,) * NX, unroll=4)
    for s in range(NX):
        plan[2 * NX, NX + s] = found[s]

    chats = NX * NC * COLUMN
    tenants = o_row.shape[1]
    o_col = jnp.sum(
        jnp.where(iota((tenants, tenants), 0) == iota((tenants, tenants), 1), o_row[...] >> 1, 0),
        axis=1,
        keepdims=True,
    )
    by_row = jnp.sum(
        jnp.where(t_row[...] == iota((tenants, chats), 0), o_col, 0), axis=0, keepdims=True
    )

    def key(chip, chat):
        place = chat >> 2
        return (((place >> 4) * 2 + (place & 1)) << 5) + chip

    row = key(by_row, iota((1, chats), 1))
    square = (chats, chats)
    col = jnp.sum(
        jnp.where(iota(square, 0) == iota(square, 1), row, 0), axis=1, keepdims=True
    )
    fullest = jnp.max(jnp.sum(jnp.where(col == row, 1.0, 0.0), axis=1, keepdims=True))
    rounds[0] = (fullest.astype(jnp.int32) + ROOM - 1) >> 3


def root_part(q_ref, blocks, values, out):
    for g in range(KV):
        for n, (_, v) in enumerate(blocks):
            rows = slice(n * 512, (n + 1) * 512)
            values[g, rows, :HD] = v[:, g * HD : (g + 1) * HD]
            values[g, rows, HD:] = jnp.ones((512, HD), BF16)
    diagonal = head_diagonal()
    rows = COLUMN // 2
    for h in range(2):
        chats = slice(h * rows, (h + 1) * rows)
        line = None
        for g in range(KV):
            heads = slice(g * GROUP, (g + 1) * GROUP)
            lanes = slice(g * HD, (g + 1) * HD)
            query = q_ref[chats, heads, :].reshape(rows * GROUP, HD)
            scores = [scores_of(query, k[:, lanes]) for k, _ in blocks]
            peak = functools.reduce(
                jnp.maximum, [jnp.max(s, axis=1, keepdims=True) for s in scores]
            )
            numer = None
            for n, s in enumerate(scores):
                weights = jnp.exp2((s - peak) * SCALE2).astype(BF16)
                part = dot(weights, values[g, n * 512 : (n + 1) * 512, :])
                numer = part if numer is None else numer + part
            total = numer[:, HD:]
            share = (numer[:, :HD] / total).astype(BF16)
            out[chats, heads, :] = share.reshape(rows, GROUP, HD)
            level = (peak * SCALE2 + jnp.log2(total)).reshape(rows, GROUP, HD)
            part = jnp.sum(jnp.where(diagonal[None, heads], level, 0.0), axis=1)
            line = part if line is None else line + part
        out[chats, HEADS:, :] = level_parts(line)


def home_part(length_ref, q_ref, wk, wv, sk, sv, nk, nv, share_ref, level_ref):
    diagonal = head_diagonal()
    first = lax.axis_index("z") * HOME
    pad = jnp.zeros((3, KV * HD), F32)
    few_k, few_v = (
        [
            jnp.concatenate([s[j].astype(F32), n[j : j + 1].astype(F32), pad]).astype(BF16)
            for j in range(HOME)
        ]
        for s, n in ((sk, nk), (sv, nv))
    )
    pairs = [(g, j) for g in range(KV) for j in range(HOME)]
    recent, few = [], []
    for g, j in pairs:
        lanes = slice(g * HD, (g + 1) * HD)
        query = q_ref[first + j, g * GROUP : (g + 1) * GROUP, :]
        used = iota((GROUP, 512), 1) < length_ref[j]
        recent.append(jnp.where(used, scores_of(query, wk[j, :, lanes]), FLOOR))
        few.append(scores_of(query, few_k[j][:, lanes]))
    recent = jnp.concatenate(recent, axis=0)
    few = jnp.concatenate(few, axis=0)
    few = jnp.where(iota(few.shape, 1) < 5, few, FLOOR)
    peak = jnp.maximum(jnp.max(recent, axis=1, keepdims=True), jnp.max(few, axis=1, keepdims=True))
    recent = jnp.exp2((recent - peak) * SCALE2)
    few = jnp.exp2((few - peak) * SCALE2)
    total = jnp.sum(recent, axis=1, keepdims=True) + jnp.sum(few, axis=1, keepdims=True)
    recent, few = recent.astype(BF16), few.astype(BF16)
    level = jnp.broadcast_to(peak * SCALE2 + jnp.log2(total), (KV * HOME * GROUP, HD))
    level = level.reshape(KV, HOME, GROUP, HD)
    line = None
    for g in range(KV):
        part = jnp.where(diagonal[None, g * GROUP : (g + 1) * GROUP], level[g], 0.0)
        part = jnp.sum(part, axis=1)
        line = part if line is None else line + part
    level_ref[...] = line
    for n, (g, j) in enumerate(pairs):
        lanes = slice(g * HD, (g + 1) * HD)
        rows = slice(n * GROUP, (n + 1) * GROUP)
        numer = dot(recent[rows], wv[j, :, lanes]) + dot(few[rows], few_v[j][:, lanes])
        share_ref[j, g * GROUP : (g + 1) * GROUP, :] = numer / total[rows]


def near_kernel(q_ref, k, v, out, values):
    root_part(q_ref, [(k, v)], values, out)


def far_kernel(length_ref, q_ref, *refs):
    *blocks, sk, sv, nk, nv, wk, wv, out, share, level, values, wks, wvs, sems = refs
    copies = [
        pltpu.make_async_copy(wk, wks, sems.at[0]),
        pltpu.make_async_copy(wv, wvs, sems.at[1]),
    ]
    for copy in copies:
        copy.start()
    root_part(q_ref, list(zip(blocks[::2], blocks[1::2])), values, out)
    for copy in copies:
        copy.wait()
    home_part(length_ref, q_ref, wks, wvs, sk, sv, nk, nv, share, level)


def select_kernel(plan, turn, q_ref, out):
    start = turn if isinstance(turn, int) else turn[0] * ROOM
    chats = [plan[t, start + e] for t in range(NX) for e in range(ROOM)]
    for n, chat in enumerate(chats):
        out[n] = q_ref[chat]


def prefix_kernel(plan, turn, q_ref, pk0, pk1, pv0, pv1, out, qs, lists):
    start = turn if isinstance(turn, int) else turn[0] * ROOM
    diagonal = head_diagonal()
    zero = jnp.int32(0)
    lists[0, 0] = zero
    lists[1, 0] = zero
    n0, n1 = zero, zero
    for s in range(NX):

        def scan(e, found, s=s):
            slot = plan[NX + s, start + e]
            lists[0, found[0]] = s * ROOM + e
            lists[1, found[1]] = s * ROOM + e
            return found[0] + 1 - slot, found[1] + slot

        left = jnp.clip(plan[2 * NX, NX + s] - start, 0, ROOM)
        n0, n1 = lax.fori_loop(0, left, scan, (n0, n1))
    slots = ((pk0, pv0, n0), (pk1, pv1, n1))

    def step(b, _):
        results = []
        for i, (pk, pv, count) in enumerate(slots):
            last = jnp.maximum(count - 1, 0)
            chats = [lists[i, jnp.minimum(b * MEMBER + j, last)] for j in range(MEMBER)]
            line = None
            shares = []
            for g in range(KV):
                heads = slice(g * GROUP, (g + 1) * GROUP)
                lanes = slice(g * HD, (g + 1) * HD)
                for j, chat in enumerate(chats):
                    qs[i, g, j] = q_ref[chat, heads, :]
                scores = scores_of(qs[i, g].reshape(MEMBER * GROUP, HD), pk[:, lanes])
                peak = jnp.max(scores, axis=1, keepdims=True)
                weights = jnp.exp2((scores - peak) * SCALE2)
                total = jnp.sum(weights, axis=1, keepdims=True)
                numer = dot(weights.astype(BF16), pv[:, lanes])
                shares.append((numer / total).astype(BF16))
                level = jnp.broadcast_to(peak * SCALE2 + jnp.log2(total), (MEMBER * GROUP, HD))
                level = level.reshape(MEMBER, GROUP, HD)
                part = jnp.sum(jnp.where(diagonal[None, heads], level, 0.0), axis=1)
                line = part if line is None else line + part
            results.append((chats, shares, level_parts(line)))
        for (chats, shares, parts), (_, _, count) in zip(results, slots):

            @pl.when(b * MEMBER < count)
            def _(chats=chats, shares=shares, parts=parts):
                for j, chat in enumerate(chats):
                    for g in range(KV):
                        rows = slice(j * GROUP, (j + 1) * GROUP)
                        out[chat, g * GROUP : (g + 1) * GROUP, :] = shares[g][rows]
                    out[chat, HEADS:, :] = parts[j]

        return 0

    lax.fori_loop(0, (jnp.maximum(n0, n1) + MEMBER - 1) >> 3, step, 0)


def place_answers(plan, start, back, out):
    for t in range(NX):

        def place(e, _, t=t):
            out[plan[t, start + e]] = back[t * ROOM + e]
            return 0

        lax.fori_loop(0, jnp.clip(plan[2 * NX, t] - start, 0, ROOM), place, 0)


def scatter_kernel(plan, turn, back, before, out):
    out[...] = before[...]
    place_answers(plan, turn[0] * ROOM, back, out)


def weights_of(levels):
    top = functools.reduce(jnp.maximum, levels)
    weights = [jnp.exp2(v - top) for v in levels]
    total = functools.reduce(jnp.add, weights)
    return [w / total for w in weights], top + jnp.log2(total)


def read_level(ref):
    return jnp.sum(ref[:, HEADS:, :].astype(F32), axis=1)


def four_lines(weights):
    quarter = iota((1, HD), 1) // HEADS
    return functools.reduce(
        jnp.add, [jnp.where(quarter == i, w, 0.0) for i, w in enumerate(weights)]
    )


def mix(diagonal, line, shares):
    spread = jnp.where(diagonal, line, 0.0)
    high = spread.astype(BF16)
    low = (spread - high.astype(F32)).astype(BF16)
    return dot(high, shares) + dot(low, shares)


def merge_row_kernel(plan, near, far, back, before, share_ref, level_ref, out, prefix, lines, levels):
    diagonal = head_diagonal()
    prefix[...] = before[...]
    place_answers(plan, 0, back, prefix)
    level = [read_level(r) for r in (near, far, prefix)]
    weights, total = weights_of(level)
    line = four_lines(weights)
    for n, v in enumerate(level):
        levels[n] = v
    out[:, HEADS:, :] = level_parts(total)
    empty = jnp.zeros((HEADS, HD), BF16)

    def parts(i, fourth):
        sources = [near[i, :HEADS, :], far[i, :HEADS, :], prefix[i, :HEADS, :], fourth]
        return jnp.concatenate(sources, axis=0)

    for i in range(COLUMN):
        out[i, :HEADS, :] = mix(diagonal, line[i : i + 1], parts(i, empty)).astype(BF16)

    first = lax.axis_index("z") * HOME
    own = pl.ds(first, HOME)
    weights, total = weights_of([levels[n, own, :] for n in range(3)] + [level_ref[...]])
    line = four_lines(weights)
    rest = four_lines(weights[3:])
    out[own, HEADS:, :] = level_parts(total)
    nothing = jnp.zeros((3 * HEADS, HD), BF16)
    for j in range(HOME):
        home = share_ref[j]
        high = home.astype(BF16)
        low = jnp.concatenate([(home - high.astype(F32)).astype(BF16), nothing], axis=0)
        total = mix(diagonal, line[j : j + 1], parts(first + j, high))
        total = total + mix(diagonal, rest[j : j + 1], low)
        out[first + j, :HEADS, :] = total.astype(BF16)


def merge_kernel(in_ref, out):
    diagonal = head_diagonal()
    merged = []
    for y in range(NY):
        level = jnp.sum(in_ref[:, y, HEADS:, :].astype(F32), axis=1)
        weights = jnp.exp2(level - jnp.max(level, axis=0, keepdims=True))
        weights = weights / jnp.sum(weights, axis=0, keepdims=True)
        total = jnp.zeros((HEADS, HD), F32)
        for k in range(0, NZ, 4):
            line = four_lines([weights[k + i : k + i + 1] for i in range(4)])
            shares = in_ref[k : k + 4, y, :HEADS, :].reshape(4 * HEADS, HD)
            total = total + mix(diagonal, line, shares)
        merged.append(total)
    out[...] = jnp.concatenate(merged, axis=0).reshape(1, NY * HEADS * HD).astype(BF16)


def kernel(
    body, name, outs, args, scalars=0, scratch=(), limit=58, us=0.5, in_specs=None, out_specs=None
):
    return pl.pallas_call(
        body,
        out_shape=outs,
        in_specs=in_specs or [SMEM] * scalars + [VMEM] * (len(args) - scalars),
        out_specs=out_specs if out_specs is not None else jax.tree.map(lambda _: VMEM, outs),
        scratch_shapes=list(scratch),
        compiler_params=pltpu.CompilerParams(vmem_limit_bytes=limit * MIB),
        cost_estimate=pl.CostEstimate(
            flops=int(us * 8e8), bytes_accessed=int(us * 1e6), transcendentals=0
        ),
        name=name,
    )(*args)


def send(array, axis, shift):
    size = {"x": NX, "z": NZ, "c": NC, "y": NY}[axis]
    return lax.ppermute(array, axis, [(i, (i + shift) % size) for i in range(size)])


def shaped(*shape, dtype=BF16):
    return jax.ShapeDtypeStruct(shape, dtype)


def local(
    queries,
    new_keys,
    new_values,
    sink_keys,
    sink_values,
    window_keys,
    window_values,
    window_len,
    root_keys,
    root_values,
    prefix_keys,
    prefix_values,
    tenant_of,
    owner,
):
    spread = kernel(spread_kernel, "spread", shaped(NZ, NY, HEADS, HD), [queries])
    q = lax.all_to_all(
        spread.reshape(COLUMN, HEADS, HD), ("z", "y"), split_axis=0, concat_axis=0, tiled=True
    )

    swapped = [send(a, "c", 1) for a in (root_keys, root_values, prefix_keys, prefix_values)]
    (rk, rv), (rk1, rv1, pk1, pv1) = lax.optimization_barrier(
        ((root_keys, root_values), swapped)
    )
    k_left, v_left = send(rk, "x", 1), send(rv, "x", 1)
    k_right, v_right = send(rk, "x", -1), send(rv, "x", -1)

    i32 = jnp.int32
    plan, rounds = kernel(
        prepare_kernel,
        "prepare",
        [shaped(2 * NX + 1, COLUMN + 1, dtype=i32), shaped(1, dtype=i32)],
        [tenant_of, owner, tenant_of.reshape(1, -1), owner.reshape(1, -1)],
        scalars=2,
        out_specs=[SMEM] * 2,
        us=2,
    )
    def scalar_kernel(body, name, outs, turn, args, **options):
        if isinstance(turn, int):
            return kernel(
                lambda plan, *refs: body(plan, turn, *refs),
                name,
                outs,
                [plan, *args],
                scalars=1,
                **options,
            )
        return kernel(body, name, outs, [plan, turn, *args], scalars=2, **options)

    def prefix_picked(turn):
        return scalar_kernel(select_kernel, "select", shaped(NX * ROOM, HEADS, HD), turn, [q])

    picked = prefix_picked(0)
    near_q, _ = lax.optimization_barrier((q, picked))
    near = kernel(
        near_kernel,
        "near",
        shaped(COLUMN, ROWS, HD),
        [near_q, root_keys, root_values],
        scratch=[pltpu.VMEM((KV, 512, 2 * HD), BF16)],
        us=1.5,
    )
    moved = (k_left, v_left, k_right, v_right)
    moved, near = lax.optimization_barrier((moved, near))
    k_left, v_left, k_right, v_right = moved
    k_far, v_far = send(k_left, "x", 1), send(v_right, "x", -1)
    others = [(rk1, rv1)]
    for k, v in ((k_left, v_left), (k_right, v_right), (k_far, v_far)):
        others += [(k, v), (send(k, "c", 1), send(v, "c", 1))]

    def prefix_answers(turn, picked):
        asked = lax.all_to_all(picked, "x", split_axis=0, concat_axis=0, tiled=True)
        answer = scalar_kernel(
            prefix_kernel,
            "prefix",
            shaped(NX * ROOM, ROWS, HD),
            turn,
            [asked, prefix_keys, pk1, prefix_values, pv1],
            scratch=[
                pltpu.VMEM((2, KV, MEMBER, GROUP, HD), BF16),
                pltpu.SMEM((2, NX * ROOM + 1), i32),
            ],
            limit=12,
            us=2,
        )
        return lax.all_to_all(answer, "x", split_axis=0, concat_axis=0, tiled=True)

    def more(state):
        turn, before = state
        after = scalar_kernel(
            scatter_kernel,
            "scatter",
            shaped(COLUMN, ROWS, HD),
            turn,
            [prefix_answers(turn, prefix_picked(turn)), before],
        )
        return turn + 1, after

    row = lax.broadcasted_iota(i32, (COLUMN, ROWS, HD), 1)
    none = jnp.where(row == HEADS, FLOOR, 0.0).astype(BF16)
    answers = prefix_answers(0, picked)
    _, later = lax.while_loop(
        lambda state: state[0][0] < rounds[0], more, (jnp.ones((1,), i32), none)
    )
    far, home_share, home_level = kernel(
        far_kernel,
        "far",
        [
            shaped(COLUMN, ROWS, HD),
            shaped(HOME, HEADS, HD, dtype=F32),
            shaped(HOME, HD, dtype=F32),
        ],
        [
            window_len,
            q,
            *(ref for block in others for ref in block),
            sink_keys,
            sink_values,
            new_keys,
            new_values,
            window_keys,
            window_values,
        ],
        in_specs=[SMEM] + [VMEM] * (4 * NX + 3) + [pl.BlockSpec(memory_space=pl.ANY)] * 2,
        scratch=[
            pltpu.VMEM((KV, (2 * NX - 1) * 512, 2 * HD), BF16),
            pltpu.VMEM(window_keys.shape, BF16),
            pltpu.VMEM(window_values.shape, BF16),
            pltpu.SemaphoreType.DMA((2,)),
        ],
        us=8,
    )
    merged = kernel(
        merge_row_kernel,
        "merge_row",
        shaped(COLUMN, ROWS, HD),
        [plan, near, far, answers, later, home_share, home_level],
        scalars=1,
        scratch=[
            pltpu.VMEM((COLUMN, ROWS, HD), BF16),
            pltpu.VMEM((COLUMN, HD), F32),
            pltpu.VMEM((3, COLUMN, HD), F32),
        ],
        us=1.5,
    )
    back = lax.all_to_all(merged, ("z", "y"), split_axis=0, concat_axis=0, tiled=True)
    out = kernel(
        merge_kernel, "merge", shaped(1, NY * HEADS * HD), [back.reshape(NZ, NY, ROWS, HD)]
    )
    return out


def solution(mesh):
    fine = Mesh(mesh.devices.reshape(NX, NZ, NC, NY), ("x", "z", "c", "y"))
    session = ("x", "z", "c")
    placed = (
        P(("x", "z", "c", "y"), None),
        P(session, "y"),
        P(session, "y"),
        P(session, None, "y"),
        P(session, None, "y"),
        P(session, None, "y"),
        P(session, None, "y"),
        P(session),
        P(session, "y"),
        P(session, "y"),
        P(session, "y"),
        P(session, "y"),
        P(),
        P(),
    )
    return jax.shard_map(
        local,
        mesh=fine,
        in_specs=placed,
        out_specs=P(("x", "z", "c", "y"), None),
        check_vma=False,
    )
```

```python
import functools
import math

import jax
import jax.numpy as jnp
from jax import lax
from jax.experimental import pallas as pl
from jax.experimental.pallas import tpu as pltpu
from jax.sharding import Mesh, PartitionSpec as P

HD = 128
GROUP = 16
KV = 2
HEADS = KV * GROUP
HOME = 4
NX, NZ, NC, NY = 4, 8, 2, 4
ROWS = 40
SCALE2 = HD**-0.5 * math.log2(math.e)
FLOOR = -1e30
COLUMN = NZ * HOME
MEMBER = 8
ROOM = 8
MIB = 2**20

NT = (((1,), (1,)), ((), ()))
VMEM = pl.BlockSpec(memory_space=pltpu.VMEM)
SMEM = pl.BlockSpec(memory_space=pltpu.SMEM)
BF16 = jnp.bfloat16
F32 = jnp.float32


def scores_of(query, keys):
    return lax.dot_general(query, keys, NT, preferred_element_type=F32)


def dot(a, b):
    return jnp.dot(a, b, preferred_element_type=F32)


def iota(shape, dim):
    return lax.broadcasted_iota(jnp.int32, shape, dim)


def head_diagonal():
    return (iota((HEADS, HD), 1) % HEADS) == iota((HEADS, HD), 0)


def level_parts(level):
    first = level.astype(BF16).astype(F32)
    second = (level - first).astype(BF16).astype(F32)
    third = level - first - second
    row = iota((1, 8, HD), 1)
    parts = jnp.where(row == 2, third[:, None], 0.0)
    parts = jnp.where(row == 1, second[:, None], parts)
    return jnp.where(row == 0, first[:, None], parts).astype(BF16)


def prepare_kernel(tenant_ref, owner_ref, t_row, o_row, plan, rounds):
    x, z, c = lax.axis_index("x"), lax.axis_index("z"), lax.axis_index("c")
    zero = jnp.int32(0)

    def clear(i, _):
        for t in range(NX):
            plan[t, i] = zero
        return 0

    lax.fori_loop(0, COLUMN + 1, clear, 0, unroll=11)

    def slot_of(s, i):
        return owner_ref[tenant_ref[((s * NZ + (i >> 2)) * 2 + c) * HOME + (i & 3)]]

    def scan_send(i, found):
        slot = slot_of(x, i)
        target = jnp.where(((slot >> 1) & (NZ - 1)) == z, slot >> 4, NX)
        new = []
        for t in range(NX):
            plan[t, found[t]] = i
            new.append(found[t] + (target == t).astype(jnp.int32))
        return tuple(new)

    found = lax.fori_loop(0, COLUMN, scan_send, (zero,) * NX, unroll=8)
    for t in range(NX):
        plan[2 * NX, t] = found[t]

    mine = x * NZ + z

    def scan_recv(i, found):
        new = []
        for s in range(NX):
            slot = slot_of(s, i)
            plan[NX + s, found[s]] = (slot & 1) ^ c
            new.append(found[s] + ((slot >> 1) == mine).astype(jnp.int32))
        return tuple(new)

    found = lax.fori_loop(0, COLUMN, scan_recv, (zero,) * NX, unroll=4)
    for s in range(NX):
        plan[2 * NX, NX + s] = found[s]

    chats = NX * NC * COLUMN
    tenants = o_row.shape[1]
    o_col = jnp.sum(
        jnp.where(iota((tenants, tenants), 0) == iota((tenants, tenants), 1), o_row[...] >> 1, 0),
        axis=1,
        keepdims=True,
    )
    by_row = jnp.sum(
        jnp.where(t_row[...] == iota((tenants, chats), 0), o_col, 0), axis=0, keepdims=True
    )

    def key(chip, chat):
        place = chat >> 2
        return (((place >> 4) * 2 + (place & 1)) << 5) + chip

    row = key(by_row, iota((1, chats), 1))
    square = (chats, chats)
    col = jnp.sum(
        jnp.where(iota(square, 0) == iota(square, 1), row, 0), axis=1, keepdims=True
    )
    fullest = jnp.max(jnp.sum(jnp.where(col == row, 1.0, 0.0), axis=1, keepdims=True))
    rounds[0] = (fullest.astype(jnp.int32) + ROOM - 1) >> 3


def root_part(q_ref, blocks, values, out):
    for g in range(KV):
        for n, (_, v) in enumerate(blocks):
            rows = slice(n * 512, (n + 1) * 512)
            values[g, rows, :HD] = v[:, g * HD : (g + 1) * HD]
            values[g, rows, HD:] = jnp.ones((512, HD), BF16)
    diagonal = head_diagonal()
    rows = COLUMN // 2
    for h in range(2):
        chats = slice(h * rows, (h + 1) * rows)
        line = None
        for g in range(KV):
            heads = slice(g * GROUP, (g + 1) * GROUP)
            lanes = slice(g * HD, (g + 1) * HD)
            query = q_ref[chats, heads, :].reshape(rows * GROUP, HD)
            scores = [scores_of(query, k[:, lanes]) for k, _ in blocks]
            peak = functools.reduce(
                jnp.maximum, [jnp.max(s, axis=1, keepdims=True) for s in scores]
            )
            numer = None
            for n, s in enumerate(scores):
                weights = jnp.exp2((s - peak) * SCALE2).astype(BF16)
                part = dot(weights, values[g, n * 512 : (n + 1) * 512, :])
                numer = part if numer is None else numer + part
            total = numer[:, HD:]
            share = (numer[:, :HD] / total).astype(BF16)
            out[chats, heads, :] = share.reshape(rows, GROUP, HD)
            level = (peak * SCALE2 + jnp.log2(total)).reshape(rows, GROUP, HD)
            part = jnp.sum(jnp.where(diagonal[None, heads], level, 0.0), axis=1)
            line = part if line is None else line + part
        out[chats, HEADS:, :] = level_parts(line)


def home_part(length_ref, q_ref, wk, wv, sk, sv, nk, nv, share_ref, level_ref):
    diagonal = head_diagonal()
    first = lax.axis_index("z") * HOME
    pad = jnp.zeros((3, KV * HD), F32)
    few_k, few_v = (
        [
            jnp.concatenate([s[j].astype(F32), n[j : j + 1].astype(F32), pad]).astype(BF16)
            for j in range(HOME)
        ]
        for s, n in ((sk, nk), (sv, nv))
    )
    pairs = [(g, j) for g in range(KV) for j in range(HOME)]
    recent, few = [], []
    for g, j in pairs:
        lanes = slice(g * HD, (g + 1) * HD)
        query = q_ref[first + j, g * GROUP : (g + 1) * GROUP, :]
        used = iota((GROUP, 512), 1) < length_ref[j]
        recent.append(jnp.where(used, scores_of(query, wk[j, :, lanes]), FLOOR))
        few.append(scores_of(query, few_k[j][:, lanes]))
    recent = jnp.concatenate(recent, axis=0)
    few = jnp.concatenate(few, axis=0)
    few = jnp.where(iota(few.shape, 1) < 5, few, FLOOR)
    peak = jnp.maximum(jnp.max(recent, axis=1, keepdims=True), jnp.max(few, axis=1, keepdims=True))
    recent = jnp.exp2((recent - peak) * SCALE2)
    few = jnp.exp2((few - peak) * SCALE2)
    total = jnp.sum(recent, axis=1, keepdims=True) + jnp.sum(few, axis=1, keepdims=True)
    recent, few = recent.astype(BF16), few.astype(BF16)
    level = jnp.broadcast_to(peak * SCALE2 + jnp.log2(total), (KV * HOME * GROUP, HD))
    level = level.reshape(KV, HOME, GROUP, HD)
    line = None
    for g in range(KV):
        part = jnp.where(diagonal[None, g * GROUP : (g + 1) * GROUP], level[g], 0.0)
        part = jnp.sum(part, axis=1)
        line = part if line is None else line + part
    level_ref[...] = line
    for n, (g, j) in enumerate(pairs):
        lanes = slice(g * HD, (g + 1) * HD)
        rows = slice(n * GROUP, (n + 1) * GROUP)
        numer = dot(recent[rows], wv[j, :, lanes]) + dot(few[rows], few_v[j][:, lanes])
        share_ref[j, g * GROUP : (g + 1) * GROUP, :] = numer / total[rows]


def near_kernel(
    length_ref, q_ref, k, v, wk, wv, sk, sv, nk, nv, out, share, level, values, wks, wvs, sems
):
    copies = [
        pltpu.make_async_copy(wk, wks, sems.at[0]),
        pltpu.make_async_copy(wv, wvs, sems.at[1]),
    ]
    for copy in copies:
        copy.start()
    root_part(q_ref, [(k, v)], values, out)
    for copy in copies:
        copy.wait()
    home_part(length_ref, q_ref, wks, wvs, sk, sv, nk, nv, share, level)


def far_kernel(q_ref, *refs):
    out, values = refs[-2:]
    blocks = refs[:-2]
    root_part(q_ref, list(zip(blocks[::2], blocks[1::2])), values, out)


def select_kernel(plan, turn, q_ref, out):
    start = turn if isinstance(turn, int) else turn[0] * ROOM
    chats = [plan[t, start + e] for t in range(NX) for e in range(ROOM)]
    for n, chat in enumerate(chats):
        out[n] = q_ref[chat]


def prefix_kernel(plan, turn, q_ref, pk0, pk1, pv0, pv1, out, qs, lists):
    start = turn if isinstance(turn, int) else turn[0] * ROOM
    diagonal = head_diagonal()
    zero = jnp.int32(0)
    lists[0, 0] = zero
    lists[1, 0] = zero
    n0, n1 = zero, zero
    for s in range(NX):

        def scan(e, found, s=s):
            slot = plan[NX + s, start + e]
            lists[0, found[0]] = s * ROOM + e
            lists[1, found[1]] = s * ROOM + e
            return found[0] + 1 - slot, found[1] + slot

        left = jnp.clip(plan[2 * NX, NX + s] - start, 0, ROOM)
        n0, n1 = lax.fori_loop(0, left, scan, (n0, n1))
    slots = ((pk0, pv0, n0), (pk1, pv1, n1))

    def step(b, _):
        results = []
        for i, (pk, pv, count) in enumerate(slots):
            last = jnp.maximum(count - 1, 0)
            chats = [lists[i, jnp.minimum(b * MEMBER + j, last)] for j in range(MEMBER)]
            line = None
            shares = []
            for g in range(KV):
                heads = slice(g * GROUP, (g + 1) * GROUP)
                lanes = slice(g * HD, (g + 1) * HD)
                for j, chat in enumerate(chats):
                    qs[i, g, j] = q_ref[chat, heads, :]
                scores = scores_of(qs[i, g].reshape(MEMBER * GROUP, HD), pk[:, lanes])
                peak = jnp.max(scores, axis=1, keepdims=True)
                weights = jnp.exp2((scores - peak) * SCALE2)
                total = jnp.sum(weights, axis=1, keepdims=True)
                numer = dot(weights.astype(BF16), pv[:, lanes])
                shares.append((numer / total).astype(BF16))
                level = jnp.broadcast_to(peak * SCALE2 + jnp.log2(total), (MEMBER * GROUP, HD))
                level = level.reshape(MEMBER, GROUP, HD)
                part = jnp.sum(jnp.where(diagonal[None, heads], level, 0.0), axis=1)
                line = part if line is None else line + part
            results.append((chats, shares, level_parts(line)))
        for (chats, shares, parts), (_, _, count) in zip(results, slots):

            @pl.when(b * MEMBER < count)
            def _(chats=chats, shares=shares, parts=parts):
                for j, chat in enumerate(chats):
                    for g in range(KV):
                        rows = slice(j * GROUP, (j + 1) * GROUP)
                        out[chat, g * GROUP : (g + 1) * GROUP, :] = shares[g][rows]
                    out[chat, HEADS:, :] = parts[j]

        return 0

    lax.fori_loop(0, (jnp.maximum(n0, n1) + MEMBER - 1) >> 3, step, 0)


def place_answers(plan, start, back, out):
    for t in range(NX):

        def place(e, _, t=t):
            out[plan[t, start + e]] = back[t * ROOM + e]
            return 0

        lax.fori_loop(0, jnp.clip(plan[2 * NX, t] - start, 0, ROOM), place, 0)


def scatter_kernel(plan, turn, back, before, out):
    out[...] = before[...]
    place_answers(plan, turn[0] * ROOM, back, out)


def weights_of(levels):
    top = functools.reduce(jnp.maximum, levels)
    weights = [jnp.exp2(v - top) for v in levels]
    total = functools.reduce(jnp.add, weights)
    return [w / total for w in weights], top + jnp.log2(total)


def read_level(ref):
    return jnp.sum(ref[:, HEADS:, :].astype(F32), axis=1)


def four_lines(weights):
    quarter = iota((1, HD), 1) // HEADS
    return functools.reduce(
        jnp.add, [jnp.where(quarter == i, w, 0.0) for i, w in enumerate(weights)]
    )


def mix(diagonal, line, shares):
    spread = jnp.where(diagonal, line, 0.0)
    high = spread.astype(BF16)
    low = (spread - high.astype(F32)).astype(BF16)
    return dot(high, shares) + dot(low, shares)


def merge_row_kernel(plan, near, far, back, before, share_ref, level_ref, out, prefix, lines, levels):
    diagonal = head_diagonal()
    prefix[...] = before[...]
    place_answers(plan, 0, back, prefix)
    level = [read_level(r) for r in (near, far, prefix)]
    weights, total = weights_of(level)
    line = four_lines(weights)
    for n, v in enumerate(level):
        levels[n] = v
    out[:, HEADS:, :] = level_parts(total)
    empty = jnp.zeros((HEADS, HD), BF16)

    def parts(i, fourth):
        sources = [near[i, :HEADS, :], far[i, :HEADS, :], prefix[i, :HEADS, :], fourth]
        return jnp.concatenate(sources, axis=0)

    for i in range(COLUMN):
        out[i, :HEADS, :] = mix(diagonal, line[i : i + 1], parts(i, empty)).astype(BF16)

    first = lax.axis_index("z") * HOME
    own = pl.ds(first, HOME)
    weights, total = weights_of([levels[n, own, :] for n in range(3)] + [level_ref[...]])
    line = four_lines(weights)
    rest = four_lines(weights[3:])
    out[own, HEADS:, :] = level_parts(total)
    nothing = jnp.zeros((3 * HEADS, HD), BF16)
    for j in range(HOME):
        home = share_ref[j]
        high = home.astype(BF16)
        low = jnp.concatenate([(home - high.astype(F32)).astype(BF16), nothing], axis=0)
        total = mix(diagonal, line[j : j + 1], parts(first + j, high))
        total = total + mix(diagonal, rest[j : j + 1], low)
        out[first + j, :HEADS, :] = total.astype(BF16)


def merge_kernel(in_ref, out):
    diagonal = head_diagonal()
    for y in range(NY):
        level = jnp.sum(in_ref[:, y, HEADS:, :].astype(F32), axis=1)
        weights = jnp.exp2(level - jnp.max(level, axis=0, keepdims=True))
        weights = weights / jnp.sum(weights, axis=0, keepdims=True)
        total = jnp.zeros((HEADS, HD), F32)
        for k in range(0, NZ, 4):
            line = four_lines([weights[k + i : k + i + 1] for i in range(4)])
            shares = in_ref[k : k + 4, y, :HEADS, :].reshape(4 * HEADS, HD)
            total = total + mix(diagonal, line, shares)
        out[y] = total.astype(BF16)


def kernel(
    body, name, outs, args, scalars=0, scratch=(), limit=8, us=0.5, in_specs=None, out_specs=None
):
    return pl.pallas_call(
        body,
        out_shape=outs,
        in_specs=in_specs or [SMEM] * scalars + [VMEM] * (len(args) - scalars),
        out_specs=out_specs if out_specs is not None else jax.tree.map(lambda _: VMEM, outs),
        scratch_shapes=list(scratch),
        compiler_params=pltpu.CompilerParams(vmem_limit_bytes=limit * MIB),
        cost_estimate=pl.CostEstimate(
            flops=int(us * 8e8), bytes_accessed=int(us * 1e6), transcendentals=0
        ),
        name=name,
    )(*args)


def send(array, axis, shift):
    size = {"x": NX, "z": NZ, "c": NC, "y": NY}[axis]
    return lax.ppermute(array, axis, [(i, (i + shift) % size) for i in range(size)])


def shaped(*shape, dtype=BF16):
    return jax.ShapeDtypeStruct(shape, dtype)


def local(
    queries,
    new_keys,
    new_values,
    sink_keys,
    sink_values,
    window_keys,
    window_values,
    window_len,
    root_keys,
    root_values,
    prefix_keys,
    prefix_values,
    tenant_of,
    owner,
):
    spread = jnp.broadcast_to(queries.reshape(1, NY, HEADS, HD), (NZ, NY, HEADS, HD))
    q = lax.all_to_all(
        spread.reshape(COLUMN, HEADS, HD), ("z", "y"), split_axis=0, concat_axis=0, tiled=True
    )

    k_left, v_left = send(root_keys, "x", 1), send(root_values, "x", 1)
    k_right, v_right = send(root_keys, "x", -1), send(root_values, "x", -1)
    i32 = jnp.int32
    tenant_of, _ = lax.optimization_barrier((tenant_of, spread))
    plan, rounds = kernel(
        prepare_kernel,
        "prepare",
        [shaped(2 * NX + 1, COLUMN + 1, dtype=i32), shaped(1, dtype=i32)],
        [tenant_of, owner, tenant_of.reshape(1, -1), owner.reshape(1, -1)],
        scalars=2,
        out_specs=[SMEM] * 2,
        us=2,
    )
    anywhere = pl.BlockSpec(memory_space=pl.ANY)
    near, home_share, home_level = kernel(
        near_kernel,
        "near",
        [
            shaped(COLUMN, ROWS, HD),
            shaped(HOME, HEADS, HD, dtype=F32),
            shaped(HOME, HD, dtype=F32),
        ],
        [
            window_len,
            q,
            root_keys,
            root_values,
            window_keys,
            window_values,
            sink_keys,
            sink_values,
            new_keys,
            new_values,
        ],
        in_specs=[SMEM] + [VMEM] * 3 + [anywhere] * 2 + [VMEM] * 4,
        scratch=[
            pltpu.VMEM((KV, 512, 2 * HD), BF16),
            pltpu.VMEM(window_keys.shape, BF16),
            pltpu.VMEM(window_values.shape, BF16),
            pltpu.SemaphoreType.DMA((2,)),
        ],
        limit=14,
        us=4,
    )

    def scalar_kernel(body, name, outs, turn, args, **options):
        if isinstance(turn, int):
            return kernel(
                lambda plan, *refs: body(plan, turn, *refs),
                name,
                outs,
                [plan, *args],
                scalars=1,
                **options,
            )
        return kernel(body, name, outs, [plan, turn, *args], scalars=2, **options)

    def prefix_picked(turn):
        return scalar_kernel(select_kernel, "select", shaped(NX * ROOM, HEADS, HD), turn, [q])

    picked = prefix_picked(0)
    tied = (prefix_keys, prefix_values, k_left, v_left, k_right, v_right, plan)
    pk, pv, k_left, v_left, k_right, v_right, plan = lax.optimization_barrier(tied)
    k_far, v_far = send(k_left, "x", 1), send(v_right, "x", -1)
    pk1, pv1 = send(pk, "c", 1), send(pv, "c", 1)
    rk, rv, _ = lax.optimization_barrier((root_keys, root_values, picked))
    others = [(send(rk, "c", 1), send(rv, "c", 1))]
    for k, v in ((k_left, v_left), (k_right, v_right), (k_far, v_far)):
        others += [(k, v), (send(k, "c", 1), send(v, "c", 1))]

    def prefix_answers(turn, picked):
        asked = lax.all_to_all(picked, "x", split_axis=0, concat_axis=0, tiled=True)
        answer = scalar_kernel(
            prefix_kernel,
            "prefix",
            shaped(NX * ROOM, ROWS, HD),
            turn,
            [asked, prefix_keys, pk1, prefix_values, pv1],
            scratch=[
                pltpu.VMEM((2, KV, MEMBER, GROUP, HD), BF16),
                pltpu.SMEM((2, NX * ROOM + 1), i32),
            ],
            us=2,
        )
        return lax.all_to_all(answer, "x", split_axis=0, concat_axis=0, tiled=True)

    def more(state):
        turn, before = state
        after = scalar_kernel(
            scatter_kernel,
            "scatter",
            shaped(COLUMN, ROWS, HD),
            turn,
            [prefix_answers(turn, prefix_picked(turn)), before],
        )
        return turn + 1, after

    row = lax.broadcasted_iota(i32, (COLUMN, ROWS, HD), 1)
    none = jnp.where(row == HEADS, FLOOR, 0.0).astype(BF16)
    answers = prefix_answers(0, picked)
    _, later = lax.while_loop(
        lambda state: state[0][0] < rounds[0], more, (jnp.ones((1,), i32), none)
    )
    far = kernel(
        far_kernel,
        "far",
        shaped(COLUMN, ROWS, HD),
        [q, *(ref for block in others for ref in block)],
        scratch=[pltpu.VMEM((KV, (2 * NX - 1) * 512, 2 * HD), BF16)],
        limit=28,
        us=6,
    )
    merged = kernel(
        merge_row_kernel,
        "merge_row",
        shaped(COLUMN, ROWS, HD),
        [plan, near, far, answers, later, home_share, home_level],
        scalars=1,
        scratch=[
            pltpu.VMEM((COLUMN, ROWS, HD), BF16),
            pltpu.VMEM((COLUMN, HD), F32),
            pltpu.VMEM((3, COLUMN, HD), F32),
        ],
        us=1.5,
    )
    back = lax.all_to_all(merged, ("z", "y"), split_axis=0, concat_axis=0, tiled=True)
    out = kernel(
        merge_kernel, "merge", shaped(NY, HEADS, HD), [back.reshape(NZ, NY, ROWS, HD)]
    )
    return out.reshape(1, NY * HEADS * HD)


def solution(mesh):
    fine = Mesh(mesh.devices.reshape(NX, NZ, NC, NY), ("x", "z", "c", "y"))
    session = ("x", "z", "c")
    placed = (
        P(("x", "z", "c", "y"), None),
        P(session, "y"),
        P(session, "y"),
        P(session, None, "y"),
        P(session, None, "y"),
        P(session, None, "y"),
        P(session, None, "y"),
        P(session),
        P(session, "y"),
        P(session, "y"),
        P(session, "y"),
        P(session, "y"),
        P(),
        P(),
    )
    return jax.shard_map(
        local,
        mesh=fine,
        in_specs=placed,
        out_specs=P(("x", "z", "c", "y"), None),
        check_vma=False,
    )
```

```python
import functools
import math

import jax
import jax.numpy as jnp
from jax import lax
from jax.experimental import pallas as pl
from jax.experimental.pallas import tpu as pltpu
from jax.sharding import Mesh, PartitionSpec as P

HD = 128
GROUP = 16
KV = 2
HEADS = KV * GROUP
HOME = 4
NX, NZ, NC, NY = 4, 8, 2, 4
ROWS = 40
SCALE2 = HD**-0.5 * math.log2(math.e)
FLOOR = -1e30
COLUMN = NZ * HOME
MEMBER = 8
ROOM = 8
MIB = 2**20

NT = (((1,), (1,)), ((), ()))
VMEM = pl.BlockSpec(memory_space=pltpu.VMEM)
SMEM = pl.BlockSpec(memory_space=pltpu.SMEM)
BF16 = jnp.bfloat16
F32 = jnp.float32


def scores_of(query, keys):
    return lax.dot_general(query, keys, NT, preferred_element_type=F32)


def dot(a, b):
    return jnp.dot(a, b, preferred_element_type=F32)


def iota(shape, dim):
    return lax.broadcasted_iota(jnp.int32, shape, dim)


def head_diagonal():
    return (iota((HEADS, HD), 1) % HEADS) == iota((HEADS, HD), 0)


def level_parts(level):
    first = level.astype(BF16).astype(F32)
    second = (level - first).astype(BF16).astype(F32)
    third = level - first - second
    row = iota((1, 8, HD), 1)
    parts = jnp.where(row == 2, third[:, None], 0.0)
    parts = jnp.where(row == 1, second[:, None], parts)
    return jnp.where(row == 0, first[:, None], parts).astype(BF16)


def prepare_kernel(tenant_ref, owner_ref, t_row, o_row, plan, rounds):
    x, z, c = lax.axis_index("x"), lax.axis_index("z"), lax.axis_index("c")
    zero = jnp.int32(0)

    def clear(i, _):
        for t in range(NX):
            plan[t, i] = zero
        return 0

    lax.fori_loop(0, COLUMN + 1, clear, 0, unroll=11)

    def slot_of(s, i):
        return owner_ref[tenant_ref[((s * NZ + (i >> 2)) * 2 + c) * HOME + (i & 3)]]

    def scan_send(i, found):
        slot = slot_of(x, i)
        target = jnp.where(((slot >> 1) & (NZ - 1)) == z, slot >> 4, NX)
        new = []
        for t in range(NX):
            plan[t, found[t]] = i
            new.append(found[t] + (target == t).astype(jnp.int32))
        return tuple(new)

    found = lax.fori_loop(0, COLUMN, scan_send, (zero,) * NX, unroll=8)
    for t in range(NX):
        plan[2 * NX, t] = found[t]

    mine = x * NZ + z

    def scan_recv(i, found):
        new = []
        for s in range(NX):
            slot = slot_of(s, i)
            plan[NX + s, found[s]] = (slot & 1) ^ c
            new.append(found[s] + ((slot >> 1) == mine).astype(jnp.int32))
        return tuple(new)

    found = lax.fori_loop(0, COLUMN, scan_recv, (zero,) * NX, unroll=4)
    for s in range(NX):
        plan[2 * NX, NX + s] = found[s]

    chats = NX * NC * COLUMN
    tenants = o_row.shape[1]
    o_col = jnp.sum(
        jnp.where(iota((tenants, tenants), 0) == iota((tenants, tenants), 1), o_row[...] >> 1, 0),
        axis=1,
        keepdims=True,
    )
    by_row = jnp.sum(
        jnp.where(t_row[...] == iota((tenants, chats), 0), o_col, 0), axis=0, keepdims=True
    )

    def key(chip, chat):
        place = chat >> 2
        return (((place >> 4) * 2 + (place & 1)) << 5) + chip

    row = key(by_row, iota((1, chats), 1))
    square = (chats, chats)
    col = jnp.sum(
        jnp.where(iota(square, 0) == iota(square, 1), row, 0), axis=1, keepdims=True
    )
    fullest = jnp.max(jnp.sum(jnp.where(col == row, 1.0, 0.0), axis=1, keepdims=True))
    rounds[0] = (fullest.astype(jnp.int32) + ROOM - 1) >> 3


def root_part(q_ref, blocks, values, out):
    for g in range(KV):
        for n, (_, v) in enumerate(blocks):
            rows = slice(n * 512, (n + 1) * 512)
            values[g, rows, :HD] = v[:, g * HD : (g + 1) * HD]
            values[g, rows, HD:] = jnp.ones((512, HD), BF16)
    diagonal = head_diagonal()
    rows = COLUMN // 2
    for h in range(2):
        chats = slice(h * rows, (h + 1) * rows)
        line = None
        for g in range(KV):
            heads = slice(g * GROUP, (g + 1) * GROUP)
            lanes = slice(g * HD, (g + 1) * HD)
            query = q_ref[chats, heads, :].reshape(rows * GROUP, HD)
            scores = [scores_of(query, k[:, lanes]) for k, _ in blocks]
            peak = functools.reduce(
                jnp.maximum, [jnp.max(s, axis=1, keepdims=True) for s in scores]
            )
            numer = None
            for n, s in enumerate(scores):
                weights = jnp.exp2(((s - peak) * SCALE2).astype(BF16))
                part = dot(weights, values[g, n * 512 : (n + 1) * 512, :])
                numer = part if numer is None else numer + part
            total = numer[:, HD:]
            share = (numer[:, :HD] / total).astype(BF16)
            out[chats, heads, :] = share.reshape(rows, GROUP, HD)
            level = (peak * SCALE2 + jnp.log2(total)).reshape(rows, GROUP, HD)
            part = jnp.sum(jnp.where(diagonal[None, heads], level, 0.0), axis=1)
            line = part if line is None else line + part
        out[chats, HEADS:, :] = level_parts(line)


def home_part(length_ref, q_ref, wk, wv, sk, sv, nk, nv, share_ref, level_ref):
    diagonal = head_diagonal()
    first = lax.axis_index("z") * HOME
    pad = jnp.zeros((3, KV * HD), F32)
    few_k, few_v = (
        [
            jnp.concatenate([s[j].astype(F32), n[j : j + 1].astype(F32), pad]).astype(BF16)
            for j in range(HOME)
        ]
        for s, n in ((sk, nk), (sv, nv))
    )
    pairs = [(g, j) for g in range(KV) for j in range(HOME)]
    recent, few = [], []
    for g, j in pairs:
        lanes = slice(g * HD, (g + 1) * HD)
        query = q_ref[first + j, g * GROUP : (g + 1) * GROUP, :]
        used = iota((GROUP, 512), 1) < length_ref[j]
        recent.append(jnp.where(used, scores_of(query, wk[j, :, lanes]), FLOOR))
        few.append(scores_of(query, few_k[j][:, lanes]))
    recent = jnp.concatenate(recent, axis=0)
    few = jnp.concatenate(few, axis=0)
    few = jnp.where(iota(few.shape, 1) < 5, few, FLOOR)
    peak = jnp.maximum(jnp.max(recent, axis=1, keepdims=True), jnp.max(few, axis=1, keepdims=True))
    recent = jnp.exp2((recent - peak) * SCALE2)
    few = jnp.exp2((few - peak) * SCALE2)
    total = jnp.sum(recent, axis=1, keepdims=True) + jnp.sum(few, axis=1, keepdims=True)
    recent, few = recent.astype(BF16), few.astype(BF16)
    level = jnp.broadcast_to(peak * SCALE2 + jnp.log2(total), (KV * HOME * GROUP, HD))
    level = level.reshape(KV, HOME, GROUP, HD)
    line = None
    for g in range(KV):
        part = jnp.where(diagonal[None, g * GROUP : (g + 1) * GROUP], level[g], 0.0)
        part = jnp.sum(part, axis=1)
        line = part if line is None else line + part
    level_ref[...] = line
    for n, (g, j) in enumerate(pairs):
        lanes = slice(g * HD, (g + 1) * HD)
        rows = slice(n * GROUP, (n + 1) * GROUP)
        numer = dot(recent[rows], wv[j, :, lanes]) + dot(few[rows], few_v[j][:, lanes])
        share_ref[j, g * GROUP : (g + 1) * GROUP, :] = numer / total[rows]


def near_kernel(
    length_ref, q_ref, k, v, wk, wv, sk, sv, nk, nv, out, share, level, values, wks, wvs, sems
):
    copies = [
        pltpu.make_async_copy(wk, wks, sems.at[0]),
        pltpu.make_async_copy(wv, wvs, sems.at[1]),
    ]
    for copy in copies:
        copy.start()
    root_part(q_ref, [(k, v)], values, out)
    for copy in copies:
        copy.wait()
    home_part(length_ref, q_ref, wks, wvs, sk, sv, nk, nv, share, level)


def far_kernel(q_ref, *refs):
    out, values = refs[-2:]
    blocks = refs[:-2]
    root_part(q_ref, list(zip(blocks[::2], blocks[1::2])), values, out)


def select_kernel(plan, turn, q_ref, out):
    start = turn if isinstance(turn, int) else turn[0] * ROOM
    chats = [plan[t, start + e] for t in range(NX) for e in range(ROOM)]
    for n, chat in enumerate(chats):
        out[n] = q_ref[chat]


def prefix_kernel(plan, turn, q_ref, pk0, pk1, pv0, pv1, out, qs, lists):
    start = turn if isinstance(turn, int) else turn[0] * ROOM
    diagonal = head_diagonal()
    zero = jnp.int32(0)
    lists[0, 0] = zero
    lists[1, 0] = zero
    n0, n1 = zero, zero
    for s in range(NX):

        def scan(e, found, s=s):
            slot = plan[NX + s, start + e]
            lists[0, found[0]] = s * ROOM + e
            lists[1, found[1]] = s * ROOM + e
            return found[0] + 1 - slot, found[1] + slot

        left = jnp.clip(plan[2 * NX, NX + s] - start, 0, ROOM)
        n0, n1 = lax.fori_loop(0, left, scan, (n0, n1))
    slots = ((pk0, pv0, n0), (pk1, pv1, n1))

    def step(b, _):
        results = []
        for i, (pk, pv, count) in enumerate(slots):
            last = jnp.maximum(count - 1, 0)
            chats = [lists[i, jnp.minimum(b * MEMBER + j, last)] for j in range(MEMBER)]
            line = None
            shares = []
            for g in range(KV):
                heads = slice(g * GROUP, (g + 1) * GROUP)
                lanes = slice(g * HD, (g + 1) * HD)
                for j, chat in enumerate(chats):
                    qs[i, g, j] = q_ref[chat, heads, :]
                scores = scores_of(qs[i, g].reshape(MEMBER * GROUP, HD), pk[:, lanes])
                peak = jnp.max(scores, axis=1, keepdims=True)
                weights = jnp.exp2((scores - peak) * SCALE2)
                total = jnp.sum(weights, axis=1, keepdims=True)
                numer = dot(weights.astype(BF16), pv[:, lanes])
                shares.append((numer / total).astype(BF16))
                level = jnp.broadcast_to(peak * SCALE2 + jnp.log2(total), (MEMBER * GROUP, HD))
                level = level.reshape(MEMBER, GROUP, HD)
                part = jnp.sum(jnp.where(diagonal[None, heads], level, 0.0), axis=1)
                line = part if line is None else line + part
            results.append((chats, shares, level_parts(line)))
        for (chats, shares, parts), (_, _, count) in zip(results, slots):

            @pl.when(b * MEMBER < count)
            def _(chats=chats, shares=shares, parts=parts):
                for j, chat in enumerate(chats):
                    for g in range(KV):
                        rows = slice(j * GROUP, (j + 1) * GROUP)
                        out[chat, g * GROUP : (g + 1) * GROUP, :] = shares[g][rows]
                    out[chat, HEADS:, :] = parts[j]

        return 0

    lax.fori_loop(0, (jnp.maximum(n0, n1) + MEMBER - 1) >> 3, step, 0)


def place_answers(plan, start, back, out):
    for t in range(NX):

        def place(e, _, t=t):
            out[plan[t, start + e]] = back[t * ROOM + e]
            return 0

        lax.fori_loop(0, jnp.clip(plan[2 * NX, t] - start, 0, ROOM), place, 0)


def scatter_kernel(plan, turn, back, before, out):
    out[...] = before[...]
    place_answers(plan, turn[0] * ROOM, back, out)


def weights_of(levels):
    top = functools.reduce(jnp.maximum, levels)
    weights = [jnp.exp2(v - top) for v in levels]
    total = functools.reduce(jnp.add, weights)
    return [w / total for w in weights], top + jnp.log2(total)


def read_level(ref):
    return jnp.sum(ref[:, HEADS:, :].astype(F32), axis=1)


def four_lines(weights):
    quarter = iota((1, HD), 1) // HEADS
    return functools.reduce(
        jnp.add, [jnp.where(quarter == i, w, 0.0) for i, w in enumerate(weights)]
    )


def mix(diagonal, line, shares):
    spread = jnp.where(diagonal, line, 0.0)
    high = spread.astype(BF16)
    low = (spread - high.astype(F32)).astype(BF16)
    return dot(high, shares) + dot(low, shares)


def merge_row_kernel(plan, near, far, back, before, share_ref, level_ref, out, prefix, lines, levels):
    diagonal = head_diagonal()
    prefix[...] = before[...]
    place_answers(plan, 0, back, prefix)
    level = [read_level(r) for r in (near, far, prefix)]
    weights, total = weights_of(level)
    line = four_lines(weights)
    for n, v in enumerate(level):
        levels[n] = v
    out[:, HEADS:, :] = level_parts(total)
    empty = jnp.zeros((HEADS, HD), BF16)

    def parts(i, fourth):
        sources = [near[i, :HEADS, :], far[i, :HEADS, :], prefix[i, :HEADS, :], fourth]
        return jnp.concatenate(sources, axis=0)

    for i in range(COLUMN):
        out[i, :HEADS, :] = mix(diagonal, line[i : i + 1], parts(i, empty)).astype(BF16)

    first = lax.axis_index("z") * HOME
    own = pl.ds(first, HOME)
    weights, total = weights_of([levels[n, own, :] for n in range(3)] + [level_ref[...]])
    line = four_lines(weights)
    rest = four_lines(weights[3:])
    out[own, HEADS:, :] = level_parts(total)
    nothing = jnp.zeros((3 * HEADS, HD), BF16)
    for j in range(HOME):
        home = share_ref[j]
        high = home.astype(BF16)
        low = jnp.concatenate([(home - high.astype(F32)).astype(BF16), nothing], axis=0)
        total = mix(diagonal, line[j : j + 1], parts(first + j, high))
        total = total + mix(diagonal, rest[j : j + 1], low)
        out[first + j, :HEADS, :] = total.astype(BF16)


def merge_kernel(in_ref, out):
    diagonal = head_diagonal()
    for y in range(NY):
        level = jnp.sum(in_ref[:, y, HEADS:, :].astype(F32), axis=1)
        weights = jnp.exp2(level - jnp.max(level, axis=0, keepdims=True))
        weights = weights / jnp.sum(weights, axis=0, keepdims=True)
        total = jnp.zeros((HEADS, HD), F32)
        for k in range(0, NZ, 4):
            line = four_lines([weights[k + i : k + i + 1] for i in range(4)])
            shares = in_ref[k : k + 4, y, :HEADS, :].reshape(4 * HEADS, HD)
            total = total + mix(diagonal, line, shares)
        out[y] = total.astype(BF16)


def kernel(
    body, name, outs, args, scalars=0, scratch=(), limit=8, us=0.5, in_specs=None, out_specs=None
):
    return pl.pallas_call(
        body,
        out_shape=outs,
        in_specs=in_specs or [SMEM] * scalars + [VMEM] * (len(args) - scalars),
        out_specs=out_specs if out_specs is not None else jax.tree.map(lambda _: VMEM, outs),
        scratch_shapes=list(scratch),
        compiler_params=pltpu.CompilerParams(vmem_limit_bytes=limit * MIB),
        cost_estimate=pl.CostEstimate(
            flops=int(us * 8e8), bytes_accessed=int(us * 1e6), transcendentals=0
        ),
        name=name,
    )(*args)


def send(array, axis, shift):
    size = {"x": NX, "z": NZ, "c": NC, "y": NY}[axis]
    return lax.ppermute(array, axis, [(i, (i + shift) % size) for i in range(size)])


def shaped(*shape, dtype=BF16):
    return jax.ShapeDtypeStruct(shape, dtype)


def local(
    queries,
    new_keys,
    new_values,
    sink_keys,
    sink_values,
    window_keys,
    window_values,
    window_len,
    root_keys,
    root_values,
    prefix_keys,
    prefix_values,
    tenant_of,
    owner,
):
    spread = jnp.broadcast_to(queries.reshape(1, NY, HEADS, HD), (NZ, NY, HEADS, HD))
    q = lax.all_to_all(
        spread.reshape(COLUMN, HEADS, HD), ("z", "y"), split_axis=0, concat_axis=0, tiled=True
    )

    k_left, v_left = send(root_keys, "x", 1), send(root_values, "x", 1)
    k_right, v_right = send(root_keys, "x", -1), send(root_values, "x", -1)
    i32 = jnp.int32
    tenant_of, _ = lax.optimization_barrier((tenant_of, spread))
    plan, rounds = kernel(
        prepare_kernel,
        "prepare",
        [shaped(2 * NX + 1, COLUMN + 1, dtype=i32), shaped(1, dtype=i32)],
        [tenant_of, owner, tenant_of.reshape(1, -1), owner.reshape(1, -1)],
        scalars=2,
        out_specs=[SMEM] * 2,
        us=2,
    )
    anywhere = pl.BlockSpec(memory_space=pl.ANY)
    near, home_share, home_level = kernel(
        near_kernel,
        "near",
        [
            shaped(COLUMN, ROWS, HD),
            shaped(HOME, HEADS, HD, dtype=F32),
            shaped(HOME, HD, dtype=F32),
        ],
        [
            window_len,
            q,
            root_keys,
            root_values,
            window_keys,
            window_values,
            sink_keys,
            sink_values,
            new_keys,
            new_values,
        ],
        in_specs=[SMEM] + [VMEM] * 3 + [anywhere] * 2 + [VMEM] * 4,
        scratch=[
            pltpu.VMEM((KV, 512, 2 * HD), BF16),
            pltpu.VMEM(window_keys.shape, BF16),
            pltpu.VMEM(window_values.shape, BF16),
            pltpu.SemaphoreType.DMA((2,)),
        ],
        limit=14,
        us=4,
    )

    def scalar_kernel(body, name, outs, turn, args, **options):
        if isinstance(turn, int):
            return kernel(
                lambda plan, *refs: body(plan, turn, *refs),
                name,
                outs,
                [plan, *args],
                scalars=1,
                **options,
            )
        return kernel(body, name, outs, [plan, turn, *args], scalars=2, **options)

    def prefix_picked(turn):
        return scalar_kernel(select_kernel, "select", shaped(NX * ROOM, HEADS, HD), turn, [q])

    picked = prefix_picked(0)
    tied = (prefix_keys, prefix_values, k_left, v_left, k_right, v_right, plan)
    pk, pv, k_left, v_left, k_right, v_right, plan = lax.optimization_barrier(tied)
    k_far, v_far = send(k_left, "x", 1), send(v_right, "x", -1)
    pk1, pv1 = send(pk, "c", 1), send(pv, "c", 1)
    rk, rv, _ = lax.optimization_barrier((root_keys, root_values, picked))
    others = [(send(rk, "c", 1), send(rv, "c", 1))]
    for k, v in ((k_left, v_left), (k_right, v_right), (k_far, v_far)):
        others += [(k, v), (send(k, "c", 1), send(v, "c", 1))]

    def prefix_answers(turn, picked):
        asked = lax.all_to_all(picked, "x", split_axis=0, concat_axis=0, tiled=True)
        answer = scalar_kernel(
            prefix_kernel,
            "prefix",
            shaped(NX * ROOM, ROWS, HD),
            turn,
            [asked, prefix_keys, pk1, prefix_values, pv1],
            scratch=[
                pltpu.VMEM((2, KV, MEMBER, GROUP, HD), BF16),
                pltpu.SMEM((2, NX * ROOM + 1), i32),
            ],
            us=2,
        )
        return lax.all_to_all(answer, "x", split_axis=0, concat_axis=0, tiled=True)

    def more(state):
        turn, before = state
        after = scalar_kernel(
            scatter_kernel,
            "scatter",
            shaped(COLUMN, ROWS, HD),
            turn,
            [prefix_answers(turn, prefix_picked(turn)), before],
        )
        return turn + 1, after

    row = lax.broadcasted_iota(i32, (COLUMN, ROWS, HD), 1)
    none = jnp.where(row == HEADS, FLOOR, 0.0).astype(BF16)
    answers = prefix_answers(0, picked)
    _, later = lax.while_loop(
        lambda state: state[0][0] < rounds[0], more, (jnp.ones((1,), i32), none)
    )
    far = kernel(
        far_kernel,
        "far",
        shaped(COLUMN, ROWS, HD),
        [q, *(ref for block in others for ref in block)],
        scratch=[pltpu.VMEM((KV, (2 * NX - 1) * 512, 2 * HD), BF16)],
        limit=28,
        us=6,
    )
    merged = kernel(
        merge_row_kernel,
        "merge_row",
        shaped(COLUMN, ROWS, HD),
        [plan, near, far, answers, later, home_share, home_level],
        scalars=1,
        scratch=[
            pltpu.VMEM((COLUMN, ROWS, HD), BF16),
            pltpu.VMEM((COLUMN, HD), F32),
            pltpu.VMEM((3, COLUMN, HD), F32),
        ],
        us=1.5,
    )
    back = lax.all_to_all(merged, ("z", "y"), split_axis=0, concat_axis=0, tiled=True)
    out = kernel(
        merge_kernel, "merge", shaped(NY, HEADS, HD), [back.reshape(NZ, NY, ROWS, HD)]
    )
    return out.reshape(1, NY * HEADS * HD)


def solution(mesh):
    fine = Mesh(mesh.devices.reshape(NX, NZ, NC, NY), ("x", "z", "c", "y"))
    session = ("x", "z", "c")
    placed = (
        P(("x", "z", "c", "y"), None),
        P(session, "y"),
        P(session, "y"),
        P(session, None, "y"),
        P(session, None, "y"),
        P(session, None, "y"),
        P(session, None, "y"),
        P(session),
        P(session, "y"),
        P(session, "y"),
        P(session, "y"),
        P(session, "y"),
        P(),
        P(),
    )
    return jax.shard_map(
        local,
        mesh=fine,
        in_specs=placed,
        out_specs=P(("x", "z", "c", "y"), None),
        check_vma=False,
    )
```

```python
import functools
import math

import jax
import jax.numpy as jnp
from jax import lax
from jax.experimental import pallas as pl
from jax.experimental.pallas import tpu as pltpu
from jax.sharding import Mesh, PartitionSpec as P

HD = 128
GROUP = 16
KV = 2
HEADS = KV * GROUP
HOME = 4
NX, NZ, NC, NY = 4, 8, 2, 4
ROWS = 40
SCALE2 = HD**-0.5 * math.log2(math.e)
FLOOR = -1e30
COLUMN = NZ * HOME
MEMBER = 8
ROOM = 8
MIB = 2**20

NT = (((1,), (1,)), ((), ()))
VMEM = pl.BlockSpec(memory_space=pltpu.VMEM)
SMEM = pl.BlockSpec(memory_space=pltpu.SMEM)
BF16 = jnp.bfloat16
F32 = jnp.float32


def scores_of(query, keys):
    return lax.dot_general(query, keys, NT, preferred_element_type=F32)


def dot(a, b):
    return jnp.dot(a, b, preferred_element_type=F32)


def iota(shape, dim):
    return lax.broadcasted_iota(jnp.int32, shape, dim)


def head_diagonal():
    return (iota((HEADS, HD), 1) % HEADS) == iota((HEADS, HD), 0)


def level_parts(level):
    first = level.astype(BF16).astype(F32)
    second = (level - first).astype(BF16).astype(F32)
    third = level - first - second
    row = iota((1, 8, HD), 1)
    parts = jnp.where(row == 2, third[:, None], 0.0)
    parts = jnp.where(row == 1, second[:, None], parts)
    return jnp.where(row == 0, first[:, None], parts).astype(BF16)


def prepare_kernel(tenant_ref, owner_ref, t_row, o_row, plan, rounds):
    x, z, c = lax.axis_index("x"), lax.axis_index("z"), lax.axis_index("c")
    zero = jnp.int32(0)

    def clear(i, _):
        for t in range(NX):
            plan[t, i] = zero
        return 0

    lax.fori_loop(0, COLUMN + 1, clear, 0, unroll=11)

    def slot_of(s, i):
        return owner_ref[tenant_ref[((s * NZ + (i >> 2)) * 2 + c) * HOME + (i & 3)]]

    def scan_send(i, found):
        slot = slot_of(x, i)
        target = jnp.where(((slot >> 1) & (NZ - 1)) == z, slot >> 4, NX)
        new = []
        for t in range(NX):
            plan[t, found[t]] = i
            new.append(found[t] + (target == t).astype(jnp.int32))
        return tuple(new)

    found = lax.fori_loop(0, COLUMN, scan_send, (zero,) * NX, unroll=8)
    for t in range(NX):
        plan[2 * NX, t] = found[t]

    mine = x * NZ + z

    def scan_recv(i, found):
        new = []
        for s in range(NX):
            slot = slot_of(s, i)
            plan[NX + s, found[s]] = (slot & 1) ^ c
            new.append(found[s] + ((slot >> 1) == mine).astype(jnp.int32))
        return tuple(new)

    found = lax.fori_loop(0, COLUMN, scan_recv, (zero,) * NX, unroll=4)
    for s in range(NX):
        plan[2 * NX, NX + s] = found[s]

    chats = NX * NC * COLUMN
    tenants = o_row.shape[1]
    o_col = jnp.sum(
        jnp.where(iota((tenants, tenants), 0) == iota((tenants, tenants), 1), o_row[...] >> 1, 0),
        axis=1,
        keepdims=True,
    )
    by_row = jnp.sum(
        jnp.where(t_row[...] == iota((tenants, chats), 0), o_col, 0), axis=0, keepdims=True
    )

    def key(chip, chat):
        place = chat >> 2
        return (((place >> 4) * 2 + (place & 1)) << 5) + chip

    row = key(by_row, iota((1, chats), 1))
    square = (chats, chats)
    col = jnp.sum(
        jnp.where(iota(square, 0) == iota(square, 1), row, 0), axis=1, keepdims=True
    )
    fullest = jnp.max(jnp.sum(jnp.where(col == row, 1.0, 0.0), axis=1, keepdims=True))
    rounds[0] = (fullest.astype(jnp.int32) + ROOM - 1) >> 3


def root_part(q_ref, blocks, values, out):
    for g in range(KV):
        for n, (_, v) in enumerate(blocks):
            rows = slice(n * 512, (n + 1) * 512)
            values[g, rows, :HD] = v[:, g * HD : (g + 1) * HD]
            values[g, rows, HD:] = jnp.ones((512, HD), BF16)
    diagonal = head_diagonal()
    line = None
    for g in range(KV):
        heads = slice(g * GROUP, (g + 1) * GROUP)
        lanes = slice(g * HD, (g + 1) * HD)
        query = q_ref[:, heads, :].reshape(COLUMN * GROUP, HD)
        scores = [scores_of(query, k[:, lanes]) for k, _ in blocks]
        peak = functools.reduce(jnp.maximum, [jnp.max(s, axis=1, keepdims=True) for s in scores])
        numer = None
        for n, s in enumerate(scores):
            weights = jnp.exp2((s - peak) * SCALE2).astype(BF16)
            part = dot(weights, values[g, n * 512 : (n + 1) * 512, :])
            numer = part if numer is None else numer + part
        total = numer[:, HD:]
        share = (numer[:, :HD] / total).astype(BF16)
        out[:, heads, :] = share.reshape(COLUMN, GROUP, HD)
        level = (peak * SCALE2 + jnp.log2(total)).reshape(COLUMN, GROUP, HD)
        part = jnp.sum(jnp.where(diagonal[None, heads], level, 0.0), axis=1)
        line = part if line is None else line + part
    out[:, HEADS:, :] = level_parts(line)


def home_part(length_ref, q_ref, wk, wv, sk, sv, nk, nv, share_ref, level_ref):
    diagonal = head_diagonal()
    first = lax.axis_index("z") * HOME
    pad = jnp.zeros((3, KV * HD), F32)
    few_k, few_v = (
        [
            jnp.concatenate([s[j].astype(F32), n[j : j + 1].astype(F32), pad]).astype(BF16)
            for j in range(HOME)
        ]
        for s, n in ((sk, nk), (sv, nv))
    )
    pairs = [(g, j) for g in range(KV) for j in range(HOME)]
    recent, few = [], []
    for g, j in pairs:
        lanes = slice(g * HD, (g + 1) * HD)
        query = q_ref[first + j, g * GROUP : (g + 1) * GROUP, :]
        used = iota((GROUP, 512), 1) < length_ref[j]
        recent.append(jnp.where(used, scores_of(query, wk[j, :, lanes]), FLOOR))
        few.append(scores_of(query, few_k[j][:, lanes]))
    recent = jnp.concatenate(recent, axis=0)
    few = jnp.concatenate(few, axis=0)
    few = jnp.where(iota(few.shape, 1) < 5, few, FLOOR)
    peak = jnp.maximum(jnp.max(recent, axis=1, keepdims=True), jnp.max(few, axis=1, keepdims=True))
    recent = jnp.exp2((recent - peak) * SCALE2)
    few = jnp.exp2((few - peak) * SCALE2)
    total = jnp.sum(recent, axis=1, keepdims=True) + jnp.sum(few, axis=1, keepdims=True)
    recent, few = recent.astype(BF16), few.astype(BF16)
    level = jnp.broadcast_to(peak * SCALE2 + jnp.log2(total), (KV * HOME * GROUP, HD))
    level = level.reshape(KV, HOME, GROUP, HD)
    line = None
    for g in range(KV):
        part = jnp.where(diagonal[None, g * GROUP : (g + 1) * GROUP], level[g], 0.0)
        part = jnp.sum(part, axis=1)
        line = part if line is None else line + part
    level_ref[...] = line
    for n, (g, j) in enumerate(pairs):
        lanes = slice(g * HD, (g + 1) * HD)
        rows = slice(n * GROUP, (n + 1) * GROUP)
        numer = dot(recent[rows], wv[j, :, lanes]) + dot(few[rows], few_v[j][:, lanes])
        share_ref[j, g * GROUP : (g + 1) * GROUP, :] = numer / total[rows]


def near_kernel(
    length_ref, q_ref, k, v, wk, wv, sk, sv, nk, nv, out, share, level, values, wks, wvs, sems
):
    copies = [
        pltpu.make_async_copy(wk, wks, sems.at[0]),
        pltpu.make_async_copy(wv, wvs, sems.at[1]),
    ]
    for copy in copies:
        copy.start()
    root_part(q_ref, [(k, v)], values, out)
    for copy in copies:
        copy.wait()
    home_part(length_ref, q_ref, wks, wvs, sk, sv, nk, nv, share, level)


def far_kernel(q_ref, *refs):
    out, values = refs[-2:]
    blocks = refs[:-2]
    root_part(q_ref, list(zip(blocks[::2], blocks[1::2])), values, out)


def select_kernel(plan, turn, q_ref, out):
    start = turn if isinstance(turn, int) else turn[0] * ROOM
    chats = [plan[t, start + e] for t in range(NX) for e in range(ROOM)]
    for n, chat in enumerate(chats):
        out[n] = q_ref[chat]


def prefix_kernel(plan, turn, q_ref, pk0, pk1, pv0, pv1, out, qs, lists):
    start = turn if isinstance(turn, int) else turn[0] * ROOM
    diagonal = head_diagonal()
    zero = jnp.int32(0)
    lists[0, 0] = zero
    lists[1, 0] = zero
    n0, n1 = zero, zero
    for s in range(NX):

        def scan(e, found, s=s):
            slot = plan[NX + s, start + e]
            lists[0, found[0]] = s * ROOM + e
            lists[1, found[1]] = s * ROOM + e
            return found[0] + 1 - slot, found[1] + slot

        left = jnp.clip(plan[2 * NX, NX + s] - start, 0, ROOM)
        n0, n1 = lax.fori_loop(0, left, scan, (n0, n1))
    slots = ((pk0, pv0, n0), (pk1, pv1, n1))

    def step(b, _):
        results = []
        for i, (pk, pv, count) in enumerate(slots):
            last = jnp.maximum(count - 1, 0)
            chats = [lists[i, jnp.minimum(b * MEMBER + j, last)] for j in range(MEMBER)]
            line = None
            shares = []
            for g in range(KV):
                heads = slice(g * GROUP, (g + 1) * GROUP)
                lanes = slice(g * HD, (g + 1) * HD)
                for j, chat in enumerate(chats):
                    qs[i, g, j] = q_ref[chat, heads, :]
                scores = scores_of(qs[i, g].reshape(MEMBER * GROUP, HD), pk[:, lanes])
                peak = jnp.max(scores, axis=1, keepdims=True)
                weights = jnp.exp2((scores - peak) * SCALE2)
                total = jnp.sum(weights, axis=1, keepdims=True)
                numer = dot(weights.astype(BF16), pv[:, lanes])
                shares.append((numer / total).astype(BF16))
                level = jnp.broadcast_to(peak * SCALE2 + jnp.log2(total), (MEMBER * GROUP, HD))
                level = level.reshape(MEMBER, GROUP, HD)
                part = jnp.sum(jnp.where(diagonal[None, heads], level, 0.0), axis=1)
                line = part if line is None else line + part
            results.append((chats, shares, level_parts(line)))
        for (chats, shares, parts), (_, _, count) in zip(results, slots):

            @pl.when(b * MEMBER < count)
            def _(chats=chats, shares=shares, parts=parts):
                for j, chat in enumerate(chats):
                    for g in range(KV):
                        rows = slice(j * GROUP, (j + 1) * GROUP)
                        out[chat, g * GROUP : (g + 1) * GROUP, :] = shares[g][rows]
                    out[chat, HEADS:, :] = parts[j]

        return 0

    lax.fori_loop(0, (jnp.maximum(n0, n1) + MEMBER - 1) >> 3, step, 0)


def place_answers(plan, start, back, out):
    row = iota((COLUMN, ROWS, HD), 1)
    out[...] = jnp.where(row == HEADS, FLOOR, 0.0).astype(BF16)
    for t in range(NX):

        def place(e, _, t=t):
            out[plan[t, start + e]] = back[t * ROOM + e]
            return 0

        lax.fori_loop(0, jnp.clip(plan[2 * NX, t] - start, 0, ROOM), place, 0)


def weights_of(levels):
    top = functools.reduce(jnp.maximum, levels)
    weights = [jnp.exp2(v - top) for v in levels]
    total = functools.reduce(jnp.add, weights)
    return [w / total for w in weights], top + jnp.log2(total)


def read_level(ref):
    return jnp.sum(ref[:, HEADS:, :].astype(F32), axis=1)


def four_lines(weights):
    quarter = iota((1, HD), 1) // HEADS
    return functools.reduce(
        jnp.add, [jnp.where(quarter == i, w, 0.0) for i, w in enumerate(weights)]
    )


def mix(diagonal, line, shares):
    spread = jnp.where(diagonal, line, 0.0)
    high = spread.astype(BF16)
    low = (spread - high.astype(F32)).astype(BF16)
    return dot(high, shares) + dot(low, shares)


def more_kernel(plan, turn, back, before, out, prefix):
    diagonal = head_diagonal()
    place_answers(plan, turn[0] * ROOM, back, prefix)
    weights, total = weights_of([read_level(r) for r in (before, prefix)])
    line = four_lines(weights)
    out[:, HEADS:, :] = level_parts(total)
    empty = jnp.zeros((2 * HEADS, HD), BF16)
    for i in range(COLUMN):
        shares = jnp.concatenate([before[i, :HEADS, :], prefix[i, :HEADS, :], empty], axis=0)
        out[i, :HEADS, :] = mix(diagonal, line[i : i + 1], shares).astype(BF16)


def merge_row_kernel(plan, near, far, back, share_ref, level_ref, out, prefix, levels):
    diagonal = head_diagonal()
    place_answers(plan, 0, back, prefix)
    level = [read_level(r) for r in (near, far, prefix)]
    weights, total = weights_of(level)
    line = four_lines(weights)
    for n, v in enumerate(level):
        levels[n] = v
    out[:, HEADS:, :] = level_parts(total)
    empty = jnp.zeros((HEADS, HD), BF16)

    def parts(i, fourth):
        sources = [near[i, :HEADS, :], far[i, :HEADS, :], prefix[i, :HEADS, :], fourth]
        return jnp.concatenate(sources, axis=0)

    for i in range(COLUMN):
        out[i, :HEADS, :] = mix(diagonal, line[i : i + 1], parts(i, empty)).astype(BF16)

    first = lax.axis_index("z") * HOME
    own = pl.ds(first, HOME)
    weights, total = weights_of([levels[n, own, :] for n in range(3)] + [level_ref[...]])
    line = four_lines(weights)
    rest = four_lines(weights[3:])
    out[own, HEADS:, :] = level_parts(total)
    nothing = jnp.zeros((3 * HEADS, HD), BF16)
    for j in range(HOME):
        home = share_ref[j]
        high = home.astype(BF16)
        low = jnp.concatenate([(home - high.astype(F32)).astype(BF16), nothing], axis=0)
        total = mix(diagonal, line[j : j + 1], parts(first + j, high))
        total = total + mix(diagonal, rest[j : j + 1], low)
        out[first + j, :HEADS, :] = total.astype(BF16)


def merge_kernel(in_ref, out):
    diagonal = head_diagonal()
    for y in range(NY):
        level = jnp.sum(in_ref[:, y, HEADS:, :].astype(F32), axis=1)
        weights = jnp.exp2(level - jnp.max(level, axis=0, keepdims=True))
        weights = weights / jnp.sum(weights, axis=0, keepdims=True)
        total = jnp.zeros((HEADS, HD), F32)
        for k in range(0, NZ, 4):
            line = four_lines([weights[k + i : k + i + 1] for i in range(4)])
            shares = in_ref[k : k + 4, y, :HEADS, :].reshape(4 * HEADS, HD)
            total = total + mix(diagonal, line, shares)
        out[y] = total.astype(BF16)


def kernel(
    body, name, outs, args, scalars=0, scratch=(), limit=8, us=0.5, in_specs=None, out_specs=None
):
    return pl.pallas_call(
        body,
        out_shape=outs,
        in_specs=in_specs or [SMEM] * scalars + [VMEM] * (len(args) - scalars),
        out_specs=out_specs if out_specs is not None else jax.tree.map(lambda _: VMEM, outs),
        scratch_shapes=list(scratch),
        compiler_params=pltpu.CompilerParams(vmem_limit_bytes=limit * MIB),
        cost_estimate=pl.CostEstimate(
            flops=int(us * 8e8), bytes_accessed=int(us * 1e6), transcendentals=0
        ),
        name=name,
    )(*args)


def send(array, axis, shift):
    size = {"x": NX, "z": NZ, "c": NC, "y": NY}[axis]
    return lax.ppermute(array, axis, [(i, (i + shift) % size) for i in range(size)])


def shaped(*shape, dtype=BF16):
    return jax.ShapeDtypeStruct(shape, dtype)


def local(
    queries,
    new_keys,
    new_values,
    sink_keys,
    sink_values,
    window_keys,
    window_values,
    window_len,
    root_keys,
    root_values,
    prefix_keys,
    prefix_values,
    tenant_of,
    owner,
):
    spread = jnp.broadcast_to(queries.reshape(1, NY, HEADS, HD), (NZ, NY, HEADS, HD))
    q = lax.all_to_all(
        spread.reshape(COLUMN, HEADS, HD), ("z", "y"), split_axis=0, concat_axis=0, tiled=True
    )

    k_left, v_left = send(root_keys, "x", 1), send(root_values, "x", 1)
    k_right, v_right = send(root_keys, "x", -1), send(root_values, "x", -1)
    i32 = jnp.int32
    tenant_of, _ = lax.optimization_barrier((tenant_of, spread))
    plan, rounds = kernel(
        prepare_kernel,
        "prepare",
        [shaped(2 * NX + 1, COLUMN + 1, dtype=i32), shaped(1, dtype=i32)],
        [tenant_of, owner, tenant_of.reshape(1, -1), owner.reshape(1, -1)],
        scalars=2,
        out_specs=[SMEM] * 2,
        us=2,
    )
    anywhere = pl.BlockSpec(memory_space=pl.ANY)
    near, home_share, home_level = kernel(
        near_kernel,
        "near",
        [
            shaped(COLUMN, ROWS, HD),
            shaped(HOME, HEADS, HD, dtype=F32),
            shaped(HOME, HD, dtype=F32),
        ],
        [
            window_len,
            q,
            root_keys,
            root_values,
            window_keys,
            window_values,
            sink_keys,
            sink_values,
            new_keys,
            new_values,
        ],
        in_specs=[SMEM] + [VMEM] * 3 + [anywhere] * 2 + [VMEM] * 4,
        scratch=[
            pltpu.VMEM((KV, 512, 2 * HD), BF16),
            pltpu.VMEM(window_keys.shape, BF16),
            pltpu.VMEM(window_values.shape, BF16),
            pltpu.SemaphoreType.DMA((2,)),
        ],
        limit=14,
        us=4,
    )

    def scalar_kernel(body, name, outs, turn, args, **options):
        if isinstance(turn, int):
            return kernel(
                lambda plan, *refs: body(plan, turn, *refs),
                name,
                outs,
                [plan, *args],
                scalars=1,
                **options,
            )
        return kernel(body, name, outs, [plan, turn, *args], scalars=2, **options)

    def prefix_picked(turn):
        return scalar_kernel(select_kernel, "select", shaped(NX * ROOM, HEADS, HD), turn, [q])

    picked = prefix_picked(0)
    tied = (prefix_keys, prefix_values, k_left, v_left, k_right, v_right, plan)
    pk, pv, k_left, v_left, k_right, v_right, plan = lax.optimization_barrier(tied)
    k_far, v_far = send(k_left, "x", 1), send(v_right, "x", -1)
    pk1, pv1 = send(pk, "c", 1), send(pv, "c", 1)
    rk, rv, _ = lax.optimization_barrier((root_keys, root_values, picked))
    others = [(send(rk, "c", 1), send(rv, "c", 1))]
    for k, v in ((k_left, v_left), (k_right, v_right), (k_far, v_far)):
        others += [(k, v), (send(k, "c", 1), send(v, "c", 1))]

    def prefix_answers(turn, picked):
        asked = lax.all_to_all(picked, "x", split_axis=0, concat_axis=0, tiled=True)
        answer = scalar_kernel(
            prefix_kernel,
            "prefix",
            shaped(NX * ROOM, ROWS, HD),
            turn,
            [asked, prefix_keys, pk1, prefix_values, pv1],
            scratch=[
                pltpu.VMEM((2, KV, MEMBER, GROUP, HD), BF16),
                pltpu.SMEM((2, NX * ROOM + 1), i32),
            ],
            us=2,
        )
        return lax.all_to_all(answer, "x", split_axis=0, concat_axis=0, tiled=True)

    def more(state):
        turn, before = state
        after = kernel(
            more_kernel,
            "more",
            shaped(COLUMN, ROWS, HD),
            [plan, turn, prefix_answers(turn, prefix_picked(turn)), before],
            scalars=2,
            scratch=[pltpu.VMEM((COLUMN, ROWS, HD), BF16)],
        )
        return turn + 1, after

    answers = prefix_answers(0, picked)
    _, near = lax.while_loop(
        lambda state: state[0][0] < rounds[0], more, (jnp.ones((1,), i32), near)
    )
    far = kernel(
        far_kernel,
        "far",
        shaped(COLUMN, ROWS, HD),
        [q, *(ref for block in others for ref in block)],
        scratch=[pltpu.VMEM((KV, (2 * NX - 1) * 512, 2 * HD), BF16)],
        limit=36,
        us=6,
    )
    merged = kernel(
        merge_row_kernel,
        "merge_row",
        shaped(COLUMN, ROWS, HD),
        [plan, near, far, answers, home_share, home_level],
        scalars=1,
        scratch=[
            pltpu.VMEM((COLUMN, ROWS, HD), BF16),
            pltpu.VMEM((3, COLUMN, HD), F32),
        ],
        us=1.5,
    )
    back = lax.all_to_all(merged, ("z", "y"), split_axis=0, concat_axis=0, tiled=True)
    out = kernel(
        merge_kernel, "merge", shaped(NY, HEADS, HD), [back.reshape(NZ, NY, ROWS, HD)]
    )
    return out.reshape(1, NY * HEADS * HD)


def solution(mesh):
    fine = Mesh(mesh.devices.reshape(NX, NZ, NC, NY), ("x", "z", "c", "y"))
    session = ("x", "z", "c")
    placed = (
        P(("x", "z", "c", "y"), None),
        P(session, "y"),
        P(session, "y"),
        P(session, None, "y"),
        P(session, None, "y"),
        P(session, None, "y"),
        P(session, None, "y"),
        P(session),
        P(session, "y"),
        P(session, "y"),
        P(session, "y"),
        P(session, "y"),
        P(),
        P(),
    )
    return jax.shard_map(
        local,
        mesh=fine,
        in_specs=placed,
        out_specs=P(("x", "z", "c", "y"), None),
        check_vma=False,
    )
```

```python
import functools
import math

import jax
import jax.numpy as jnp
from jax import lax
from jax.experimental import pallas as pl
from jax.experimental.pallas import tpu as pltpu
from jax.sharding import Mesh, PartitionSpec as P

HD = 128
GROUP = 16
KV = 2
HEADS = KV * GROUP
HOME = 4
NX, NZ, NC, NY = 4, 8, 2, 4
ROWS = 40
SCALE2 = HD**-0.5 * math.log2(math.e)
FLOOR = -1e30
COLUMN = NZ * HOME
MEMBER = 8
ROOM = 8
MIB = 2**20

NT = (((1,), (1,)), ((), ()))
VMEM = pl.BlockSpec(memory_space=pltpu.VMEM)
SMEM = pl.BlockSpec(memory_space=pltpu.SMEM)
BF16 = jnp.bfloat16
F32 = jnp.float32


def scores_of(query, keys):
    return lax.dot_general(query, keys, NT, preferred_element_type=F32)


def dot(a, b):
    return jnp.dot(a, b, preferred_element_type=F32)


def iota(shape, dim):
    return lax.broadcasted_iota(jnp.int32, shape, dim)


def head_diagonal():
    return (iota((HEADS, HD), 1) % HEADS) == iota((HEADS, HD), 0)


def level_parts(level):
    first = level.astype(BF16).astype(F32)
    second = (level - first).astype(BF16).astype(F32)
    third = level - first - second
    row = iota((1, 8, HD), 1)
    parts = jnp.where(row == 2, third[:, None], 0.0)
    parts = jnp.where(row == 1, second[:, None], parts)
    return jnp.where(row == 0, first[:, None], parts).astype(BF16)


def prepare_kernel(tenant_ref, owner_ref, t_row, o_row, plan, rounds):
    x, z, c = lax.axis_index("x"), lax.axis_index("z"), lax.axis_index("c")
    zero = jnp.int32(0)

    def clear(i, _):
        for t in range(NX):
            plan[t, i] = zero
        return 0

    lax.fori_loop(0, COLUMN + 1, clear, 0, unroll=11)

    def slot_of(s, i):
        return owner_ref[tenant_ref[((s * NZ + (i >> 2)) * 2 + c) * HOME + (i & 3)]]

    def scan_send(i, found):
        slot = slot_of(x, i)
        target = jnp.where(((slot >> 1) & (NZ - 1)) == z, slot >> 4, NX)
        new = []
        for t in range(NX):
            plan[t, found[t]] = i
            new.append(found[t] + (target == t).astype(jnp.int32))
        return tuple(new)

    found = lax.fori_loop(0, COLUMN, scan_send, (zero,) * NX, unroll=8)
    for t in range(NX):
        plan[2 * NX, t] = found[t]

    mine = x * NZ + z

    def scan_recv(i, found):
        new = []
        for s in range(NX):
            slot = slot_of(s, i)
            plan[NX + s, found[s]] = (slot & 1) ^ c
            new.append(found[s] + ((slot >> 1) == mine).astype(jnp.int32))
        return tuple(new)

    found = lax.fori_loop(0, COLUMN, scan_recv, (zero,) * NX, unroll=4)
    for s in range(NX):
        plan[2 * NX, NX + s] = found[s]

    chats = NX * NC * COLUMN
    tenants = o_row.shape[1]
    o_col = jnp.sum(
        jnp.where(iota((tenants, tenants), 0) == iota((tenants, tenants), 1), o_row[...] >> 1, 0),
        axis=1,
        keepdims=True,
    )
    by_row = jnp.sum(
        jnp.where(t_row[...] == iota((tenants, chats), 0), o_col, 0), axis=0, keepdims=True
    )

    def key(chip, chat):
        place = chat >> 2
        return (((place >> 4) * 2 + (place & 1)) << 5) + chip

    row = key(by_row, iota((1, chats), 1))
    square = (chats, chats)
    col = jnp.sum(
        jnp.where(iota(square, 0) == iota(square, 1), row, 0), axis=1, keepdims=True
    )
    fullest = jnp.max(jnp.sum(jnp.where(col == row, 1.0, 0.0), axis=1, keepdims=True))
    rounds[0] = (fullest.astype(jnp.int32) + ROOM - 1) >> 3


def root_part(q_ref, blocks, values, out):
    for g in range(KV):
        for n, (_, v) in enumerate(blocks):
            rows = slice(n * 512, (n + 1) * 512)
            values[g, rows, :HD] = v[:, g * HD : (g + 1) * HD]
            values[g, rows, HD:] = jnp.ones((512, HD), BF16)
    diagonal = head_diagonal()
    rows = COLUMN // 2
    for h in range(2):
        chats = slice(h * rows, (h + 1) * rows)
        line = None
        for g in range(KV):
            heads = slice(g * GROUP, (g + 1) * GROUP)
            lanes = slice(g * HD, (g + 1) * HD)
            query = q_ref[chats, heads, :].reshape(rows * GROUP, HD)
            scores = [scores_of(query, k[:, lanes]) for k, _ in blocks]
            peak = jnp.max(functools.reduce(jnp.maximum, scores), axis=1, keepdims=True)
            numer = None
            for n, s in enumerate(scores):
                weights = jnp.exp2((s - peak) * SCALE2).astype(BF16)
                part = dot(weights, values[g, n * 512 : (n + 1) * 512, :])
                numer = part if numer is None else numer + part
            total = numer[:, HD:]
            share = (numer[:, :HD] / total).astype(BF16)
            out[chats, heads, :] = share.reshape(rows, GROUP, HD)
            level = (peak * SCALE2 + jnp.log2(total)).reshape(rows, GROUP, HD)
            part = jnp.sum(jnp.where(diagonal[None, heads], level, 0.0), axis=1)
            line = part if line is None else line + part
        out[chats, HEADS:, :] = level_parts(line)


def home_part(length_ref, q_ref, wk, wv, sk, sv, nk, nv, share_ref, level_ref):
    diagonal = head_diagonal()
    first = lax.axis_index("z") * HOME
    pad = jnp.zeros((3, KV * HD), F32)
    few_k, few_v = (
        [
            jnp.concatenate([s[j].astype(F32), n[j : j + 1].astype(F32), pad]).astype(BF16)
            for j in range(HOME)
        ]
        for s, n in ((sk, nk), (sv, nv))
    )
    pairs = [(g, j) for g in range(KV) for j in range(HOME)]
    recent, few = [], []
    for g, j in pairs:
        lanes = slice(g * HD, (g + 1) * HD)
        query = q_ref[first + j, g * GROUP : (g + 1) * GROUP, :]
        used = iota((GROUP, 512), 1) < length_ref[j]
        recent.append(jnp.where(used, scores_of(query, wk[j, :, lanes]), FLOOR))
        few.append(scores_of(query, few_k[j][:, lanes]))
    recent = jnp.concatenate(recent, axis=0)
    few = jnp.concatenate(few, axis=0)
    few = jnp.where(iota(few.shape, 1) < 5, few, FLOOR)
    peak = jnp.maximum(jnp.max(recent, axis=1, keepdims=True), jnp.max(few, axis=1, keepdims=True))
    recent = jnp.exp2((recent - peak) * SCALE2)
    few = jnp.exp2((few - peak) * SCALE2)
    total = jnp.sum(recent, axis=1, keepdims=True) + jnp.sum(few, axis=1, keepdims=True)
    recent, few = recent.astype(BF16), few.astype(BF16)
    level = jnp.broadcast_to(peak * SCALE2 + jnp.log2(total), (KV * HOME * GROUP, HD))
    level = level.reshape(KV, HOME, GROUP, HD)
    line = None
    for g in range(KV):
        part = jnp.where(diagonal[None, g * GROUP : (g + 1) * GROUP], level[g], 0.0)
        part = jnp.sum(part, axis=1)
        line = part if line is None else line + part
    level_ref[...] = line
    for n, (g, j) in enumerate(pairs):
        lanes = slice(g * HD, (g + 1) * HD)
        rows = slice(n * GROUP, (n + 1) * GROUP)
        numer = dot(recent[rows], wv[j, :, lanes]) + dot(few[rows], few_v[j][:, lanes])
        share_ref[j, g * GROUP : (g + 1) * GROUP, :] = numer / total[rows]


def near_kernel(
    length_ref, q_ref, k, v, wk, wv, sk, sv, nk, nv, out, share, level, values, wks, wvs, sems
):
    copies = [
        pltpu.make_async_copy(wk, wks, sems.at[0]),
        pltpu.make_async_copy(wv, wvs, sems.at[1]),
    ]
    for copy in copies:
        copy.start()
    root_part(q_ref, [(k, v)], values, out)
    for copy in copies:
        copy.wait()
    home_part(length_ref, q_ref, wks, wvs, sk, sv, nk, nv, share, level)


def far_kernel(q_ref, *refs):
    out, values = refs[-2:]
    blocks = refs[:-2]
    root_part(q_ref, list(zip(blocks[::2], blocks[1::2])), values, out)


def select_kernel(plan, turn, q_ref, out):
    start = turn if isinstance(turn, int) else turn[0] * ROOM
    chats = [plan[t, start + e] for t in range(NX) for e in range(ROOM)]
    for n, chat in enumerate(chats):
        out[n] = q_ref[chat]


def prefix_kernel(plan, turn, q_ref, pk0, pk1, pv0, pv1, out, qs, lists):
    start = turn if isinstance(turn, int) else turn[0] * ROOM
    diagonal = head_diagonal()
    zero = jnp.int32(0)
    lists[0, 0] = zero
    lists[1, 0] = zero
    n0, n1 = zero, zero
    for s in range(NX):

        def scan(e, found, s=s):
            slot = plan[NX + s, start + e]
            lists[0, found[0]] = s * ROOM + e
            lists[1, found[1]] = s * ROOM + e
            return found[0] + 1 - slot, found[1] + slot

        left = jnp.clip(plan[2 * NX, NX + s] - start, 0, ROOM)
        n0, n1 = lax.fori_loop(0, left, scan, (n0, n1))
    slots = ((pk0, pv0, n0), (pk1, pv1, n1))

    def step(b, _):
        results = []
        for i, (pk, pv, count) in enumerate(slots):
            last = jnp.maximum(count - 1, 0)
            chats = [lists[i, jnp.minimum(b * MEMBER + j, last)] for j in range(MEMBER)]
            line = None
            shares = []
            for g in range(KV):
                heads = slice(g * GROUP, (g + 1) * GROUP)
                lanes = slice(g * HD, (g + 1) * HD)
                for j, chat in enumerate(chats):
                    qs[i, g, j] = q_ref[chat, heads, :]
                scores = scores_of(qs[i, g].reshape(MEMBER * GROUP, HD), pk[:, lanes])
                peak = jnp.max(scores, axis=1, keepdims=True)
                weights = jnp.exp2((scores - peak) * SCALE2)
                total = jnp.sum(weights, axis=1, keepdims=True)
                numer = dot(weights.astype(BF16), pv[:, lanes])
                shares.append((numer / total).astype(BF16))
                level = jnp.broadcast_to(peak * SCALE2 + jnp.log2(total), (MEMBER * GROUP, HD))
                level = level.reshape(MEMBER, GROUP, HD)
                part = jnp.sum(jnp.where(diagonal[None, heads], level, 0.0), axis=1)
                line = part if line is None else line + part
            results.append((chats, shares, level_parts(line)))
        for (chats, shares, parts), (_, _, count) in zip(results, slots):

            @pl.when(b * MEMBER < count)
            def _(chats=chats, shares=shares, parts=parts):
                for j, chat in enumerate(chats):
                    for g in range(KV):
                        rows = slice(j * GROUP, (j + 1) * GROUP)
                        out[chat, g * GROUP : (g + 1) * GROUP, :] = shares[g][rows]
                    out[chat, HEADS:, :] = parts[j]

        return 0

    lax.fori_loop(0, (jnp.maximum(n0, n1) + MEMBER - 1) >> 3, step, 0)


def place_answers(plan, start, back, out):
    row = iota((COLUMN, ROWS, HD), 1)
    out[...] = jnp.where(row == HEADS, FLOOR, 0.0).astype(BF16)
    for t in range(NX):

        def place(e, _, t=t):
            out[plan[t, start + e]] = back[t * ROOM + e]
            return 0

        lax.fori_loop(0, jnp.clip(plan[2 * NX, t] - start, 0, ROOM), place, 0)


def weights_of(levels):
    top = functools.reduce(jnp.maximum, levels)
    weights = [jnp.exp2(v - top) for v in levels]
    total = functools.reduce(jnp.add, weights)
    return [w / total for w in weights], top + jnp.log2(total)


def read_level(ref):
    return jnp.sum(ref[:, HEADS:, :].astype(F32), axis=1)


def four_lines(weights):
    quarter = iota((1, HD), 1) // HEADS
    return functools.reduce(
        jnp.add, [jnp.where(quarter == i, w, 0.0) for i, w in enumerate(weights)]
    )


def mix(diagonal, line, shares):
    spread = jnp.where(diagonal, line, 0.0)
    high = spread.astype(BF16)
    low = (spread - high.astype(F32)).astype(BF16)
    return dot(high, shares) + dot(low, shares)


def more_kernel(plan, turn, back, before, out, prefix):
    diagonal = head_diagonal()
    place_answers(plan, turn[0] * ROOM, back, prefix)
    weights, total = weights_of([read_level(r) for r in (before, prefix)])
    line = four_lines(weights)
    out[:, HEADS:, :] = level_parts(total)
    empty = jnp.zeros((2 * HEADS, HD), BF16)
    for i in range(COLUMN):
        shares = jnp.concatenate([before[i, :HEADS, :], prefix[i, :HEADS, :], empty], axis=0)
        out[i, :HEADS, :] = mix(diagonal, line[i : i + 1], shares).astype(BF16)


def merge_row_kernel(plan, near, far, back, share_ref, level_ref, out, prefix, levels):
    diagonal = head_diagonal()
    place_answers(plan, 0, back, prefix)
    level = [read_level(r) for r in (near, far, prefix)]
    weights, total = weights_of(level)
    line = four_lines(weights)
    for n, v in enumerate(level):
        levels[n] = v
    out[:, HEADS:, :] = level_parts(total)
    empty = jnp.zeros((HEADS, HD), BF16)

    def parts(i, fourth):
        sources = [near[i, :HEADS, :], far[i, :HEADS, :], prefix[i, :HEADS, :], fourth]
        return jnp.concatenate(sources, axis=0)

    for i in range(COLUMN):
        out[i, :HEADS, :] = mix(diagonal, line[i : i + 1], parts(i, empty)).astype(BF16)

    first = lax.axis_index("z") * HOME
    own = pl.ds(first, HOME)
    weights, total = weights_of([levels[n, own, :] for n in range(3)] + [level_ref[...]])
    line = four_lines(weights)
    rest = four_lines(weights[3:])
    out[own, HEADS:, :] = level_parts(total)
    nothing = jnp.zeros((3 * HEADS, HD), BF16)
    for j in range(HOME):
        home = share_ref[j]
        high = home.astype(BF16)
        low = jnp.concatenate([(home - high.astype(F32)).astype(BF16), nothing], axis=0)
        total = mix(diagonal, line[j : j + 1], parts(first + j, high))
        total = total + mix(diagonal, rest[j : j + 1], low)
        out[first + j, :HEADS, :] = total.astype(BF16)


def merge_kernel(in_ref, out):
    diagonal = head_diagonal()
    for y in range(NY):
        level = jnp.sum(in_ref[:, y, HEADS:, :].astype(F32), axis=1)
        weights = jnp.exp2(level - jnp.max(level, axis=0, keepdims=True))
        weights = weights / jnp.sum(weights, axis=0, keepdims=True)
        total = jnp.zeros((HEADS, HD), F32)
        for k in range(0, NZ, 4):
            line = four_lines([weights[k + i : k + i + 1] for i in range(4)])
            shares = in_ref[k : k + 4, y, :HEADS, :].reshape(4 * HEADS, HD)
            total = total + mix(diagonal, line, shares)
        out[y] = total.astype(BF16)


def kernel(
    body, name, outs, args, scalars=0, scratch=(), limit=8, us=0.5, in_specs=None, out_specs=None
):
    return pl.pallas_call(
        body,
        out_shape=outs,
        in_specs=in_specs or [SMEM] * scalars + [VMEM] * (len(args) - scalars),
        out_specs=out_specs if out_specs is not None else jax.tree.map(lambda _: VMEM, outs),
        scratch_shapes=list(scratch),
        compiler_params=pltpu.CompilerParams(vmem_limit_bytes=limit * MIB),
        cost_estimate=pl.CostEstimate(
            flops=int(us * 8e8), bytes_accessed=int(us * 1e6), transcendentals=0
        ),
        name=name,
    )(*args)


def send(array, axis, shift):
    size = {"x": NX, "z": NZ, "c": NC, "y": NY}[axis]
    return lax.ppermute(array, axis, [(i, (i + shift) % size) for i in range(size)])


def shaped(*shape, dtype=BF16):
    return jax.ShapeDtypeStruct(shape, dtype)


def local(
    queries,
    new_keys,
    new_values,
    sink_keys,
    sink_values,
    window_keys,
    window_values,
    window_len,
    root_keys,
    root_values,
    prefix_keys,
    prefix_values,
    tenant_of,
    owner,
):
    spread = jnp.broadcast_to(queries.reshape(1, NY, HEADS, HD), (NZ, NY, HEADS, HD))
    q = lax.all_to_all(
        spread.reshape(COLUMN, HEADS, HD), ("z", "y"), split_axis=0, concat_axis=0, tiled=True
    )

    k_left, v_left = send(root_keys, "x", 1), send(root_values, "x", 1)
    k_right, v_right = send(root_keys, "x", -1), send(root_values, "x", -1)
    i32 = jnp.int32
    tenant_of, _ = lax.optimization_barrier((tenant_of, spread))
    plan, rounds = kernel(
        prepare_kernel,
        "prepare",
        [shaped(2 * NX + 1, COLUMN + 1, dtype=i32), shaped(1, dtype=i32)],
        [tenant_of, owner, tenant_of.reshape(1, -1), owner.reshape(1, -1)],
        scalars=2,
        out_specs=[SMEM] * 2,
        us=2,
    )
    anywhere = pl.BlockSpec(memory_space=pl.ANY)
    near, home_share, home_level = kernel(
        near_kernel,
        "near",
        [
            shaped(COLUMN, ROWS, HD),
            shaped(HOME, HEADS, HD, dtype=F32),
            shaped(HOME, HD, dtype=F32),
        ],
        [
            window_len,
            q,
            root_keys,
            root_values,
            window_keys,
            window_values,
            sink_keys,
            sink_values,
            new_keys,
            new_values,
        ],
        in_specs=[SMEM] + [VMEM] * 3 + [anywhere] * 2 + [VMEM] * 4,
        scratch=[
            pltpu.VMEM((KV, 512, 2 * HD), BF16),
            pltpu.VMEM(window_keys.shape, BF16),
            pltpu.VMEM(window_values.shape, BF16),
            pltpu.SemaphoreType.DMA((2,)),
        ],
        limit=14,
        us=4,
    )

    def scalar_kernel(body, name, outs, turn, args, **options):
        if isinstance(turn, int):
            return kernel(
                lambda plan, *refs: body(plan, turn, *refs),
                name,
                outs,
                [plan, *args],
                scalars=1,
                **options,
            )
        return kernel(body, name, outs, [plan, turn, *args], scalars=2, **options)

    def prefix_picked(turn):
        return scalar_kernel(select_kernel, "select", shaped(NX * ROOM, HEADS, HD), turn, [q])

    picked = prefix_picked(0)
    tied = (prefix_keys, prefix_values, k_left, v_left, k_right, v_right, plan)
    pk, pv, k_left, v_left, k_right, v_right, plan = lax.optimization_barrier(tied)
    k_far, v_far = send(k_left, "x", 1), send(v_right, "x", -1)
    pk1, pv1 = send(pk, "c", 1), send(pv, "c", 1)
    rk, rv, _ = lax.optimization_barrier((root_keys, root_values, picked))
    others = [(send(rk, "c", 1), send(rv, "c", 1))]
    for k, v in ((k_left, v_left), (k_right, v_right), (k_far, v_far)):
        others += [(k, v), (send(k, "c", 1), send(v, "c", 1))]

    def prefix_answers(turn, picked):
        asked = lax.all_to_all(picked, "x", split_axis=0, concat_axis=0, tiled=True)
        answer = scalar_kernel(
            prefix_kernel,
            "prefix",
            shaped(NX * ROOM, ROWS, HD),
            turn,
            [asked, prefix_keys, pk1, prefix_values, pv1],
            scratch=[
                pltpu.VMEM((2, KV, MEMBER, GROUP, HD), BF16),
                pltpu.SMEM((2, NX * ROOM + 1), i32),
            ],
            us=2,
        )
        return lax.all_to_all(answer, "x", split_axis=0, concat_axis=0, tiled=True)

    def more(state):
        turn, before = state
        after = kernel(
            more_kernel,
            "more",
            shaped(COLUMN, ROWS, HD),
            [plan, turn, prefix_answers(turn, prefix_picked(turn)), before],
            scalars=2,
            scratch=[pltpu.VMEM((COLUMN, ROWS, HD), BF16)],
        )
        return turn + 1, after

    answers = prefix_answers(0, picked)
    _, near = lax.while_loop(
        lambda state: state[0][0] < rounds[0], more, (jnp.ones((1,), i32), near)
    )
    far = kernel(
        far_kernel,
        "far",
        shaped(COLUMN, ROWS, HD),
        [q, *(ref for block in others for ref in block)],
        scratch=[pltpu.VMEM((KV, (2 * NX - 1) * 512, 2 * HD), BF16)],
        limit=28,
        us=6,
    )
    merged = kernel(
        merge_row_kernel,
        "merge_row",
        shaped(COLUMN, ROWS, HD),
        [plan, near, far, answers, home_share, home_level],
        scalars=1,
        scratch=[
            pltpu.VMEM((COLUMN, ROWS, HD), BF16),
            pltpu.VMEM((3, COLUMN, HD), F32),
        ],
        us=1.5,
    )
    back = lax.all_to_all(merged, ("z", "y"), split_axis=0, concat_axis=0, tiled=True)
    out = kernel(
        merge_kernel, "merge", shaped(NY, HEADS, HD), [back.reshape(NZ, NY, ROWS, HD)]
    )
    return out.reshape(1, NY * HEADS * HD)


def solution(mesh):
    fine = Mesh(mesh.devices.reshape(NX, NZ, NC, NY), ("x", "z", "c", "y"))
    session = ("x", "z", "c")
    placed = (
        P(("x", "z", "c", "y"), None),
        P(session, "y"),
        P(session, "y"),
        P(session, None, "y"),
        P(session, None, "y"),
        P(session, None, "y"),
        P(session, None, "y"),
        P(session),
        P(session, "y"),
        P(session, "y"),
        P(session, "y"),
        P(session, "y"),
        P(),
        P(),
    )
    return jax.shard_map(
        local,
        mesh=fine,
        in_specs=placed,
        out_specs=P(("x", "z", "c", "y"), None),
        check_vma=False,
    )
```

```python
import functools
import math

import jax
import jax.numpy as jnp
from jax import lax
from jax.experimental import pallas as pl
from jax.experimental.pallas import tpu as pltpu
from jax.sharding import Mesh, PartitionSpec as P

HD = 128
GROUP = 16
KV = 2
HEADS = KV * GROUP
HOME = 4
NX, NZ, NC, NY = 4, 8, 2, 4
ROWS = 40
SCALE2 = HD**-0.5 * math.log2(math.e)
FLOOR = -1e30
COLUMN = NZ * HOME
MEMBER = 8
ROOM = 8
MIB = 2**20

NT = (((1,), (1,)), ((), ()))
VMEM = pl.BlockSpec(memory_space=pltpu.VMEM)
SMEM = pl.BlockSpec(memory_space=pltpu.SMEM)
BF16 = jnp.bfloat16
F32 = jnp.float32


def scores_of(query, keys):
    return lax.dot_general(query, keys, NT, preferred_element_type=F32)


def dot(a, b):
    return jnp.dot(a, b, preferred_element_type=F32)


def iota(shape, dim):
    return lax.broadcasted_iota(jnp.int32, shape, dim)


def head_diagonal():
    return (iota((HEADS, HD), 1) % HEADS) == iota((HEADS, HD), 0)


def level_parts(level):
    first = level.astype(BF16).astype(F32)
    second = (level - first).astype(BF16).astype(F32)
    third = level - first - second
    row = iota((1, 8, HD), 1)
    parts = jnp.where(row == 2, third[:, None], 0.0)
    parts = jnp.where(row == 1, second[:, None], parts)
    return jnp.where(row == 0, first[:, None], parts).astype(BF16)


def prepare_kernel(tenant_ref, owner_ref, t_row, o_row, plan, rounds):
    x, z, c = lax.axis_index("x"), lax.axis_index("z"), lax.axis_index("c")
    zero = jnp.int32(0)

    def clear(i, _):
        for t in range(NX):
            plan[t, i] = zero
        return 0

    lax.fori_loop(0, COLUMN + 1, clear, 0, unroll=11)

    def slot_of(s, i):
        return owner_ref[tenant_ref[((s * NZ + (i >> 2)) * 2 + c) * HOME + (i & 3)]]

    def scan_send(i, found):
        slot = slot_of(x, i)
        target = jnp.where(((slot >> 1) & (NZ - 1)) == z, slot >> 4, NX)
        new = []
        for t in range(NX):
            plan[t, found[t]] = i
            new.append(found[t] + (target == t).astype(jnp.int32))
        return tuple(new)

    found = lax.fori_loop(0, COLUMN, scan_send, (zero,) * NX, unroll=8)
    for t in range(NX):
        plan[2 * NX, t] = found[t]

    mine = x * NZ + z

    def scan_recv(i, found):
        new = []
        for s in range(NX):
            slot = slot_of(s, i)
            plan[NX + s, found[s]] = (slot & 1) ^ c
            new.append(found[s] + ((slot >> 1) == mine).astype(jnp.int32))
        return tuple(new)

    found = lax.fori_loop(0, COLUMN, scan_recv, (zero,) * NX, unroll=4)
    for s in range(NX):
        plan[2 * NX, NX + s] = found[s]

    chats = NX * NC * COLUMN
    tenants = o_row.shape[1]
    o_col = jnp.sum(
        jnp.where(iota((tenants, tenants), 0) == iota((tenants, tenants), 1), o_row[...] >> 1, 0),
        axis=1,
        keepdims=True,
    )
    by_row = jnp.sum(
        jnp.where(t_row[...] == iota((tenants, chats), 0), o_col, 0), axis=0, keepdims=True
    )

    def key(chip, chat):
        place = chat >> 2
        return (((place >> 4) * 2 + (place & 1)) << 5) + chip

    row = key(by_row, iota((1, chats), 1))
    square = (chats, chats)
    col = jnp.sum(
        jnp.where(iota(square, 0) == iota(square, 1), row, 0), axis=1, keepdims=True
    )
    fullest = jnp.max(jnp.sum(jnp.where(col == row, 1.0, 0.0), axis=1, keepdims=True))
    rounds[0] = (fullest.astype(jnp.int32) + ROOM - 1) >> 3


def root_part(q_ref, blocks, values, out):
    for g in range(KV):
        for n, (_, v) in enumerate(blocks):
            rows = slice(n * 512, (n + 1) * 512)
            values[g, rows, :HD] = v[:, g * HD : (g + 1) * HD]
            values[g, rows, HD:] = jnp.ones((512, HD), BF16)
    diagonal = head_diagonal()
    rows = COLUMN // 2
    for h in range(2):
        chats = slice(h * rows, (h + 1) * rows)
        line = None
        for g in range(KV):
            heads = slice(g * GROUP, (g + 1) * GROUP)
            lanes = slice(g * HD, (g + 1) * HD)
            query = q_ref[chats, heads, :].reshape(rows * GROUP, HD)
            scores = [scores_of(query, k[:, lanes]) for k, _ in blocks]
            peak = jnp.max(functools.reduce(jnp.maximum, scores), axis=1, keepdims=True)
            numer = None
            for n, s in enumerate(scores):
                weights = jnp.exp2((s - peak) * SCALE2).astype(BF16)
                part = dot(weights, values[g, n * 512 : (n + 1) * 512, :])
                numer = part if numer is None else numer + part
            total = numer[:, HD:]
            share = (numer[:, :HD] / total).astype(BF16)
            out[chats, heads, :] = share.reshape(rows, GROUP, HD)
            level = (peak * SCALE2 + jnp.log2(total)).reshape(rows, GROUP, HD)
            part = jnp.sum(jnp.where(diagonal[None, heads], level, 0.0), axis=1)
            line = part if line is None else line + part
        out[chats, HEADS:, :] = level_parts(line)


def home_part(length_ref, q_ref, wk, wv, sk, sv, nk, nv, share_ref, level_ref):
    diagonal = head_diagonal()
    first = lax.axis_index("z") * HOME
    pad = jnp.zeros((3, KV * HD), F32)
    few_k, few_v = (
        [
            jnp.concatenate([s[j].astype(F32), n[j : j + 1].astype(F32), pad]).astype(BF16)
            for j in range(HOME)
        ]
        for s, n in ((sk, nk), (sv, nv))
    )
    pairs = [(g, j) for g in range(KV) for j in range(HOME)]
    recent, few = [], []
    for g, j in pairs:
        lanes = slice(g * HD, (g + 1) * HD)
        query = q_ref[first + j, g * GROUP : (g + 1) * GROUP, :]
        used = iota((GROUP, 512), 1) < length_ref[j]
        recent.append(jnp.where(used, scores_of(query, wk[j, :, lanes]), FLOOR))
        few.append(scores_of(query, few_k[j][:, lanes]))
    recent = jnp.concatenate(recent, axis=0)
    few = jnp.concatenate(few, axis=0)
    few = jnp.where(iota(few.shape, 1) < 5, few, FLOOR)
    peak = jnp.maximum(jnp.max(recent, axis=1, keepdims=True), jnp.max(few, axis=1, keepdims=True))
    recent = jnp.exp2((recent - peak) * SCALE2)
    few = jnp.exp2((few - peak) * SCALE2)
    total = jnp.sum(recent, axis=1, keepdims=True) + jnp.sum(few, axis=1, keepdims=True)
    recent, few = recent.astype(BF16), few.astype(BF16)
    level = jnp.broadcast_to(peak * SCALE2 + jnp.log2(total), (KV * HOME * GROUP, HD))
    level = level.reshape(KV, HOME, GROUP, HD)
    line = None
    for g in range(KV):
        part = jnp.where(diagonal[None, g * GROUP : (g + 1) * GROUP], level[g], 0.0)
        part = jnp.sum(part, axis=1)
        line = part if line is None else line + part
    level_ref[...] = line
    for n, (g, j) in enumerate(pairs):
        lanes = slice(g * HD, (g + 1) * HD)
        rows = slice(n * GROUP, (n + 1) * GROUP)
        numer = dot(recent[rows], wv[j, :, lanes]) + dot(few[rows], few_v[j][:, lanes])
        share_ref[j, g * GROUP : (g + 1) * GROUP, :] = numer / total[rows]


def near_kernel(
    length_ref, q_ref, k, v, wk, wv, sk, sv, nk, nv, out, share, level, values, wks, wvs, sems
):
    copies = [
        pltpu.make_async_copy(wk, wks, sems.at[0]),
        pltpu.make_async_copy(wv, wvs, sems.at[1]),
    ]
    for copy in copies:
        copy.start()
    root_part(q_ref, [(k, v)], values, out)
    for copy in copies:
        copy.wait()
    home_part(length_ref, q_ref, wks, wvs, sk, sv, nk, nv, share, level)


def far_kernel(q_ref, *refs):
    out, values = refs[-2:]
    blocks = refs[:-2]
    root_part(q_ref, list(zip(blocks[::2], blocks[1::2])), values, out)


def select_kernel(plan, turn, q_ref, out):
    start = turn if isinstance(turn, int) else turn[0] * ROOM
    chats = [plan[t, start + e] for t in range(NX) for e in range(ROOM)]
    for n, chat in enumerate(chats):
        out[n] = q_ref[chat]


def prefix_kernel(plan, turn, q_ref, pk0, pk1, pv0, pv1, out, qs, lists):
    start = turn if isinstance(turn, int) else turn[0] * ROOM
    diagonal = head_diagonal()
    zero = jnp.int32(0)
    lists[0, 0] = zero
    lists[1, 0] = zero
    n0, n1 = zero, zero
    for s in range(NX):

        def scan(e, found, s=s):
            slot = plan[NX + s, start + e]
            lists[0, found[0]] = s * ROOM + e
            lists[1, found[1]] = s * ROOM + e
            return found[0] + 1 - slot, found[1] + slot

        left = jnp.clip(plan[2 * NX, NX + s] - start, 0, ROOM)
        n0, n1 = lax.fori_loop(0, left, scan, (n0, n1))
    slots = ((pk0, pv0, n0), (pk1, pv1, n1))

    def part(i, base, size):
        pk, pv, count = slots[i]
        last = jnp.maximum(count - 1, 0)
        chats = [lists[i, jnp.minimum(base + j, last)] for j in range(size)]
        line = None
        shares = []
        for g in range(KV):
            heads = slice(g * GROUP, (g + 1) * GROUP)
            lanes = slice(g * HD, (g + 1) * HD)
            for j, chat in enumerate(chats):
                qs[i, g, j] = q_ref[chat, heads, :]
            scores = scores_of(qs[i, g, :size].reshape(size * GROUP, HD), pk[:, lanes])
            peak = jnp.max(scores, axis=1, keepdims=True)
            weights = jnp.exp2((scores - peak) * SCALE2)
            total = jnp.sum(weights, axis=1, keepdims=True)
            numer = dot(weights.astype(BF16), pv[:, lanes])
            shares.append((numer / total).astype(BF16))
            level = jnp.broadcast_to(peak * SCALE2 + jnp.log2(total), (size * GROUP, HD))
            level = level.reshape(size, GROUP, HD)
            row = jnp.sum(jnp.where(diagonal[None, heads], level, 0.0), axis=1)
            line = row if line is None else line + row
        return chats, shares, level_parts(line)

    def store(chats, shares, parts):
        for j, chat in enumerate(chats):
            for g in range(KV):
                rows = slice(j * GROUP, (j + 1) * GROUP)
                out[chat, g * GROUP : (g + 1) * GROUP, :] = shares[g][rows]
            out[chat, HEADS:, :] = parts[j]

    @pl.when(jnp.maximum(n0, n1) > 0)
    def _():
        results = [part(i, 0, MEMBER) for i in range(2)]
        for i in range(2):
            pl.when(slots[i][2] > 0)(functools.partial(store, *results[i]))

    for i in range(2):

        def further(b, _, i=i):
            store(*part(i, MEMBER + b * (MEMBER // 2), MEMBER // 2))
            return 0

        left = jnp.maximum(slots[i][2] - MEMBER, 0)
        lax.fori_loop(0, (left + MEMBER // 2 - 1) >> 2, further, 0)


def place_answers(plan, start, back, out):
    row = iota((COLUMN, ROWS, HD), 1)
    out[...] = jnp.where(row == HEADS, FLOOR, 0.0).astype(BF16)
    for t in range(NX):

        def place(e, _, t=t):
            out[plan[t, start + e]] = back[t * ROOM + e]
            return 0

        lax.fori_loop(0, jnp.clip(plan[2 * NX, t] - start, 0, ROOM), place, 0)


def weights_of(levels):
    top = functools.reduce(jnp.maximum, levels)
    weights = [jnp.exp2(v - top) for v in levels]
    total = functools.reduce(jnp.add, weights)
    return [w / total for w in weights], top + jnp.log2(total)


def read_level(ref):
    return jnp.sum(ref[:, HEADS:, :].astype(F32), axis=1)


def four_lines(weights):
    quarter = iota((1, HD), 1) // HEADS
    return functools.reduce(
        jnp.add, [jnp.where(quarter == i, w, 0.0) for i, w in enumerate(weights)]
    )


def mix(diagonal, line, shares):
    spread = jnp.where(diagonal, line, 0.0)
    high = spread.astype(BF16)
    low = (spread - high.astype(F32)).astype(BF16)
    return dot(high, shares) + dot(low, shares)


def more_kernel(plan, turn, back, before, out, prefix):
    diagonal = head_diagonal()
    place_answers(plan, turn[0] * ROOM, back, prefix)
    weights, total = weights_of([read_level(r) for r in (before, prefix)])
    line = four_lines(weights)
    out[:, HEADS:, :] = level_parts(total)
    empty = jnp.zeros((2 * HEADS, HD), BF16)
    for i in range(COLUMN):
        shares = jnp.concatenate([before[i, :HEADS, :], prefix[i, :HEADS, :], empty], axis=0)
        out[i, :HEADS, :] = mix(diagonal, line[i : i + 1], shares).astype(BF16)


def merge_row_kernel(plan, near, far, back, share_ref, level_ref, out, prefix, levels):
    diagonal = head_diagonal()
    place_answers(plan, 0, back, prefix)
    level = [read_level(r) for r in (near, far, prefix)]
    weights, total = weights_of(level)
    line = four_lines(weights)
    for n, v in enumerate(level):
        levels[n] = v
    out[:, HEADS:, :] = level_parts(total)
    empty = jnp.zeros((HEADS, HD), BF16)

    def parts(i, fourth):
        sources = [near[i, :HEADS, :], far[i, :HEADS, :], prefix[i, :HEADS, :], fourth]
        return jnp.concatenate(sources, axis=0)

    for i in range(COLUMN):
        out[i, :HEADS, :] = mix(diagonal, line[i : i + 1], parts(i, empty)).astype(BF16)

    first = lax.axis_index("z") * HOME
    own = pl.ds(first, HOME)
    weights, total = weights_of([levels[n, own, :] for n in range(3)] + [level_ref[...]])
    line = four_lines(weights)
    rest = four_lines(weights[3:])
    out[own, HEADS:, :] = level_parts(total)
    nothing = jnp.zeros((3 * HEADS, HD), BF16)
    for j in range(HOME):
        home = share_ref[j]
        high = home.astype(BF16)
        low = jnp.concatenate([(home - high.astype(F32)).astype(BF16), nothing], axis=0)
        total = mix(diagonal, line[j : j + 1], parts(first + j, high))
        total = total + mix(diagonal, rest[j : j + 1], low)
        out[first + j, :HEADS, :] = total.astype(BF16)


def merge_kernel(in_ref, out):
    diagonal = head_diagonal()
    for y in range(NY):
        level = jnp.sum(in_ref[:, y, HEADS:, :].astype(F32), axis=1)
        weights = jnp.exp2(level - jnp.max(level, axis=0, keepdims=True))
        weights = weights / jnp.sum(weights, axis=0, keepdims=True)
        total = jnp.zeros((HEADS, HD), F32)
        for k in range(0, NZ, 4):
            line = four_lines([weights[k + i : k + i + 1] for i in range(4)])
            shares = in_ref[k : k + 4, y, :HEADS, :].reshape(4 * HEADS, HD)
            total = total + mix(diagonal, line, shares)
        out[y] = total.astype(BF16)


def kernel(
    body, name, outs, args, scalars=0, scratch=(), limit=8, us=0.5, in_specs=None, out_specs=None
):
    return pl.pallas_call(
        body,
        out_shape=outs,
        in_specs=in_specs or [SMEM] * scalars + [VMEM] * (len(args) - scalars),
        out_specs=out_specs if out_specs is not None else jax.tree.map(lambda _: VMEM, outs),
        scratch_shapes=list(scratch),
        compiler_params=pltpu.CompilerParams(vmem_limit_bytes=limit * MIB),
        cost_estimate=pl.CostEstimate(
            flops=int(us * 8e8), bytes_accessed=int(us * 1e6), transcendentals=0
        ),
        name=name,
    )(*args)


def send(array, axis, shift):
    size = {"x": NX, "z": NZ, "c": NC, "y": NY}[axis]
    return lax.ppermute(array, axis, [(i, (i + shift) % size) for i in range(size)])


def shaped(*shape, dtype=BF16):
    return jax.ShapeDtypeStruct(shape, dtype)


def local(
    queries,
    new_keys,
    new_values,
    sink_keys,
    sink_values,
    window_keys,
    window_values,
    window_len,
    root_keys,
    root_values,
    prefix_keys,
    prefix_values,
    tenant_of,
    owner,
):
    spread = jnp.broadcast_to(queries.reshape(1, NY, HEADS, HD), (NZ, NY, HEADS, HD))
    q = lax.all_to_all(
        spread.reshape(COLUMN, HEADS, HD), ("z", "y"), split_axis=0, concat_axis=0, tiled=True
    )

    k_left, v_left = send(root_keys, "x", 1), send(root_values, "x", 1)
    k_right, v_right = send(root_keys, "x", -1), send(root_values, "x", -1)
    i32 = jnp.int32
    tenant_of, _ = lax.optimization_barrier((tenant_of, spread))
    plan, rounds = kernel(
        prepare_kernel,
        "prepare",
        [shaped(2 * NX + 1, COLUMN + 1, dtype=i32), shaped(1, dtype=i32)],
        [tenant_of, owner, tenant_of.reshape(1, -1), owner.reshape(1, -1)],
        scalars=2,
        out_specs=[SMEM] * 2,
        us=2,
    )
    anywhere = pl.BlockSpec(memory_space=pl.ANY)
    near, home_share, home_level = kernel(
        near_kernel,
        "near",
        [
            shaped(COLUMN, ROWS, HD),
            shaped(HOME, HEADS, HD, dtype=F32),
            shaped(HOME, HD, dtype=F32),
        ],
        [
            window_len,
            q,
            root_keys,
            root_values,
            window_keys,
            window_values,
            sink_keys,
            sink_values,
            new_keys,
            new_values,
        ],
        in_specs=[SMEM] + [VMEM] * 3 + [anywhere] * 2 + [VMEM] * 4,
        scratch=[
            pltpu.VMEM((KV, 512, 2 * HD), BF16),
            pltpu.VMEM(window_keys.shape, BF16),
            pltpu.VMEM(window_values.shape, BF16),
            pltpu.SemaphoreType.DMA((2,)),
        ],
        limit=14,
        us=4,
    )

    def scalar_kernel(body, name, outs, turn, args, **options):
        if isinstance(turn, int):
            return kernel(
                lambda plan, *refs: body(plan, turn, *refs),
                name,
                outs,
                [plan, *args],
                scalars=1,
                **options,
            )
        return kernel(body, name, outs, [plan, turn, *args], scalars=2, **options)

    def prefix_picked(turn):
        return scalar_kernel(select_kernel, "select", shaped(NX * ROOM, HEADS, HD), turn, [q])

    picked = prefix_picked(0)
    tied = (prefix_keys, prefix_values, k_left, v_left, k_right, v_right, plan)
    pk, pv, k_left, v_left, k_right, v_right, plan = lax.optimization_barrier(tied)
    k_far, v_far = send(k_left, "x", 1), send(v_right, "x", -1)
    pk1, pv1 = send(pk, "c", 1), send(pv, "c", 1)
    rk, rv, _ = lax.optimization_barrier((root_keys, root_values, picked))
    others = [(send(rk, "c", 1), send(rv, "c", 1))]
    for k, v in ((k_left, v_left), (k_right, v_right), (k_far, v_far)):
        others += [(k, v), (send(k, "c", 1), send(v, "c", 1))]

    def over_x(array):
        return lax.all_to_all(array, "x", split_axis=0, concat_axis=0, tiled=True)

    def prefix_answers(turn, asked):
        answer = scalar_kernel(
            prefix_kernel,
            "prefix",
            shaped(NX * ROOM, ROWS, HD),
            turn,
            [asked, prefix_keys, pk1, prefix_values, pv1],
            scratch=[
                pltpu.VMEM((2, KV, MEMBER, GROUP, HD), BF16),
                pltpu.SMEM((2, NX * ROOM + 1), i32),
            ],
            us=2,
        )
        return over_x(answer)

    def more(state):
        turn, before = state
        after = kernel(
            more_kernel,
            "more",
            shaped(COLUMN, ROWS, HD),
            [plan, turn, prefix_answers(turn, over_x(prefix_picked(turn))), before],
            scalars=2,
            scratch=[pltpu.VMEM((COLUMN, ROWS, HD), BF16)],
        )
        return turn + 1, after

    answers = prefix_answers(0, over_x(picked))
    _, near = lax.while_loop(
        lambda state: state[0][0] < rounds[0], more, (jnp.ones((1,), i32), near)
    )
    far = kernel(
        far_kernel,
        "far",
        shaped(COLUMN, ROWS, HD),
        [q, *(ref for block in others for ref in block)],
        scratch=[pltpu.VMEM((KV, (2 * NX - 1) * 512, 2 * HD), BF16)],
        limit=28,
        us=6,
    )
    merged = kernel(
        merge_row_kernel,
        "merge_row",
        shaped(COLUMN, ROWS, HD),
        [plan, near, far, answers, home_share, home_level],
        scalars=1,
        scratch=[
            pltpu.VMEM((COLUMN, ROWS, HD), BF16),
            pltpu.VMEM((3, COLUMN, HD), F32),
        ],
        us=1.5,
    )
    back = lax.all_to_all(merged, ("z", "y"), split_axis=0, concat_axis=0, tiled=True)
    out = kernel(
        merge_kernel, "merge", shaped(NY, HEADS, HD), [back.reshape(NZ, NY, ROWS, HD)]
    )
    return out.reshape(1, NY * HEADS * HD)


def solution(mesh):
    fine = Mesh(mesh.devices.reshape(NX, NZ, NC, NY), ("x", "z", "c", "y"))
    session = ("x", "z", "c")
    placed = (
        P(("x", "z", "c", "y"), None),
        P(session, "y"),
        P(session, "y"),
        P(session, None, "y"),
        P(session, None, "y"),
        P(session, None, "y"),
        P(session, None, "y"),
        P(session),
        P(session, "y"),
        P(session, "y"),
        P(session, "y"),
        P(session, "y"),
        P(),
        P(),
    )
    return jax.shard_map(
        local,
        mesh=fine,
        in_specs=placed,
        out_specs=P(("x", "z", "c", "y"), None),
        check_vma=False,
    )
```

```python
import functools
import math

import jax
import jax.numpy as jnp
from jax import lax
from jax.experimental import pallas as pl
from jax.experimental.pallas import tpu as pltpu
from jax.sharding import Mesh, PartitionSpec as P

HD = 128
GROUP = 16
KV = 2
HEADS = KV * GROUP
HOME = 4
NX, NZ, NC, NY = 4, 8, 2, 4
ROWS = 40
SCALE2 = HD**-0.5 * math.log2(math.e)
FLOOR = -1e30
COLUMN = NZ * HOME
MEMBER = 8
ROOM = 8
MIB = 2**20

NT = (((1,), (1,)), ((), ()))
VMEM = pl.BlockSpec(memory_space=pltpu.VMEM)
SMEM = pl.BlockSpec(memory_space=pltpu.SMEM)
BF16 = jnp.bfloat16
F32 = jnp.float32


def scores_of(query, keys):
    return lax.dot_general(query, keys, NT, preferred_element_type=F32)


def dot(a, b):
    return jnp.dot(a, b, preferred_element_type=F32)


def iota(shape, dim):
    return lax.broadcasted_iota(jnp.int32, shape, dim)


def head_diagonal():
    return (iota((HEADS, HD), 1) % HEADS) == iota((HEADS, HD), 0)


def level_parts(level):
    first = level.astype(BF16).astype(F32)
    second = (level - first).astype(BF16).astype(F32)
    third = level - first - second
    row = iota((1, 8, HD), 1)
    parts = jnp.where(row == 2, third[:, None], 0.0)
    parts = jnp.where(row == 1, second[:, None], parts)
    return jnp.where(row == 0, first[:, None], parts).astype(BF16)


def prepare_kernel(tenant_ref, owner_ref, t_row, o_row, plan, rounds):
    x, z, c = lax.axis_index("x"), lax.axis_index("z"), lax.axis_index("c")
    zero = jnp.int32(0)

    def clear(i, _):
        for t in range(NX):
            plan[t, i] = zero
        return 0

    lax.fori_loop(0, COLUMN + 1, clear, 0, unroll=11)

    def slot_of(s, i):
        return owner_ref[tenant_ref[((s * NZ + (i >> 2)) * 2 + c) * HOME + (i & 3)]]

    def scan_send(i, found):
        slot = slot_of(x, i)
        target = jnp.where(((slot >> 1) & (NZ - 1)) == z, slot >> 4, NX)
        new = []
        for t in range(NX):
            plan[t, found[t]] = i
            new.append(found[t] + (target == t).astype(jnp.int32))
        return tuple(new)

    found = lax.fori_loop(0, COLUMN, scan_send, (zero,) * NX, unroll=8)
    for t in range(NX):
        plan[2 * NX, t] = found[t]

    mine = x * NZ + z

    def scan_recv(i, found):
        new = []
        for s in range(NX):
            slot = slot_of(s, i)
            plan[NX + s, found[s]] = (slot & 1) ^ c
            new.append(found[s] + ((slot >> 1) == mine).astype(jnp.int32))
        return tuple(new)

    found = lax.fori_loop(0, COLUMN, scan_recv, (zero,) * NX, unroll=4)
    for s in range(NX):
        plan[2 * NX, NX + s] = found[s]

    chats = NX * NC * COLUMN
    tenants = o_row.shape[1]
    o_col = jnp.sum(
        jnp.where(iota((tenants, tenants), 0) == iota((tenants, tenants), 1), o_row[...] >> 1, 0),
        axis=1,
        keepdims=True,
    )
    by_row = jnp.sum(
        jnp.where(t_row[...] == iota((tenants, chats), 0), o_col, 0), axis=0, keepdims=True
    )

    def key(chip, chat):
        place = chat >> 2
        return (((place >> 4) * 2 + (place & 1)) << 5) + chip

    row = key(by_row, iota((1, chats), 1))
    square = (chats, chats)
    col = jnp.sum(
        jnp.where(iota(square, 0) == iota(square, 1), row, 0), axis=1, keepdims=True
    )
    fullest = jnp.max(jnp.sum(jnp.where(col == row, 1.0, 0.0), axis=1, keepdims=True))
    rounds[0] = (fullest.astype(jnp.int32) + ROOM - 1) >> 3


def root_part(q_ref, blocks, values, out):
    for g in range(KV):
        for n, (_, v) in enumerate(blocks):
            rows = slice(n * 512, (n + 1) * 512)
            values[g, rows, :HD] = v[:, g * HD : (g + 1) * HD]
            values[g, rows, HD:] = jnp.ones((512, HD), BF16)
    diagonal = head_diagonal()
    rows = COLUMN // 2
    tiles = [(h, g) for h in range(2) for g in range(KV)]

    def score(tile, n):
        h, g = tile
        query = q_ref[h * rows : (h + 1) * rows, g * GROUP : (g + 1) * GROUP, :]
        return scores_of(
            query.reshape(rows * GROUP, HD), blocks[n][0][:, g * HD : (g + 1) * HD]
        )

    count = len(blocks)
    scores = [score(tiles[0], n) for n in range(count)]
    highest = functools.reduce(jnp.maximum, scores)
    line = None
    for t, (h, g) in enumerate(tiles):
        chats = slice(h * rows, (h + 1) * rows)
        heads = slice(g * GROUP, (g + 1) * GROUP)
        peak = jnp.max(highest, axis=1, keepdims=True)
        numer, later, highest = None, [], None
        for n, s in enumerate(scores):
            if t + 1 < len(tiles):
                later.append(score(tiles[t + 1], n))
                highest = later[0] if n == 0 else jnp.maximum(highest, later[n])
            weights = jnp.exp2((s - peak) * SCALE2).astype(BF16)
            part = dot(weights, values[g, n * 512 : (n + 1) * 512, :])
            numer = part if numer is None else numer + part
        scores = later
        total = numer[:, HD:]
        share = (numer[:, :HD] / total).astype(BF16)
        out[chats, heads, :] = share.reshape(rows, GROUP, HD)
        level = (peak * SCALE2 + jnp.log2(total)).reshape(rows, GROUP, HD)
        part = jnp.sum(jnp.where(diagonal[None, heads], level, 0.0), axis=1)
        line = part if g == 0 else line + part
        if g == KV - 1:
            out[chats, HEADS:, :] = level_parts(line)


def home_part(length_ref, q_ref, wk, wv, sk, sv, nk, nv, share_ref, level_ref):
    diagonal = head_diagonal()
    first = lax.axis_index("z") * HOME
    pad = jnp.zeros((3, KV * HD), F32)
    few_k, few_v = (
        [
            jnp.concatenate([s[j].astype(F32), n[j : j + 1].astype(F32), pad]).astype(BF16)
            for j in range(HOME)
        ]
        for s, n in ((sk, nk), (sv, nv))
    )
    pairs = [(g, j) for g in range(KV) for j in range(HOME)]
    recent, few = [], []
    for g, j in pairs:
        lanes = slice(g * HD, (g + 1) * HD)
        query = q_ref[first + j, g * GROUP : (g + 1) * GROUP, :]
        used = iota((GROUP, 512), 1) < length_ref[j]
        recent.append(jnp.where(used, scores_of(query, wk[j, :, lanes]), FLOOR))
        few.append(scores_of(query, few_k[j][:, lanes]))
    recent = jnp.concatenate(recent, axis=0)
    few = jnp.concatenate(few, axis=0)
    few = jnp.where(iota(few.shape, 1) < 5, few, FLOOR)
    peak = jnp.maximum(jnp.max(recent, axis=1, keepdims=True), jnp.max(few, axis=1, keepdims=True))
    recent = jnp.exp2((recent - peak) * SCALE2)
    few = jnp.exp2((few - peak) * SCALE2)
    total = jnp.sum(recent, axis=1, keepdims=True) + jnp.sum(few, axis=1, keepdims=True)
    recent, few = recent.astype(BF16), few.astype(BF16)
    level = jnp.broadcast_to(peak * SCALE2 + jnp.log2(total), (KV * HOME * GROUP, HD))
    level = level.reshape(KV, HOME, GROUP, HD)
    line = None
    for g in range(KV):
        part = jnp.where(diagonal[None, g * GROUP : (g + 1) * GROUP], level[g], 0.0)
        part = jnp.sum(part, axis=1)
        line = part if line is None else line + part
    level_ref[...] = line
    for n, (g, j) in enumerate(pairs):
        lanes = slice(g * HD, (g + 1) * HD)
        rows = slice(n * GROUP, (n + 1) * GROUP)
        numer = dot(recent[rows], wv[j, :, lanes]) + dot(few[rows], few_v[j][:, lanes])
        share_ref[j, g * GROUP : (g + 1) * GROUP, :] = numer / total[rows]


def near_kernel(
    length_ref, q_ref, k, v, wk, wv, sk, sv, nk, nv, out, share, level, values, wks, wvs, sems
):
    copies = [
        pltpu.make_async_copy(wk, wks, sems.at[0]),
        pltpu.make_async_copy(wv, wvs, sems.at[1]),
    ]
    for copy in copies:
        copy.start()
    root_part(q_ref, [(k, v)], values, out)
    for copy in copies:
        copy.wait()
    home_part(length_ref, q_ref, wks, wvs, sk, sv, nk, nv, share, level)


def far_kernel(q_ref, *refs):
    out, values = refs[-2:]
    blocks = refs[:-2]
    root_part(q_ref, list(zip(blocks[::2], blocks[1::2])), values, out)


def select_kernel(plan, turn, q_ref, out):
    start = turn if isinstance(turn, int) else turn[0] * ROOM
    chats = [plan[t, start + e] for t in range(NX) for e in range(ROOM)]
    for n, chat in enumerate(chats):
        out[n] = q_ref[chat]


def prefix_kernel(plan, turn, q_ref, pk0, pk1, pv0, pv1, out, qs, lists):
    start = turn if isinstance(turn, int) else turn[0] * ROOM
    diagonal = head_diagonal()
    zero = jnp.int32(0)
    lists[0, 0] = zero
    lists[1, 0] = zero
    n0, n1 = zero, zero
    for s in range(NX):

        def scan(e, found, s=s):
            slot = plan[NX + s, start + e]
            lists[0, found[0]] = s * ROOM + e
            lists[1, found[1]] = s * ROOM + e
            return found[0] + 1 - slot, found[1] + slot

        left = jnp.clip(plan[2 * NX, NX + s] - start, 0, ROOM)
        n0, n1 = lax.fori_loop(0, left, scan, (n0, n1))
    slots = ((pk0, pv0, n0), (pk1, pv1, n1))

    def part(i, base, size):
        pk, pv, count = slots[i]
        last = jnp.maximum(count - 1, 0)
        chats = [lists[i, jnp.minimum(base + j, last)] for j in range(size)]
        line = None
        shares = []
        for g in range(KV):
            heads = slice(g * GROUP, (g + 1) * GROUP)
            lanes = slice(g * HD, (g + 1) * HD)
            for j, chat in enumerate(chats):
                qs[i, g, j] = q_ref[chat, heads, :]
            scores = scores_of(qs[i, g, :size].reshape(size * GROUP, HD), pk[:, lanes])
            peak = jnp.max(scores, axis=1, keepdims=True)
            weights = jnp.exp2((scores - peak) * SCALE2)
            total = jnp.sum(weights, axis=1, keepdims=True)
            numer = dot(weights.astype(BF16), pv[:, lanes])
            shares.append((numer / total).astype(BF16))
            level = jnp.broadcast_to(peak * SCALE2 + jnp.log2(total), (size * GROUP, HD))
            level = level.reshape(size, GROUP, HD)
            row = jnp.sum(jnp.where(diagonal[None, heads], level, 0.0), axis=1)
            line = row if line is None else line + row
        return chats, shares, level_parts(line)

    def store(chats, shares, parts):
        for j, chat in enumerate(chats):
            for g in range(KV):
                rows = slice(j * GROUP, (j + 1) * GROUP)
                out[chat, g * GROUP : (g + 1) * GROUP, :] = shares[g][rows]
            out[chat, HEADS:, :] = parts[j]

    @pl.when(jnp.maximum(n0, n1) > 0)
    def _():
        results = [part(i, 0, MEMBER) for i in range(2)]
        for i in range(2):
            pl.when(slots[i][2] > 0)(functools.partial(store, *results[i]))

    for i in range(2):

        def further(b, _, i=i):
            store(*part(i, MEMBER + b * (MEMBER // 2), MEMBER // 2))
            return 0

        left = jnp.maximum(slots[i][2] - MEMBER, 0)
        lax.fori_loop(0, (left + MEMBER // 2 - 1) >> 2, further, 0)


def place_answers(plan, start, back, out):
    row = iota((COLUMN, ROWS, HD), 1)
    out[...] = jnp.where(row == HEADS, FLOOR, 0.0).astype(BF16)
    for t in range(NX):

        def place(e, _, t=t):
            out[plan[t, start + e]] = back[t * ROOM + e]
            return 0

        lax.fori_loop(0, jnp.clip(plan[2 * NX, t] - start, 0, ROOM), place, 0)


def weights_of(levels):
    top = functools.reduce(jnp.maximum, levels)
    weights = [jnp.exp2(v - top) for v in levels]
    total = functools.reduce(jnp.add, weights)
    return [w / total for w in weights], top + jnp.log2(total)


def read_level(ref):
    return jnp.sum(ref[:, HEADS:, :].astype(F32), axis=1)


def four_lines(weights):
    quarter = iota((1, HD), 1) // HEADS
    return functools.reduce(
        jnp.add, [jnp.where(quarter == i, w, 0.0) for i, w in enumerate(weights)]
    )


def mix(diagonal, line, shares):
    spread = jnp.where(diagonal, line, 0.0)
    high = spread.astype(BF16)
    low = (spread - high.astype(F32)).astype(BF16)
    return dot(high, shares) + dot(low, shares)


def more_kernel(plan, turn, back, before, out, prefix):
    diagonal = head_diagonal()
    place_answers(plan, turn[0] * ROOM, back, prefix)
    weights, total = weights_of([read_level(r) for r in (before, prefix)])
    line = four_lines(weights)
    out[:, HEADS:, :] = level_parts(total)
    empty = jnp.zeros((2 * HEADS, HD), BF16)
    for i in range(COLUMN):
        shares = jnp.concatenate([before[i, :HEADS, :], prefix[i, :HEADS, :], empty], axis=0)
        out[i, :HEADS, :] = mix(diagonal, line[i : i + 1], shares).astype(BF16)


def merge_row_kernel(plan, near, far, back, share_ref, level_ref, out, prefix, levels):
    diagonal = head_diagonal()
    place_answers(plan, 0, back, prefix)
    level = [read_level(r) for r in (near, far, prefix)]
    weights, total = weights_of(level)
    line = four_lines(weights)
    for n, v in enumerate(level):
        levels[n] = v
    out[:, HEADS:, :] = level_parts(total)
    empty = jnp.zeros((HEADS, HD), BF16)

    def parts(i, fourth):
        sources = [near[i, :HEADS, :], far[i, :HEADS, :], prefix[i, :HEADS, :], fourth]
        return jnp.concatenate(sources, axis=0)

    for i in range(COLUMN):
        out[i, :HEADS, :] = mix(diagonal, line[i : i + 1], parts(i, empty)).astype(BF16)

    first = lax.axis_index("z") * HOME
    own = pl.ds(first, HOME)
    weights, total = weights_of([levels[n, own, :] for n in range(3)] + [level_ref[...]])
    line = four_lines(weights)
    rest = four_lines(weights[3:])
    out[own, HEADS:, :] = level_parts(total)
    nothing = jnp.zeros((3 * HEADS, HD), BF16)
    for j in range(HOME):
        home = share_ref[j]
        high = home.astype(BF16)
        low = jnp.concatenate([(home - high.astype(F32)).astype(BF16), nothing], axis=0)
        total = mix(diagonal, line[j : j + 1], parts(first + j, high))
        total = total + mix(diagonal, rest[j : j + 1], low)
        out[first + j, :HEADS, :] = total.astype(BF16)


def merge_kernel(in_ref, out):
    diagonal = head_diagonal()
    for y in range(NY):
        level = jnp.sum(in_ref[:, y, HEADS:, :].astype(F32), axis=1)
        weights = jnp.exp2(level - jnp.max(level, axis=0, keepdims=True))
        weights = weights / jnp.sum(weights, axis=0, keepdims=True)
        total = jnp.zeros((HEADS, HD), F32)
        for k in range(0, NZ, 4):
            line = four_lines([weights[k + i : k + i + 1] for i in range(4)])
            shares = in_ref[k : k + 4, y, :HEADS, :].reshape(4 * HEADS, HD)
            total = total + mix(diagonal, line, shares)
        out[y] = total.astype(BF16)


def kernel(
    body, name, outs, args, scalars=0, scratch=(), limit=8, us=0.5, in_specs=None, out_specs=None
):
    return pl.pallas_call(
        body,
        out_shape=outs,
        in_specs=in_specs or [SMEM] * scalars + [VMEM] * (len(args) - scalars),
        out_specs=out_specs if out_specs is not None else jax.tree.map(lambda _: VMEM, outs),
        scratch_shapes=list(scratch),
        compiler_params=pltpu.CompilerParams(vmem_limit_bytes=limit * MIB),
        cost_estimate=pl.CostEstimate(
            flops=int(us * 8e8), bytes_accessed=int(us * 1e6), transcendentals=0
        ),
        name=name,
    )(*args)


def send(array, axis, shift):
    size = {"x": NX, "z": NZ, "c": NC, "y": NY}[axis]
    return lax.ppermute(array, axis, [(i, (i + shift) % size) for i in range(size)])


def shaped(*shape, dtype=BF16):
    return jax.ShapeDtypeStruct(shape, dtype)


def local(
    queries,
    new_keys,
    new_values,
    sink_keys,
    sink_values,
    window_keys,
    window_values,
    window_len,
    root_keys,
    root_values,
    prefix_keys,
    prefix_values,
    tenant_of,
    owner,
):
    spread = jnp.broadcast_to(queries.reshape(1, NY, HEADS, HD), (NZ, NY, HEADS, HD))
    q = lax.all_to_all(
        spread.reshape(COLUMN, HEADS, HD), ("z", "y"), split_axis=0, concat_axis=0, tiled=True
    )

    k_left, v_left = send(root_keys, "x", 1), send(root_values, "x", 1)
    k_right, v_right = send(root_keys, "x", -1), send(root_values, "x", -1)
    i32 = jnp.int32
    tenant_of, _ = lax.optimization_barrier((tenant_of, spread))
    plan, rounds = kernel(
        prepare_kernel,
        "prepare",
        [shaped(2 * NX + 1, COLUMN + 1, dtype=i32), shaped(1, dtype=i32)],
        [tenant_of, owner, tenant_of.reshape(1, -1), owner.reshape(1, -1)],
        scalars=2,
        out_specs=[SMEM] * 2,
        us=2,
    )
    anywhere = pl.BlockSpec(memory_space=pl.ANY)
    near, home_share, home_level = kernel(
        near_kernel,
        "near",
        [
            shaped(COLUMN, ROWS, HD),
            shaped(HOME, HEADS, HD, dtype=F32),
            shaped(HOME, HD, dtype=F32),
        ],
        [
            window_len,
            q,
            root_keys,
            root_values,
            window_keys,
            window_values,
            sink_keys,
            sink_values,
            new_keys,
            new_values,
        ],
        in_specs=[SMEM] + [VMEM] * 3 + [anywhere] * 2 + [VMEM] * 4,
        scratch=[
            pltpu.VMEM((KV, 512, 2 * HD), BF16),
            pltpu.VMEM(window_keys.shape, BF16),
            pltpu.VMEM(window_values.shape, BF16),
            pltpu.SemaphoreType.DMA((2,)),
        ],
        limit=14,
        us=4,
    )

    def scalar_kernel(body, name, outs, turn, args, **options):
        if isinstance(turn, int):
            return kernel(
                lambda plan, *refs: body(plan, turn, *refs),
                name,
                outs,
                [plan, *args],
                scalars=1,
                **options,
            )
        return kernel(body, name, outs, [plan, turn, *args], scalars=2, **options)

    def prefix_picked(turn):
        return scalar_kernel(select_kernel, "select", shaped(NX * ROOM, HEADS, HD), turn, [q])

    picked = prefix_picked(0)
    tied = (prefix_keys, prefix_values, k_left, v_left, k_right, v_right, plan)
    pk, pv, k_left, v_left, k_right, v_right, plan = lax.optimization_barrier(tied)
    k_far, v_far = send(k_left, "x", 1), send(v_right, "x", -1)
    pk1, pv1 = send(pk, "c", 1), send(pv, "c", 1)
    rk, rv, _ = lax.optimization_barrier((root_keys, root_values, picked))
    others = [(send(rk, "c", 1), send(rv, "c", 1))]
    for k, v in ((k_left, v_left), (k_right, v_right), (k_far, v_far)):
        others += [(k, v), (send(k, "c", 1), send(v, "c", 1))]

    def over_x(array):
        return lax.all_to_all(array, "x", split_axis=0, concat_axis=0, tiled=True)

    def prefix_answers(turn, asked):
        answer = scalar_kernel(
            prefix_kernel,
            "prefix",
            shaped(NX * ROOM, ROWS, HD),
            turn,
            [asked, prefix_keys, pk1, prefix_values, pv1],
            scratch=[
                pltpu.VMEM((2, KV, MEMBER, GROUP, HD), BF16),
                pltpu.SMEM((2, NX * ROOM + 1), i32),
            ],
            us=2,
        )
        return over_x(answer)

    def more(state):
        turn, before = state
        after = kernel(
            more_kernel,
            "more",
            shaped(COLUMN, ROWS, HD),
            [plan, turn, prefix_answers(turn, over_x(prefix_picked(turn))), before],
            scalars=2,
            scratch=[pltpu.VMEM((COLUMN, ROWS, HD), BF16)],
        )
        return turn + 1, after

    answers = prefix_answers(0, over_x(picked))
    _, near = lax.while_loop(
        lambda state: state[0][0] < rounds[0], more, (jnp.ones((1,), i32), near)
    )
    far = kernel(
        far_kernel,
        "far",
        shaped(COLUMN, ROWS, HD),
        [q, *(ref for block in others for ref in block)],
        scratch=[pltpu.VMEM((KV, (2 * NX - 1) * 512, 2 * HD), BF16)],
        limit=28,
        us=6,
    )
    merged = kernel(
        merge_row_kernel,
        "merge_row",
        shaped(COLUMN, ROWS, HD),
        [plan, near, far, answers, home_share, home_level],
        scalars=1,
        scratch=[
            pltpu.VMEM((COLUMN, ROWS, HD), BF16),
            pltpu.VMEM((3, COLUMN, HD), F32),
        ],
        us=1.5,
    )
    back = lax.all_to_all(merged, ("z", "y"), split_axis=0, concat_axis=0, tiled=True)
    out = kernel(
        merge_kernel, "merge", shaped(NY, HEADS, HD), [back.reshape(NZ, NY, ROWS, HD)]
    )
    return out.reshape(1, NY * HEADS * HD)


def solution(mesh):
    fine = Mesh(mesh.devices.reshape(NX, NZ, NC, NY), ("x", "z", "c", "y"))
    session = ("x", "z", "c")
    placed = (
        P(("x", "z", "c", "y"), None),
        P(session, "y"),
        P(session, "y"),
        P(session, None, "y"),
        P(session, None, "y"),
        P(session, None, "y"),
        P(session, None, "y"),
        P(session),
        P(session, "y"),
        P(session, "y"),
        P(session, "y"),
        P(session, "y"),
        P(),
        P(),
    )
    return jax.shard_map(
        local,
        mesh=fine,
        in_specs=placed,
        out_specs=P(("x", "z", "c", "y"), None),
        check_vma=False,
    )
```
